32 devices in a mesh: dp: 16 (over z, y, x), seq: 2 (over core).
Axes of the slice: x: 2, y: 2, z: 4, core: 2. Of those that a mesh axis runs over, the one named last changes fastest.
Arguments:
- inputs: float32 [32, 8192, 768], P('dp', 'seq'), may hold values from -45 to 45
- conv_one: bfloat16 [5, 768, 768], replicated, may hold values from -0.09375 to 0.09375
- conv_two: bfloat16 [3, 768, 384], replicated, may hold values from -0.125 to 0.125
- conv_three: bfloat16 [384, 768], replicated, may hold values from -0.3125 to 0.3125
- gain_one: float32 [768], replicated, may hold values from 0.5 to 1.5
- shift_one: float32 [768], replicated, may hold values from -2 to 2
- gain_two: float32 [768], replicated, may hold values from 0.5 to 1.5
- shift_two: float32 [768], replicated, may hold values from -2 to 2
- gain_three: float32 [384], replicated, may hold values from 0.5 to 1.5
- shift_three: float32 [384], replicated, may hold values from -2 to 2
- cotangent: float32 [32, 4096, 768], P('dp', 'seq'), may hold values from -6 to 6
Outputs:
- outputs: float32 [32, 4096, 768], P('dp', 'seq')
- input_grad: float32 [32, 8192, 768], P('dp', 'seq')
- conv_one_grad: float32 [5, 768, 768], replicated
- conv_two_grad: float32 [3, 768, 384], replicated
- conv_three_grad: float32 [384, 768], replicated
- gain_one_grad: float32 [768], replicated
- shift_one_grad: float32 [768], replicated
- gain_two_grad: float32 [768], replicated
- shift_two_grad: float32 [768], replicated
- gain_three_grad: float32 [384], replicated
- shift_three_grad: float32 [384], replicated
The draws below stay inside these ranges and needn't reach their ends.
All inputs are finite; a program needn't handle non-finite values.
Results may differ from the reference program's by a relative error of at most 0.0084.
Values may be sent and summed in bfloat16 or wider, within the bound.
A program may use at most 320 MiB of HBM per device.

```python
import math
import jax
import jax.numpy as jnp
from jax import lax

C = 768
CB = 384
LENGTH = 8192
WINDOWS = 32


def draw_inputs(key, part):
    key = jax.random.fold_in(key, 7)
    first, second = jax.random.split(key, 2)
    places = jnp.arange(WINDOWS * LENGTH, dtype=jnp.float32).reshape(WINDOWS, LENGTH, 1)
    rising = 0.6 + 1.2 * places / (WINDOWS * LENGTH)
    base = jnp.clip(jax.random.normal(first, (WINDOWS, LENGTH, C), jnp.float32), -6.0, 6.0)
    scales = jnp.exp(jax.random.uniform(second, (C,), jnp.float32, math.log(0.4), math.log(4.0)))
    return base * rising * scales


def shard_levels(own_key, shape, pieces, low, top_value):
    def one(axis_at, blocks):
        steps = jax.random.uniform(jax.random.fold_in(jax.random.fold_in(own_key, 6), axis_at), (blocks,), jnp.float32, low / len(pieces), top_value / len(pieces))
        return jnp.repeat(jnp.exp(steps), shape[axis_at] // blocks).reshape((-1,) + (1,) * (len(shape) - axis_at - 1))

    loudness = one(*pieces[0])
    for cut in pieces[1:]:
        loudness = loudness * one(*cut)
    return loudness


def normal_values(own_key, extent, scale, limit, shards=(), kind=jnp.bfloat16):
    entries = jax.random.normal(own_key, extent, jnp.float32) * scale
    if len(shards) > 0:
        entries = shard_levels(own_key, extent, shards, -0.22, 0.18) * entries
    return jnp.clip(entries, min=-limit, max=limit).astype(kind)


def setup_inputs(seed: int = 0) -> dict:
    streams_of = jax.random.split(jax.random.key(seed), 12)
    return {
        "inputs": draw_inputs(jax.random.fold_in(streams_of[11], 71), 0),
        "conv_one": normal_values(streams_of[1], (5, C, C), (5 * C) ** -0.5, 0.09375),
        "conv_two": normal_values(streams_of[2], (3, C, CB), (3 * C) ** -0.5, 0.125),
        "conv_three": normal_values(streams_of[3], (CB, C), CB ** -0.5, 0.3125),
        "gain_one": jnp.clip(jax.random.uniform(streams_of[4], (C,), jnp.float32, 0.5, 1.5), 0.5, 1.5),
        "shift_one": normal_values(streams_of[5], (C,), 0.5, 2.0, (), jnp.float32),
        "gain_two": jnp.clip(jax.random.uniform(streams_of[6], (C,), jnp.float32, 0.5, 1.5), 0.5, 1.5),
        "shift_two": normal_values(streams_of[7], (C,), 0.5, 2.0, (), jnp.float32),
        "gain_three": jnp.clip(jax.random.uniform(streams_of[8], (CB,), jnp.float32, 0.5, 1.5), 0.5, 1.5),
        "shift_three": normal_values(streams_of[9], (CB,), 0.5, 2.0, (), jnp.float32),
        "cotangent": normal_values(streams_of[10], (WINDOWS, LENGTH // 2, C), 1.0, 6.0, ((0, 16), (1, 2)), jnp.float32),
    }


epsilon = 1e-05
highest = lax.Precision.HIGHEST

@jax.custom_vjp
def low(v):
    return lax.optimization_barrier(v.astype(jnp.bfloat16)).astype(jnp.float32)

@jax.custom_vjp
def low_back(v):
    return v

def low_keep(v):
    return (low(v), None)

def low_pass(kept, grad):
    return (grad,)

def back_keep(v):
    return (v, None)

def back_low(kept, grad):
    return (low(grad),)
low.defvjp(low_keep, low_pass)
low_back.defvjp(back_keep, back_low)

def batch_norm(values, gain, offset):
    center = lax.optimization_barrier(jnp.mean(values, axis=(0, 1)))
    spread = lax.optimization_barrier(jnp.mean(values * values, axis=(0, 1))) - center * center
    return (values - center) * lax.rsqrt(spread + epsilon) * gain + offset

def conv_apply(values, weight, dilation):
    reach = weight.shape[0] // 2 * dilation
    length = values.shape[1]
    padded = jnp.pad(values, ((0, 0), (reach, reach), (0, 0)))
    summed = jnp.einsum('wtc,cd->wtd', padded[:, 0:length], weight[0], precision=highest)
    for tap_index in range(1, weight.shape[0]):
        start = tap_index * dilation
        summed = summed + jnp.einsum('wtc,cd->wtd', padded[:, start:start + length], weight[tap_index], precision=highest)
    return summed

def forward(inputs, conv_one, conv_two, conv_three, gain_one, shift_one, gain_two, shift_two, gain_three, shift_three):
    hidden_one = low(jax.nn.gelu(batch_norm(inputs, gain_one, shift_one)))
    conv_out = low_back(conv_apply(hidden_one, conv_one, 1))
    pooled = 0.5 * (conv_out[:, 0::2] + conv_out[:, 1::2])
    hidden_two = low(jax.nn.gelu(batch_norm(pooled, gain_two, shift_two)))
    narrow = low_back(conv_apply(hidden_two, conv_two, 5))
    hidden_three = low(jax.nn.gelu(batch_norm(narrow, gain_three, shift_three)))
    branch = low_back(jnp.einsum('wtc,cd->wtd', hidden_three, conv_three, precision=highest))
    return pooled + branch

def reference(inputs, conv_one, conv_two, conv_three, gain_one, shift_one, gain_two, shift_two, gain_three, shift_three, cotangent):
    outputs, pullback = jax.vjp(forward, inputs, conv_one.astype(jnp.float32), conv_two.astype(jnp.float32), conv_three.astype(jnp.float32), gain_one, shift_one, gain_two, shift_two, gain_three, shift_three)
    input_grad, one_grad, two_grad, three_grad, gain_one_grad, shift_one_grad, gain_two_grad, shift_two_grad, gain_three_grad, shift_three_grad = pullback(cotangent)
    return (outputs, input_grad, one_grad, two_grad, three_grad, gain_one_grad, shift_one_grad, gain_two_grad, shift_two_grad, gain_three_grad, shift_three_grad)
```

```python
import functools

import jax
import jax.numpy as jnp
from jax import lax
from jax.experimental import pallas as pl
from jax.experimental.pallas import tpu as pltpu
from jax.sharding import PartitionSpec as P

epsilon = 1e-05
bf16 = jnp.bfloat16
f32 = jnp.float32
LANES = 128
UNIT = 64
SUB = 32
EDGE = 8
MESH = pl.DeviceIdType.MESH
LINEAR = 0.7978845608028654
CUBIC = 0.7978845608028654 * 0.044715
VMEM_LIMIT = 60 << 20
NN = (((1,), (0,)), ((), ()))
NT = (((1,), (1,)), ((), ()))
TN = (((0,), (0,)), ((), ()))


def dot(a, b, dims=NN):
    return lax.dot_general(a, b, dims, preferred_element_type=f32)


def gelu(v):
    half = 0.5 * v
    return half + half * jnp.tanh(v * (LINEAR + CUBIC * (v * v)))


def gelu_both(v):
    square = v * v
    up = 0.5 + 0.5 * jnp.tanh(v * (LINEAR + CUBIC * square))
    value = v * up
    slope = up + value * (1.0 - up) * (2.0 * LINEAR + (6.0 * CUBIC) * square)
    return value, slope


def gelu_slope(v):
    square = v * v
    up = 0.5 + 0.5 * jnp.tanh(v * (LINEAR + CUBIC * square))
    return up + (v * up) * (1.0 - up) * (2.0 * LINEAR + (6.0 * CUBIC) * square)


def center_inverse(sums, entries):
    center = sums[0:1] / entries
    return center, lax.rsqrt(sums[1:2] / entries - center * center + epsilon)


def lanes(c, width=LANES):
    if isinstance(c, int):
        return pl.ds(c * width, width)
    return pl.ds(pl.multiple_of(c * width, width), width)


def folded(values):
    return jnp.sum(values.reshape(values.shape[0] // 8, 8, values.shape[1]), axis=0)


def interleave(pieces, units):
    done = 0
    for k, piece in enumerate(pieces):
        piece()
        until = (k + 1) * len(units) // len(pieces)
        for unit in units[done:until]:
            unit()
        done = until


def place_flags():
    return lax.axis_index("seq") == 0, lax.axis_index("seq") == lax.axis_size("seq") - 1


class Walk:
    def __init__(self, windows, length, tile):
        self.tile = tile
        self.per = length // tile
        self.count = windows * self.per
        self.at_start, self.at_end = place_flags()

    def where(self, i):
        return i // self.per, i % self.per

    def hide_left(self, i):
        return jnp.logical_and(i % self.per == 0, self.at_start)

    def hide_right(self, i):
        return jnp.logical_and(i % self.per == self.per - 1, self.at_end)

    def rows(self, i, scale=1):
        span = self.tile * scale
        return pl.ds(pl.multiple_of((i % self.per) * span, span), span)

    def fetch(self, i, src, left, right, dst, sem, scale=1):
        w, p = self.where(i)
        span = self.tile * scale
        low = pl.multiple_of(p * span, span)
        first, last = p == 0, p == self.per - 1
        pltpu.make_async_copy(src.at[w, pl.ds(low, span)], dst.at[pl.ds(EDGE, span)], sem).start()
        head, tail = dst.at[pl.ds(0, EDGE)], dst.at[pl.ds(EDGE + span, EDGE)]

        @pl.when(first)
        def _():
            pltpu.make_async_copy(left.at[w], head, sem).start()

        @pl.when(jnp.logical_not(first))
        def _():
            pltpu.make_async_copy(src.at[w, pl.ds(pl.multiple_of(low - EDGE, EDGE), EDGE)], head, sem).start()

        @pl.when(last)
        def _():
            pltpu.make_async_copy(right.at[w], tail, sem).start()

        @pl.when(jnp.logical_not(last))
        def _():
            pltpu.make_async_copy(src.at[w, pl.ds(pl.multiple_of(low + span, EDGE), EDGE)], tail, sem).start()


def wait_for(dst, sem):
    pltpu.make_async_copy(dst, dst, sem).wait()


ANY = pl.BlockSpec(memory_space=pl.ANY)
VM = pl.BlockSpec(memory_space=pltpu.VMEM)
DMA = pltpu.SemaphoreType.DMA


def params(flops=0, moved=0, waved=0):
    return dict(
        compiler_params=pltpu.CompilerParams(vmem_limit_bytes=VMEM_LIMIT),
        cost_estimate=pl.CostEstimate(flops=flops, bytes_accessed=moved, transcendentals=waved),
    )


def exchange_kernel(arrays, seqs, dps, *refs):
    stats = refs[0]
    sources = refs[1 : 1 + arrays]
    sums = refs[1 + arrays]
    outs = refs[2 + arrays : 2 + 3 * arrays]
    scratch = refs[2 + 3 * arrays :]
    lands = scratch[: 2 * arrays]
    message, near, far, near_send, near_recv, far_send, far_recv, edge_send, edge_recv = scratch[2 * arrays :]
    channels = stats.shape[2]
    slabs = channels // LANES
    seq, dp = lax.axis_index("seq"), lax.axis_index("dp")

    barrier = pltpu.get_barrier_semaphore()

    def greet_near(d, _):
        pl.semaphore_signal(barrier, inc=1, device_id={"seq": lax.rem(seq + d, seqs)}, device_id_type=MESH)
        return 0

    def greet_far(d, _):
        pl.semaphore_signal(barrier, inc=1, device_id={"dp": lax.rem(dp + d, dps)}, device_id_type=MESH)
        return 0

    lax.fori_loop(1, seqs, greet_near, 0)
    lax.fori_loop(1, dps, greet_far, 0)
    pl.semaphore_wait(barrier, seqs - 1 + dps - 1)

    def edge_copy(a, side):
        src = sources[a]
        length = src.shape[1]
        part = src.at[:, pl.ds(length - EDGE, EDGE)] if side == 0 else src.at[:, pl.ds(0, EDGE)]
        to = seq + 1 if side == 0 else seq - 1
        return pltpu.make_async_remote_copy(
            src_ref=part, dst_ref=lands[2 * a + side], send_sem=edge_send.at[2 * a + side],
            recv_sem=edge_recv.at[2 * a + side], device_id={"seq": to}, device_id_type=MESH,
        )

    message[...] = jnp.zeros_like(message)
    for row in range(2):
        total = jnp.sum(stats[row], axis=0, keepdims=True)
        for c in range(slabs):
            message[row * slabs + c : row * slabs + c + 1] = total[:, c * LANES : (c + 1) * LANES]

    def near_copy(d, to):
        return pltpu.make_async_remote_copy(
            src_ref=message, dst_ref=near.at[seq], send_sem=near_send.at[d], recv_sem=near_recv.at[d],
            device_id={"seq": to}, device_id_type=MESH,
        )

    def near_start(d, _):
        near_copy(d, lax.rem(seq + d, seqs)).start()
        return 0

    def near_wait(d, _):
        near_copy(d, lax.rem(seq + d, seqs)).wait()
        return 0

    lax.fori_loop(1, seqs, near_start, 0)

    for a in range(arrays):
        @pl.when(seq < seqs - 1)
        def _():
            edge_copy(a, 0).start()

        @pl.when(seq > 0)
        def _():
            edge_copy(a, 1).start()

    near[seq] = message[...]
    lax.fori_loop(1, seqs, near_wait, 0)
    far[dp] = lax.fori_loop(1, seqs, lambda s, t: t + near[s], near[0])

    def far_copy(d, to):
        return pltpu.make_async_remote_copy(
            src_ref=far.at[dp], dst_ref=far.at[dp], send_sem=far_send.at[d], recv_sem=far_recv.at[d],
            device_id={"dp": to}, device_id_type=MESH,
        )

    def far_start(d, _):
        far_copy(d, lax.rem(dp + d, dps)).start()
        return 0

    def far_wait(d, _):
        far_copy(d, lax.rem(dp + d, dps)).wait()
        return 0

    lax.fori_loop(1, dps, far_start, 0)

    for a in range(arrays):
        @pl.when(seq < seqs - 1)
        def _():
            edge_copy(a, 0).wait_send()
            edge_copy(a, 1).wait_recv()

        @pl.when(seq > 0)
        def _():
            edge_copy(a, 1).wait_send()
            edge_copy(a, 0).wait_recv()

        for side in range(2):
            outs[2 * a + side][...] = lands[2 * a + side][...]

    lax.fori_loop(1, dps, far_wait, 0)
    total = lax.fori_loop(1, dps, lambda s, t: t + far[s], far[0])
    sums[...] = jnp.zeros_like(sums)
    for row in range(2):
        for c in range(slabs):
            sums[row : row + 1, c * LANES : (c + 1) * LANES] = total[row * slabs + c : row * slabs + c + 1]


def exchange(stats, arrays, number):
    seqs, dps = lax.axis_size("seq"), lax.axis_size("dp")
    channels = stats.shape[2]
    rows = -(-2 * (channels // LANES) // 8) * 8
    edges = [jax.ShapeDtypeStruct((a.shape[0], EDGE, a.shape[2]), a.dtype) for a in arrays for _ in range(2)]
    got = pl.pallas_call(
        functools.partial(exchange_kernel, len(arrays), seqs, dps),
        out_shape=[jax.ShapeDtypeStruct((8, channels), f32)] + edges,
        in_specs=[VM] + [ANY] * len(arrays),
        out_specs=[VM] * (1 + len(edges)),
        scratch_shapes=[pltpu.VMEM(e.shape, e.dtype) for e in edges]
        + [
            pltpu.VMEM((rows, LANES), f32),
            pltpu.VMEM((seqs, rows, LANES), f32),
            pltpu.VMEM((dps, rows, LANES), f32),
            DMA((seqs,)),
            DMA((seqs,)),
            DMA((dps,)),
            DMA((dps,)),
            DMA((2 * max(len(arrays), 1),)),
            DMA((2 * max(len(arrays), 1),)),
        ],
        compiler_params=pltpu.CompilerParams(collective_id=number, has_side_effects=True),
        name=f"exchange_{number}",
    )(stats, *arrays)
    return got[0], got[1:]


def sums_kernel(x, stats):
    @pl.when(pl.program_id(0) == 0)
    def _():
        stats[...] = jnp.zeros_like(stats)

    channels = x.shape[2]
    for c in range(channels // LANES):
        total = jnp.zeros((8, LANES), f32)
        squares = jnp.zeros((8, LANES), f32)
        for r in range(0, x.shape[1], 128):
            v = x[0, r : r + 128, lanes(c)]
            total += folded(v)
            squares += folded(v * v)
        stats[0, :, lanes(c)] += total
        stats[1, :, lanes(c)] += squares


def input_sums(x):
    windows, length, channels = x.shape
    tile = min(1024, length)
    per = length // tile
    return pl.pallas_call(
        sums_kernel,
        grid=(windows * per,),
        out_shape=jax.ShapeDtypeStruct((2, 8, channels), f32),
        in_specs=[pl.BlockSpec((1, tile, channels), lambda i: (i // per, i % per, 0))],
        out_specs=pl.BlockSpec((2, 8, channels), lambda i: (0, 0, 0)),
        name="input_sums",
        **params(moved=4 * x.size),
    )(x)


def conv_one_kernel(
    tile, entries, x, left, right, sums, gain, shift, w_hbm, pooled, s_out, first_out, stats,
    xs, h_buf, lhs_a, lhs_b, outs, coef, w_ref, x_sem, s_sem, f_sem, o_sem, w_sem,
):
    windows, length, channels = x.shape
    slabs = channels // LANES
    span = 2 * tile
    walk = Walk(windows, length // 2, tile)
    tiles = walk.count
    lhs = (lhs_a, lhs_b)
    center, inverse = center_inverse(sums[...], entries)
    scale = inverse * gain[...]
    offset = shift[...] - center * scale
    for c in range(slabs):
        coef[c, 0:1] = scale[:, lanes_of(c)]
        coef[c, 1:2] = offset[:, lanes_of(c)]
    stats[...] = jnp.zeros_like(stats)

    def load(i, slot):
        walk.fetch(i, x, left, right, xs.at[slot], x_sem.at[slot], 2)

    def s_copy(i, slot, which):
        w, _ = walk.where(i)
        return pltpu.make_async_copy(
            lhs[slot].at[:, pl.ds((2 + which) * channels, channels)], s_out.at[which, w, walk.rows(i)],
            s_sem.at[slot, which],
        )

    def first_copy(i, slot):
        w, _ = walk.where(i)
        return pltpu.make_async_copy(
            lhs[slot].at[pl.ds(0, 16), pl.ds(channels, channels)], first_out.at[w], f_sem
        )

    def o_copy(i, slot):
        w, _ = walk.where(i)
        return pltpu.make_async_copy(outs.at[slot], pooled.at[w, walk.rows(i)], o_sem.at[slot])

    def activate(i, slot, c):
        scale = coef[c, 0:1]
        offset = coef[c, 1:2]
        src = xs.at[slot]
        dst = lhs[slot]
        cols = lanes(c)

        def ends():
            head = gelu(src[0:EDGE, cols] * scale + offset)
            h_buf[c, 0:EDGE] = jnp.where(walk.hide_left(i), 0.0, head)
            tail = gelu(src[EDGE + span : 2 * EDGE + span, cols] * scale + offset)
            h_buf[c, EDGE + span : 2 * EDGE + span] = jnp.where(walk.hide_right(i), 0.0, tail)

        def rows(r):
            def run():
                for q in range(EDGE + r, EDGE + r + 2 * UNIT, 2 * SUB):
                    h_buf[c, q : q + 2 * SUB] = gelu(src[q : q + 2 * SUB, cols] * scale + offset)

            return run

        def taps(r):
            def run():
                for q in range(r, r + UNIT, SUB):
                    h = [h_buf[c, pl.ds(EDGE + 2 * q + d, SUB, stride=2)] for d in range(-2, 4)]
                    for tap in range(5):
                        at = pl.ds(pl.multiple_of(tap * channels + c * LANES, LANES), LANES)
                        dst[q : q + SUB, at] = (h[tap] + h[tap + 1]).astype(bf16)

            return run

        units = [ends, rows(0)]
        for r in range(UNIT, tile, UNIT):
            units += [rows(2 * r), taps(r - UNIT)]
        return units + [taps(tile - UNIT)]

    def matmul(slot, n):
        cols = lanes(n, 256)
        src = lhs[slot]
        held = []

        def piece(k):
            def run():
                at = slice(k * channels, (k + 1) * channels)
                part = dot(src[:, at], w_ref[at, cols])
                held[:] = [held[0] + part] if held else [part]

            return run

        def finish():
            total = 0.5 * held[0]
            outs[slot, :, cols] = total
            stats[0, :, cols] += folded(total)
            stats[1, :, cols] += folded(total * total)

        return [piece(k) for k in range(5)], finish

    load(0, 0)
    wait_for(xs.at[0], x_sem.at[0])
    w_copy = pltpu.make_async_copy(w_hbm, w_ref, w_sem)
    w_copy.start()
    load(1, 1)

    def first_slab(c, _):
        for unit in activate(0, 0, c):
            unit()
        return 0

    lax.fori_loop(0, slabs, first_slab, 0)
    for which in range(2):
        s_copy(0, 0, which).start()
    first_copy(0, 0).start()
    w_copy.wait()

    def pair(j, _):
        for slot in range(2):
            i = 2 * j + slot
            other = 1 - slot

            @pl.when(i + 1 < tiles)
            def _():
                wait_for(xs.at[other], x_sem.at[other])

            @pl.when(i + 2 < tiles)
            def _():
                load(i + 2, slot)

            @pl.when(i >= 1)
            def _():
                for which in range(2):
                    s_copy(i - 1, other, which).wait()

                @pl.when((i - 1) % walk.per == 0)
                def _():
                    first_copy(i - 1, other).wait()

            @pl.when(i >= 2)
            def _():
                o_copy(i - 2, slot).wait()

            def part(n, _):
                pieces, finish = matmul(slot, n)
                units = []
                for c in range(2):
                    units += activate(i + 1, other, 2 * n + c)
                interleave(pieces, units)
                finish()
                return 0

            lax.fori_loop(0, channels // 256, part, 0)
            o_copy(i, slot).start()

            @pl.when(i + 1 < tiles)
            def _():
                for which in range(2):
                    s_copy(i + 1, other, which).start()

                @pl.when((i + 1) % walk.per == 0)
                def _():
                    first_copy(i + 1, other).start()

        return 0

    lax.fori_loop(0, tiles // 2, pair, 0)
    for which in range(2):
        s_copy(tiles - 1, 1, which).wait()
    if walk.per == 1:
        first_copy(tiles - 1, 1).wait()
    o_copy(tiles - 2, 0).wait()
    o_copy(tiles - 1, 1).wait()


def lanes_of(c):
    return slice(c * LANES, (c + 1) * LANES)


def conv_one_forward(x, left, right, sums, gain, shift, weight, entries):
    windows, length, channels = x.shape
    half = length // 2
    tile = min(512, half)
    slabs = channels // LANES
    return pl.pallas_call(
        functools.partial(conv_one_kernel, tile, entries),
        out_shape=(
            jax.ShapeDtypeStruct((windows, half, channels), f32),
            jax.ShapeDtypeStruct((2, windows, half, channels), bf16),
            jax.ShapeDtypeStruct((windows, 16, channels), bf16),
            jax.ShapeDtypeStruct((2, 8, channels), f32),
        ),
        in_specs=[ANY, ANY, ANY, VM, VM, VM, ANY],
        out_specs=(ANY, ANY, ANY, VM),
        scratch_shapes=[
            pltpu.VMEM((2, 2 * tile + 2 * EDGE, channels), f32),
            pltpu.VMEM((slabs, 2 * tile + 2 * EDGE, LANES), f32),
            pltpu.VMEM((tile, 5 * channels), bf16),
            pltpu.VMEM((tile, 5 * channels), bf16),
            pltpu.VMEM((2, tile, channels), f32),
            pltpu.VMEM((slabs, 8, LANES), f32),
            pltpu.VMEM((5 * channels, channels), bf16),
            DMA((2,)),
            DMA((2, 2)),
            DMA,
            DMA((2,)),
            DMA,
        ],
        name="conv_one_forward",
        **params(10 * windows * half * channels * channels, 8 * x.size, x.size),
    )(x, left, right, sums, gain, shift, weight.reshape(5 * channels, channels))


def conv_two_kernel(
    tile, entries, v, left, right, sums, gain, shift, w_hbm, narrow, h_out, stats,
    vs, h_buf, lhs_a, lhs_b, outs, w_ref, v_sem, h_sem, o_sem, w_sem,
):
    windows, length, channels = v.shape
    slabs = channels // LANES
    walk = Walk(windows, length, tile)
    tiles = walk.count
    lhs = (lhs_a, lhs_b)
    center, inverse = center_inverse(sums[...], entries)
    scale = inverse * gain[...]
    offset = shift[...] - center * scale
    stats[...] = jnp.zeros_like(stats)

    def load(i, slot):
        walk.fetch(i, v, left, right, vs.at[slot], v_sem.at[slot])

    def h_copy(i, slot):
        w, _ = walk.where(i)
        return pltpu.make_async_copy(
            lhs[slot].at[:, pl.ds(channels, channels)], h_out.at[w, walk.rows(i)], h_sem.at[slot]
        )

    def o_copy(i, slot):
        w, _ = walk.where(i)
        return pltpu.make_async_copy(outs.at[slot], narrow.at[w, walk.rows(i)], o_sem.at[slot])

    def activate(i, slot, c):
        a, b = scale[:, lanes_of(c)], offset[:, lanes_of(c)]
        src, dst, cols = vs.at[slot], lhs[slot], lanes(c)

        def ends():
            head = gelu(src[0:EDGE, cols] * a + b)
            h_buf[c, 0:EDGE] = jnp.where(walk.hide_left(i), 0.0, head)
            tail = gelu(src[EDGE + tile : 2 * EDGE + tile, cols] * a + b)
            h_buf[c, EDGE + tile : 2 * EDGE + tile] = jnp.where(walk.hide_right(i), 0.0, tail)

        def rows(r):
            def run():
                q = EDGE + r
                h_buf[c, q : q + UNIT] = gelu(src[q : q + UNIT, cols] * a + b)

            return run

        def taps(r):
            def run():
                for tap in range(3):
                    at = EDGE + r + 5 * (tap - 1)
                    dst[r : r + UNIT, lanes(tap * slabs + c)] = h_buf[c, at : at + UNIT].astype(bf16)

            return run

        units = [ends, rows(0)]
        for r in range(UNIT, tile, UNIT):
            units += [rows(r), taps(r - UNIT)]
        return units + [taps(tile - UNIT)]

    load(0, 0)
    wait_for(vs.at[0], v_sem.at[0])
    w_copy = pltpu.make_async_copy(w_hbm, w_ref, w_sem)
    w_copy.start()
    load(1, 1)
    for c in range(slabs):
        for unit in activate(0, 0, c):
            unit()
    h_copy(0, 0).start()
    w_copy.wait()

    def pair(j, _):
        for slot in range(2):
            i = 2 * j + slot
            other = 1 - slot

            @pl.when(i + 1 < tiles)
            def _():
                wait_for(vs.at[other], v_sem.at[other])

            @pl.when(i + 2 < tiles)
            def _():
                load(i + 2, slot)

            @pl.when(i >= 1)
            def _():
                h_copy(i - 1, other).wait()

            @pl.when(i >= 2)
            def _():
                o_copy(i - 2, slot).wait()

            held = []

            def piece(k):
                def run():
                    at = slice(k * channels, (k + 1) * channels)
                    part = dot(lhs[slot][:, at], w_ref[at])
                    held[:] = [held[0] + part] if held else [part]

                return run

            units = []
            for c in range(slabs):
                units += activate(i + 1, other, c)
            interleave([piece(k) for k in range(3)], units)
            total = held[0]
            outs[slot] = total
            stats[0] += folded(total)
            stats[1] += folded(total * total)
            o_copy(i, slot).start()

            @pl.when(i + 1 < tiles)
            def _():
                h_copy(i + 1, other).start()

        return 0

    lax.fori_loop(0, tiles // 2, pair, 0)
    h_copy(tiles - 1, 1).wait()
    o_copy(tiles - 2, 0).wait()
    o_copy(tiles - 1, 1).wait()


def conv_two_forward(v, left, right, sums, gain, shift, weight, entries):
    windows, length, channels = v.shape
    tile = min(512, length)
    slabs = channels // LANES
    width = weight.shape[2]
    return pl.pallas_call(
        functools.partial(conv_two_kernel, tile, entries),
        out_shape=(
            jax.ShapeDtypeStruct((windows, length, width), f32),
            jax.ShapeDtypeStruct((windows, length, channels), bf16),
            jax.ShapeDtypeStruct((2, 8, width), f32),
        ),
        in_specs=[ANY, ANY, ANY, VM, VM, VM, ANY],
        out_specs=(ANY, ANY, VM),
        scratch_shapes=[
            pltpu.VMEM((2, tile + 2 * EDGE, channels), f32),
            pltpu.VMEM((slabs, tile + 2 * EDGE, LANES), f32),
            pltpu.VMEM((tile, 3 * channels), bf16),
            pltpu.VMEM((tile, 3 * channels), bf16),
            pltpu.VMEM((2, tile, width), f32),
            pltpu.VMEM((3 * channels, width), bf16),
            DMA((2,)),
            DMA((2,)),
            DMA((2,)),
            DMA,
        ],
        name="conv_two_forward",
        **params(6 * v.size * width, 8 * v.size, v.size),
    )(v, left, right, sums, gain, shift, weight.reshape(3 * channels, width))


def conv_three_kernel(
    entries, narrow, cotangent, pooled, sums, gain, shift, w_ref, outputs, da, stats, w_grad,
    branch, grad, hidden, total,
):
    tile = narrow.shape[1]
    step = pl.program_id(0)
    center, inverse = center_inverse(sums[...], entries)

    @pl.when(step == 0)
    def _():
        stats[...] = jnp.zeros_like(stats)
        total[...] = jnp.zeros_like(total)

    branch[...] = cotangent[0].astype(bf16)
    grad[...] = dot(branch[...], w_ref[...], NT)
    for c in range(narrow.shape[2] // LANES):
        cols = lanes(c)
        at = lanes_of(c)
        m, inv, g, s = center[:, at], inverse[:, at], gain[:, at], shift[:, at]
        gains = jnp.zeros((8, LANES), f32)
        shifts = jnp.zeros((8, LANES), f32)
        for r in range(0, tile, UNIT):
            normed = (narrow[0, r : r + UNIT, cols] - m) * inv
            value, slope = gelu_both(normed * g + s)
            hidden[r : r + UNIT, cols] = value.astype(bf16)
            back = slope * grad[r : r + UNIT, cols]
            da[0, r : r + UNIT, cols] = back
            gains += folded(back * normed)
            shifts += folded(back)
        stats[0, :, cols] += gains
        stats[1, :, cols] += shifts
    outputs[0] = pooled[0] + dot(hidden[...], w_ref[...])
    total[...] += dot(hidden[...], branch[...], TN)

    @pl.when(step == pl.num_programs(0) - 1)
    def _():
        w_grad[...] = total[...].astype(bf16)


def conv_three_both(narrow, cotangent, pooled, sums, gain, shift, weight, entries):
    windows, length, width = narrow.shape
    channels = weight.shape[1]
    tile = min(512, length)
    per = length // tile
    rows = lambda i: (i // per, i % per, 0)
    whole = lambda i: (0, 0)
    return pl.pallas_call(
        functools.partial(conv_three_kernel, entries),
        grid=(windows * per,),
        out_shape=(
            jax.ShapeDtypeStruct((windows, length, channels), f32),
            jax.ShapeDtypeStruct((windows, length, width), f32),
            jax.ShapeDtypeStruct((2, 8, width), f32),
            jax.ShapeDtypeStruct((width, channels), bf16),
        ),
        in_specs=[
            pl.BlockSpec((1, tile, width), rows),
            pl.BlockSpec((1, tile, channels), rows),
            pl.BlockSpec((1, tile, channels), rows),
            pl.BlockSpec((8, width), whole),
            pl.BlockSpec((1, width), whole),
            pl.BlockSpec((1, width), whole),
            pl.BlockSpec((width, channels), whole),
        ],
        out_specs=(
            pl.BlockSpec((1, tile, channels), rows),
            pl.BlockSpec((1, tile, width), rows),
            pl.BlockSpec((2, 8, width), lambda i: (0, 0, 0)),
            pl.BlockSpec((width, channels), whole),
        ),
        scratch_shapes=[
            pltpu.VMEM((tile, channels), bf16),
            pltpu.VMEM((tile, width), f32),
            pltpu.VMEM((tile, width), bf16),
            pltpu.VMEM((width, channels), f32),
        ],
        name="conv_three_both",
        **params(6 * narrow.size * channels, 12 * cotangent.size, narrow.size),
    )(narrow, cotangent, pooled, sums, gain, shift, weight)


def conv_two_back_kernel(
    tile, entries, da, da_left, da_right, v, v_left, v_right, sums3, grads3, gain3, pooled, sums2, gain2, shift2,
    h, w_hbm, da_out, stats, w_grad,
    das, vs, ps, hs, low_buf, low_a, low_b, g_buf, outs, total, w_ref, w_flip,
    a_sem, v_sem, p_sem, h_sem, o_sem, w_sem,
):
    windows, length, width = da.shape
    channels = pooled.shape[2]
    thin, slabs = width // LANES, channels // LANES
    walk = Walk(windows, length, tile)
    tiles = walk.count
    low = (low_a, low_b)
    center3, inverse3 = center_inverse(sums3[...], entries)
    grads = grads3[...]
    scale3 = inverse3 * gain3[...]
    lean = scale3 * inverse3 * (grads[0:1] / entries)
    flat = scale3 * (grads[1:2] / entries)
    center, inverse = center_inverse(sums2[...], entries)
    stats[...] = jnp.zeros_like(stats)
    total[...] = jnp.zeros_like(total)

    def load(i, slot):
        walk.fetch(i, da, da_left, da_right, das.at[slot], a_sem.at[slot])
        walk.fetch(i, v, v_left, v_right, vs.at[slot], v_sem.at[slot])

    def wait_load(slot):
        wait_for(das.at[slot], a_sem.at[slot])
        wait_for(vs.at[slot], v_sem.at[slot])

    def late_copies(i, slot):
        w, _ = walk.where(i)
        return (
            pltpu.make_async_copy(pooled.at[w, walk.rows(i)], ps.at[slot], p_sem.at[slot]),
            pltpu.make_async_copy(h.at[w, walk.rows(i)], hs.at[slot], h_sem.at[slot]),
        )

    def o_copy(i, slot):
        w, _ = walk.where(i)
        return pltpu.make_async_copy(outs.at[slot], da_out.at[w, walk.rows(i)], o_sem.at[slot])

    def lower(i, slot, c):
        at, cols = lanes_of(c), lanes(c)
        m, s, l, f = center3[:, at], scale3[:, at], lean[:, at], flat[:, at]
        dst = low[slot]

        def value(q, size):
            return das[slot, q : q + size, cols] * s - (vs[slot, q : q + size, cols] - m) * l - f

        def ends():
            low_buf[c, 0:EDGE] = jnp.where(walk.hide_left(i), 0.0, value(0, EDGE))
            low_buf[c, EDGE + tile : 2 * EDGE + tile] = jnp.where(walk.hide_right(i), 0.0, value(EDGE + tile, EDGE))

        def rows(r):
            def run():
                low_buf[c, EDGE + r : EDGE + r + UNIT] = value(EDGE + r, UNIT)

            return run

        def taps(r):
            def run():
                for tap in range(3):
                    q = EDGE + r - 5 * (tap - 1)
                    dst[r : r + UNIT, lanes(tap * thin + c)] = low_buf[c, q : q + UNIT].astype(bf16)

            return run

        units = [ends, rows(0)]
        for r in range(UNIT, tile, UNIT):
            units += [rows(r), taps(r - UNIT)]
        return units + [taps(tile - UNIT)]

    def finish(slot, c):
        at, cols = lanes_of(c), lanes(c)
        m, inv, g, s = center[:, at], inverse[:, at], gain2[:, at], shift2[:, at]
        sums = [jnp.zeros((8, LANES), f32), jnp.zeros((8, LANES), f32)]

        def rows(r):
            def run():
                normed = (ps[slot, r : r + UNIT, cols] - m) * inv
                back = gelu_slope(normed * g + s) * g_buf[r : r + UNIT, cols]
                outs[slot, r : r + UNIT, cols] = back
                sums[0] = sums[0] + folded(back * normed)
                sums[1] = sums[1] + folded(back)

            return run

        def close():
            stats[0, :, cols] += sums[0]
            stats[1, :, cols] += sums[1]

        return [rows(r) for r in range(0, tile, UNIT)] + [close]

    load(0, 0)
    w_copy = pltpu.make_async_copy(w_hbm, w_ref, w_sem)
    w_copy.start()
    for copy in late_copies(0, 0):
        copy.start()
    wait_load(0)
    load(1, 1)
    for c in range(thin):
        for unit in lower(0, 0, c):
            unit()
    w_copy.wait()
    for k in range(3):
        w_flip[k * width : (k + 1) * width] = w_ref[k].T

    def pair(j, _):
        for slot in range(2):
            i = 2 * j + slot
            other = 1 - slot

            @pl.when(i + 1 < tiles)
            def _():
                wait_load(other)
                for copy in late_copies(i + 1, other):
                    copy.start()

            @pl.when(i + 2 < tiles)
            def _():
                load(i + 2, slot)

            for copy in late_copies(i, slot):
                copy.wait()

            @pl.when(i >= 2)
            def _():
                o_copy(i - 2, slot).wait()

            def back(n):
                def run():
                    cols = lanes(n, 256)
                    g_buf[:, cols] = dot(low[slot][...], w_flip[:, cols])

                return run

            def weigh(n):
                def run():
                    at = slice(n * 256, (n + 1) * 256)
                    total[at] += dot(hs[slot, :, at], low[slot][...], TN)

                return run

            units = []
            for c in range(thin):
                units += lower(i + 1, other, c)
            interleave([back(n) for n in range(channels // 256)], units)
            units = []
            for c in range(slabs):
                units += finish(slot, c)
            interleave([weigh(n) for n in range(channels // 256)], units)
            o_copy(i, slot).start()

        return 0

    lax.fori_loop(0, tiles // 2, pair, 0)
    for k in range(3):
        w_grad[k] = total[:, k * width : (k + 1) * width].astype(bf16)
    o_copy(tiles - 2, 0).wait()
    o_copy(tiles - 1, 1).wait()


def conv_two_back(da, da_sides, v, v_sides, sums3, grads3, gain3, pooled, sums2, gain2, shift2, h, weight, entries):
    windows, length, width = da.shape
    channels = pooled.shape[2]
    tile = min(512, length)
    thin, slabs = width // LANES, channels // LANES
    return pl.pallas_call(
        functools.partial(conv_two_back_kernel, tile, entries),
        out_shape=(
            jax.ShapeDtypeStruct((windows, length, channels), f32),
            jax.ShapeDtypeStruct((2, 8, channels), f32),
            jax.ShapeDtypeStruct(weight.shape, bf16),
        ),
        in_specs=[ANY] * 6 + [VM] * 3 + [ANY] + [VM] * 3 + [ANY] * 2,
        out_specs=(ANY, VM, VM),
        scratch_shapes=[
            pltpu.VMEM((2, tile + 2 * EDGE, width), f32),
            pltpu.VMEM((2, tile + 2 * EDGE, width), f32),
            pltpu.VMEM((2, tile, channels), f32),
            pltpu.VMEM((2, tile, channels), bf16),
            pltpu.VMEM((thin, tile + 2 * EDGE, LANES), f32),
            pltpu.VMEM((tile, 3 * width), bf16),
            pltpu.VMEM((tile, 3 * width), bf16),
            pltpu.VMEM((tile, channels), f32),
            pltpu.VMEM((2, tile, channels), f32),
            pltpu.VMEM((channels, 3 * width), f32),
            pltpu.VMEM(weight.shape, bf16),
            pltpu.VMEM((3 * width, channels), bf16),
            DMA((2,)),
            DMA((2,)),
            DMA((2,)),
            DMA((2,)),
            DMA((2,)),
            DMA,
        ],
        name="conv_two_back",
        **params(12 * pooled.size * width, 16 * pooled.size, pooled.size),
    )(da, *da_sides, v, *v_sides, sums3, grads3, gain3, pooled, sums2, gain2, shift2, h, weight)


def conv_one_back_kernel(
    tile, entries, da, da_left, da_right, v, v_left, v_right, ct, ct_left, ct_right, sums2, grads2, gain2,
    x, sums1, gain1, shift1, s, first, w_hbm, da_out, stats, w_grad,
    das, vs, cts, ss, xs, firsts, low_buf, low_a, low_b, g_buf, outs, total, w_ref,
    a_sem, v_sem, c_sem, s_sem, x_sem, f_sem, o_sem, w_sem, g_sem,
):
    windows, length, channels = da.shape
    slabs = channels // LANES
    span = 2 * tile
    walk = Walk(windows, length, tile)
    tiles = walk.count
    low = (low_a, low_b)
    half_entries = entries / 2
    center2, inverse2 = center_inverse(sums2[...], half_entries)
    grads = grads2[...]
    scale2 = 0.5 * inverse2 * gain2[...]
    lean = scale2 * inverse2 * (grads[0:1] / half_entries)
    flat = scale2 * (grads[1:2] / half_entries)
    center, inverse = center_inverse(sums1[...], entries)
    stats[...] = jnp.zeros_like(stats)

    def load(i, slot):
        walk.fetch(i, da, da_left, da_right, das.at[slot], a_sem.at[slot])
        walk.fetch(i, v, v_left, v_right, vs.at[slot], v_sem.at[slot])
        walk.fetch(i, ct, ct_left, ct_right, cts.at[slot], c_sem.at[slot])

    def wait_load(slot):
        wait_for(das.at[slot], a_sem.at[slot])
        wait_for(vs.at[slot], v_sem.at[slot])
        wait_for(cts.at[slot], c_sem.at[slot])

    def late_copies(i, slot):
        w, _ = walk.where(i)
        return (
            pltpu.make_async_copy(x.at[w, walk.rows(i, 2)], xs.at[slot], x_sem.at[slot]),
            pltpu.make_async_copy(s.at[:, w, walk.rows(i)], ss.at[slot], s_sem.at[slot]),
        )

    def o_copy(i, slot):
        w, _ = walk.where(i)
        return pltpu.make_async_copy(outs.at[slot], da_out.at[w, walk.rows(i, 2)], o_sem.at[slot])

    def lower(i, slot, c):
        at, cols = lanes_of(c), lanes(c)
        m, sc, l, f = center2[:, at], scale2[:, at], lean[:, at], flat[:, at]
        dst = low[slot]

        def value(q, size):
            rows = slice(q, q + size)
            return 0.5 * cts[slot, rows, cols] + das[slot, rows, cols] * sc - (vs[slot, rows, cols] - m) * l - f

        def ends():
            low_buf[c, 0:EDGE] = jnp.where(walk.hide_left(i), 0.0, value(0, EDGE))
            low_buf[c, EDGE + tile : 2 * EDGE + tile] = jnp.where(walk.hide_right(i), 0.0, value(EDGE + tile, EDGE))

        def rows(r):
            def run():
                low_buf[c, EDGE + r : EDGE + r + UNIT] = value(EDGE + r, UNIT)

            return run

        def taps(r):
            def run():
                for tap in range(3):
                    q = EDGE + r + 1 - tap
                    dst[r : r + UNIT, lanes(tap * slabs + c)] = low_buf[c, q : q + UNIT].astype(bf16)

            return run

        units = [ends, rows(0)]
        for r in range(UNIT, tile, UNIT):
            units += [rows(r), taps(r - UNIT)]
        return units + [taps(tile - UNIT)]

    def finish(slot, c):
        at, cols = lanes_of(c), lanes(c)
        m, inv, g, sh = center[:, at], inverse[:, at], gain1[:, at], shift1[:, at]
        sums = [jnp.zeros((8, LANES), f32), jnp.zeros((8, LANES), f32)]

        def rows(r):
            def run():
                normed = (xs[slot, r : r + UNIT, cols] - m) * inv
                incoming = g_buf[c, EDGE + r : EDGE + r + UNIT] + g_buf[c, EDGE + r - 1 : EDGE + r - 1 + UNIT]
                back = gelu_slope(normed * g + sh) * incoming
                outs[slot, r : r + UNIT, cols] = back.astype(bf16)
                sums[0] = sums[0] + folded(back * normed)
                sums[1] = sums[1] + folded(back)

            return run

        def close():
            stats[0, :, cols] += sums[0]
            stats[1, :, cols] += sums[1]

        return [rows(r) for r in range(0, span, UNIT)] + [close]

    load(0, 0)
    wait_load(0)
    w_copy = pltpu.make_async_copy(w_hbm, w_ref, w_sem)
    w_copy.start()
    for copy in late_copies(0, 0):
        copy.start()
    f_copy = pltpu.make_async_copy(first, firsts, f_sem)
    f_copy.start()
    load(1, 1)
    total[...] = jnp.zeros_like(total)
    for c in range(slabs):
        for unit in lower(0, 0, c):
            unit()
    w_copy.wait()
    f_copy.wait()

    def pair(j, _):
        for slot in range(2):
            i = 2 * j + slot
            other = 1 - slot
            w, p = walk.where(i)

            @pl.when(p == 0)
            def _():
                edge = low[slot][0:16, channels : 2 * channels]
                row = lax.broadcasted_iota(jnp.int32, (16, channels), 0)
                keep = jnp.logical_and(row == 0, walk.at_start)
                here = jnp.where(keep, firsts[w].astype(f32), 0.0).astype(bf16)
                total[1] += dot(here, edge, TN)
                part = dot(edge, w_ref[1], NT) + dot(low[slot][0:16, 2 * channels :], w_ref[3], NT)
                for c in range(slabs):
                    g_buf[c, EDGE + span - 1 : EDGE + span] = part[0:1, lanes_of(c)]

            @pl.when(i + 1 < tiles)
            def _():
                wait_load(other)
                for copy in late_copies(i + 1, other):
                    copy.start()

            @pl.when(i + 2 < tiles)
            def _():
                load(i + 2, slot)

            @pl.when(i >= 2)
            def _():
                o_copy(i - 2, slot).wait()

            for c in range(slabs):
                g_buf[c, 0:EDGE] = g_buf[c, span : span + EDGE]

            def spread(n):
                at = lanes(n, 256)

                def even():
                    part = dot(low[slot][:, 0:channels], w_ref[0, at], NT)
                    part += dot(low[slot][:, channels : 2 * channels], w_ref[2, at], NT)
                    part += dot(low[slot][:, 2 * channels : 3 * channels], w_ref[4, at], NT)
                    for c in range(2):
                        g_buf[2 * n + c, pl.ds(EDGE, tile, stride=2)] = part[:, lanes_of(c)]

                def odd():
                    part = dot(low[slot][:, 0:channels], w_ref[1, at], NT)
                    part += dot(low[slot][:, channels : 2 * channels], w_ref[3, at], NT)
                    for c in range(2):
                        g_buf[2 * n + c, pl.ds(EDGE + 1, tile, stride=2)] = part[:, lanes_of(c)]

                return [even, odd]

            for n in range(channels // 256):
                units = lower(i + 1, other, 2 * n) + lower(i + 1, other, 2 * n + 1)
                interleave(spread(n), units)

            for copy in late_copies(i, slot):
                copy.wait()

            for n in range(channels // 256):
                cols = lanes(n, 256)

                def weigh(k):
                    def run():
                        at = (k // 2) * channels + n * 256
                        total[k, :, cols] += dot(ss[slot, k % 2], low[slot][:, at : at + 256], TN)

                    return run

                interleave([weigh(k) for k in range(5)], finish(slot, 2 * n) + finish(slot, 2 * n + 1))
            o_copy(i, slot).start()

        return 0

    lax.fori_loop(0, tiles // 2, pair, 0)
    w_ref[...] = total[...].astype(bf16)
    g_copy = pltpu.make_async_copy(w_ref, w_grad, g_sem)
    g_copy.start()
    o_copy(tiles - 2, 0).wait()
    o_copy(tiles - 1, 1).wait()
    g_copy.wait()


def conv_one_back(
    da, da_sides, v, v_sides, ct, ct_sides, sums2, grads2, gain2, x, sums1, gain1, shift1, s, first, weight, entries
):
    windows, length, channels = da.shape
    tile = min(512, length)
    slabs = channels // LANES
    return pl.pallas_call(
        functools.partial(conv_one_back_kernel, tile, entries),
        out_shape=(
            jax.ShapeDtypeStruct((windows, 2 * length, channels), bf16),
            jax.ShapeDtypeStruct((2, 8, channels), f32),
            jax.ShapeDtypeStruct(weight.shape, bf16),
        ),
        in_specs=[ANY] * 9 + [VM] * 3 + [ANY] + [VM] * 3 + [ANY] * 3,
        out_specs=(ANY, VM, ANY),
        scratch_shapes=[
            pltpu.VMEM((2, tile + 2 * EDGE, channels), f32),
            pltpu.VMEM((2, tile + 2 * EDGE, channels), f32),
            pltpu.VMEM((2, tile + 2 * EDGE, channels), f32),
            pltpu.VMEM((2, 2, tile, channels), bf16),
            pltpu.VMEM((2, 2 * tile, channels), f32),
            pltpu.VMEM(first.shape, bf16),
            pltpu.VMEM((slabs, tile + 2 * EDGE, LANES), f32),
            pltpu.VMEM((tile, 3 * channels), bf16),
            pltpu.VMEM((tile, 3 * channels), bf16),
            pltpu.VMEM((slabs, 2 * tile + 2 * EDGE, LANES), f32),
            pltpu.VMEM((2, 2 * tile, channels), bf16),
            pltpu.VMEM(weight.shape, f32),
            pltpu.VMEM(weight.shape, bf16),
            DMA((2,)),
            DMA((2,)),
            DMA((2,)),
            DMA((2,)),
            DMA((2,)),
            DMA,
            DMA((2,)),
            DMA,
            DMA,
        ],
        name="conv_one_back",
        **params(20 * da.size * channels, 8 * x.size, x.size),
    )(da, *da_sides, v, *v_sides, ct, *ct_sides, sums2, grads2, gain2, x, sums1, gain1, shift1, s, first, weight)


def last_kernel(entries, x, da, sums, grads, gain, out):
    center, inverse = center_inverse(sums[...], entries)
    both = grads[...]
    scale = inverse * gain[...]
    lean = scale * inverse * (both[0:1] / entries)
    flat = scale * (both[1:2] / entries)
    for c in range(x.shape[2] // LANES):
        cols, at = lanes(c), lanes_of(c)
        m, s, l, f = center[:, at], scale[:, at], lean[:, at], flat[:, at]
        for r in range(0, x.shape[1], 128):
            rows = slice(r, r + 128)
            out[0, rows, cols] = da[0, rows, cols].astype(f32) * s - (x[0, rows, cols] - m) * l - f


def input_back(x, da, sums, grads, gain, entries):
    windows, length, channels = x.shape
    tile = min(512, length)
    per = length // tile
    rows = pl.BlockSpec((1, tile, channels), lambda i: (i // per, i % per, 0))
    whole = lambda i: (0, 0)
    return pl.pallas_call(
        functools.partial(last_kernel, entries),
        grid=(windows * per,),
        out_shape=jax.ShapeDtypeStruct(x.shape, f32),
        in_specs=[
            rows,
            rows,
            pl.BlockSpec((8, channels), whole),
            pl.BlockSpec((8, channels), whole),
            pl.BlockSpec((1, channels), whole),
        ],
        out_specs=rows,
        name="input_back",
        **params(moved=10 * x.size),
    )(x, da, sums, grads, gain)


def on_device(
    inputs,
    conv_one,
    conv_two,
    conv_three,
    gain_one,
    shift_one,
    gain_two,
    shift_two,
    gain_three,
    shift_three,
    cotangent,
):
    windows, length, channels = inputs.shape
    entries = float(windows * length * lax.axis_size("dp") * lax.axis_size("seq"))
    half = entries / 2
    gain_one, shift_one, gain_two, shift_two, gain_three, shift_three = (
        v.reshape(1, -1) for v in (gain_one, shift_one, gain_two, shift_two, gain_three, shift_three)
    )
    sums1, (x_left, x_right, c_left, c_right) = exchange(input_sums(inputs), [inputs, cotangent], 0)
    pooled, s, first, stats = conv_one_forward(
        inputs, x_left, x_right, sums1, gain_one, shift_one, conv_one, entries
    )
    sums2, p_sides = exchange(stats, [pooled], 1)
    narrow, hidden_two, stats = conv_two_forward(pooled, *p_sides, sums2, gain_two, shift_two, conv_two, half)
    sums3, n_sides = exchange(stats, [narrow], 2)
    outputs, da3, stats, three_grad = conv_three_both(
        narrow, cotangent, pooled, sums3, gain_three, shift_three, conv_three, half
    )
    grads3, a_sides = exchange(stats, [da3], 3)
    da2, stats, two_grad = conv_two_back(
        da3, a_sides, narrow, n_sides, sums3, grads3, gain_three, pooled, sums2, gain_two, shift_two,
        hidden_two, conv_two, half,
    )
    grads2, b_sides = exchange(stats, [da2], 4)
    da1, stats, one_grad = conv_one_back(
        da2, b_sides, pooled, p_sides, cotangent, (c_left, c_right), sums2, grads2, gain_two,
        inputs, sums1, gain_one, shift_one, s, first, conv_one, entries,
    )
    grads1, _ = exchange(stats, [], 5)
    input_grad = input_back(inputs, da1, sums1, grads1, gain_one, entries)
    two_grad, three_grad = lax.psum((two_grad, three_grad), ("dp", "seq"))
    one_grad = lax.psum(one_grad, ("dp", "seq"))
    return (
        outputs,
        input_grad,
        one_grad.astype(f32),
        two_grad.astype(f32),
        three_grad.astype(f32),
        grads1[0],
        grads1[1],
        grads2[0],
        grads2[1],
        grads3[0],
        grads3[1],
    )


def solution(mesh):
    rows = P("dp", "seq", None)
    in_specs = (rows,) + (P(),) * 9 + (rows,)
    out_specs = (rows, rows) + (P(),) * 9
    return jax.shard_map(on_device, mesh=mesh, in_specs=in_specs, out_specs=out_specs, check_vma=False)
```

```python
import functools

import jax
import jax.numpy as jnp
from jax import lax
from jax.experimental import pallas as pl
from jax.experimental.pallas import tpu as pltpu
from jax.sharding import PartitionSpec as P

epsilon = 1e-05
bf16 = jnp.bfloat16
f32 = jnp.float32
LANES = 128
UNIT = 64
SUB = 32
EDGE = 8
MESH = pl.DeviceIdType.MESH
LINEAR = 0.7978845608028654
CUBIC = 0.7978845608028654 * 0.044715
VMEM_LIMIT = 60 << 20
EARLY = 3
NN = (((1,), (0,)), ((), ()))
NT = (((1,), (1,)), ((), ()))
TN = (((0,), (0,)), ((), ()))


def dot(a, b, dims=NN):
    return lax.dot_general(a, b, dims, preferred_element_type=f32)


def gelu(v):
    half = 0.5 * v
    return half + half * jnp.tanh(v * (LINEAR + CUBIC * (v * v)))


def gelu_both(v):
    square = v * v
    up = 0.5 + 0.5 * jnp.tanh(v * (LINEAR + CUBIC * square))
    value = v * up
    slope = up + value * (1.0 - up) * (2.0 * LINEAR + (6.0 * CUBIC) * square)
    return value, slope


def gelu_slope(v):
    square = v * v
    up = 0.5 + 0.5 * jnp.tanh(v * (LINEAR + CUBIC * square))
    return up + (v * up) * (1.0 - up) * (2.0 * LINEAR + (6.0 * CUBIC) * square)


def center_inverse(sums, entries):
    center = sums[0:1] / entries
    return center, lax.rsqrt(sums[1:2] / entries - center * center + epsilon)


def flat_row(v):
    return v[...].reshape(1, v.shape[0])


def lanes(c, width=LANES):
    if isinstance(c, int):
        return pl.ds(c * width, width)
    return pl.ds(pl.multiple_of(c * width, width), width)


def folded(values):
    return jnp.sum(values.reshape(values.shape[0] // 8, 8, values.shape[1]), axis=0)


def interleave(pieces, units):
    done = 0
    for k, piece in enumerate(pieces):
        piece()
        until = (k + 1) * len(units) // len(pieces)
        for unit in units[done:until]:
            unit()
        done = until


def place_flags():
    return lax.axis_index("seq") == 0, lax.axis_index("seq") == lax.axis_size("seq") - 1


class Walk:
    def __init__(self, windows, length, tile):
        self.tile = tile
        self.per = length // tile
        self.count = windows * self.per
        self.at_start, self.at_end = place_flags()

    def where(self, i):
        return i // self.per, i % self.per

    def hide_left(self, i):
        return jnp.logical_and(i % self.per == 0, self.at_start)

    def hide_right(self, i):
        return jnp.logical_and(i % self.per == self.per - 1, self.at_end)

    def rows(self, i, scale=1):
        span = self.tile * scale
        return pl.ds(pl.multiple_of((i % self.per) * span, span), span)

    def fetch(self, i, src, left, right, dst, sem, scale=1):
        w, p = self.where(i)
        span = self.tile * scale
        low = pl.multiple_of(p * span, span)
        first, last = p == 0, p == self.per - 1
        pltpu.make_async_copy(src.at[w, pl.ds(low, span)], dst.at[pl.ds(EDGE, span)], sem).start()
        head, tail = dst.at[pl.ds(0, EDGE)], dst.at[pl.ds(EDGE + span, EDGE)]

        @pl.when(first)
        def _():
            pltpu.make_async_copy(left.at[w], head, sem).start()

        @pl.when(jnp.logical_not(first))
        def _():
            pltpu.make_async_copy(src.at[w, pl.ds(pl.multiple_of(low - EDGE, EDGE), EDGE)], head, sem).start()

        @pl.when(last)
        def _():
            pltpu.make_async_copy(right.at[w], tail, sem).start()

        @pl.when(jnp.logical_not(last))
        def _():
            pltpu.make_async_copy(src.at[w, pl.ds(pl.multiple_of(low + span, EDGE), EDGE)], tail, sem).start()


def wait_for(dst, sem):
    pltpu.make_async_copy(dst, dst, sem).wait()


ANY = pl.BlockSpec(memory_space=pl.ANY)
VM = pl.BlockSpec(memory_space=pltpu.VMEM)
DMA = pltpu.SemaphoreType.DMA


def params(flops=0, moved=0, waved=0):
    return dict(
        compiler_params=pltpu.CompilerParams(vmem_limit_bytes=VMEM_LIMIT),
        cost_estimate=pl.CostEstimate(flops=flops, bytes_accessed=moved, transcendentals=waved),
    )


def exchange_kernel(arrays, seqs, dps, *refs):
    stats = refs[0]
    sources = refs[1 : 1 + arrays]
    sums = refs[1 + arrays]
    outs = refs[2 + arrays : 2 + 3 * arrays]
    scratch = refs[2 + 3 * arrays :]
    lands = scratch[: 2 * arrays]
    message, near, far, near_send, near_recv, far_send, far_recv, edge_send, edge_recv = scratch[2 * arrays :]
    channels = stats.shape[2]
    slabs = channels // LANES
    seq, dp = lax.axis_index("seq"), lax.axis_index("dp")

    barrier = pltpu.get_barrier_semaphore()

    def greet_near(d, _):
        pl.semaphore_signal(barrier, inc=1, device_id={"seq": lax.rem(seq + d, seqs)}, device_id_type=MESH)
        return 0

    def greet_far(d, _):
        pl.semaphore_signal(barrier, inc=1, device_id={"dp": lax.rem(dp + d, dps)}, device_id_type=MESH)
        return 0

    lax.fori_loop(1, seqs, greet_near, 0)
    lax.fori_loop(1, dps, greet_far, 0)
    pl.semaphore_wait(barrier, seqs - 1 + dps - 1)

    def edge_copy(a, side):
        src = sources[a]
        length = src.shape[1]
        part = src.at[:, pl.ds(length - EDGE, EDGE)] if side == 0 else src.at[:, pl.ds(0, EDGE)]
        to = seq + 1 if side == 0 else seq - 1
        return pltpu.make_async_remote_copy(
            src_ref=part, dst_ref=lands[2 * a + side], send_sem=edge_send.at[2 * a + side],
            recv_sem=edge_recv.at[2 * a + side], device_id={"seq": to}, device_id_type=MESH,
        )

    message[...] = jnp.zeros_like(message)
    for row in range(2):
        total = jnp.sum(stats[row], axis=0, keepdims=True)
        for c in range(slabs):
            message[row * slabs + c : row * slabs + c + 1] = total[:, c * LANES : (c + 1) * LANES]

    def near_copy(d, to):
        return pltpu.make_async_remote_copy(
            src_ref=message, dst_ref=near.at[seq], send_sem=near_send.at[d], recv_sem=near_recv.at[d],
            device_id={"seq": to}, device_id_type=MESH,
        )

    def near_start(d, _):
        near_copy(d, lax.rem(seq + d, seqs)).start()
        return 0

    def near_wait(d, _):
        near_copy(d, lax.rem(seq + d, seqs)).wait()
        return 0

    lax.fori_loop(1, seqs, near_start, 0)

    for a in range(arrays):
        @pl.when(seq < seqs - 1)
        def _():
            edge_copy(a, 0).start()

        @pl.when(seq > 0)
        def _():
            edge_copy(a, 1).start()

    near[seq] = message[...]
    lax.fori_loop(1, seqs, near_wait, 0)
    far[dp] = lax.fori_loop(1, seqs, lambda s, t: t + near[s], near[0])

    def far_copy(d, to):
        return pltpu.make_async_remote_copy(
            src_ref=far.at[dp], dst_ref=far.at[dp], send_sem=far_send.at[d], recv_sem=far_recv.at[d],
            device_id={"dp": to}, device_id_type=MESH,
        )

    def far_start(d, _):
        far_copy(d, lax.rem(dp + d, dps)).start()
        return 0

    def far_wait(d, _):
        far_copy(d, lax.rem(dp + d, dps)).wait()
        return 0

    lax.fori_loop(1, dps, far_start, 0)

    for a in range(arrays):
        @pl.when(seq < seqs - 1)
        def _():
            edge_copy(a, 0).wait_send()
            edge_copy(a, 1).wait_recv()

        @pl.when(seq > 0)
        def _():
            edge_copy(a, 1).wait_send()
            edge_copy(a, 0).wait_recv()

        for side in range(2):
            outs[2 * a + side][...] = lands[2 * a + side][...]

    lax.fori_loop(1, dps, far_wait, 0)
    total = lax.fori_loop(1, dps, lambda s, t: t + far[s], far[0])
    sums[...] = jnp.zeros_like(sums)
    for row in range(2):
        for c in range(slabs):
            sums[row : row + 1, c * LANES : (c + 1) * LANES] = total[row * slabs + c : row * slabs + c + 1]


def exchange(stats, arrays, number):
    seqs, dps = lax.axis_size("seq"), lax.axis_size("dp")
    channels = stats.shape[2]
    rows = -(-2 * (channels // LANES) // 8) * 8
    edges = [jax.ShapeDtypeStruct((a.shape[0], EDGE, a.shape[2]), a.dtype) for a in arrays for _ in range(2)]
    got = pl.pallas_call(
        functools.partial(exchange_kernel, len(arrays), seqs, dps),
        out_shape=[jax.ShapeDtypeStruct((8, channels), f32)] + edges,
        in_specs=[VM] + [ANY] * len(arrays),
        out_specs=[VM] * (1 + len(edges)),
        scratch_shapes=[pltpu.VMEM(e.shape, e.dtype) for e in edges]
        + [
            pltpu.VMEM((rows, LANES), f32),
            pltpu.VMEM((seqs, rows, LANES), f32),
            pltpu.VMEM((dps, rows, LANES), f32),
            DMA((seqs,)),
            DMA((seqs,)),
            DMA((dps,)),
            DMA((dps,)),
            DMA((2 * max(len(arrays), 1),)),
            DMA((2 * max(len(arrays), 1),)),
        ],
        compiler_params=pltpu.CompilerParams(collective_id=number, has_side_effects=True),
        name=f"exchange_{number}",
    )(stats, *arrays)
    return got[0], got[1:]


def sums_kernel(x, stats):
    @pl.when(pl.program_id(0) == 0)
    def _():
        stats[...] = jnp.zeros_like(stats)

    channels = x.shape[2]
    for c in range(channels // LANES):
        total = jnp.zeros((8, LANES), f32)
        squares = jnp.zeros((8, LANES), f32)
        for r in range(0, x.shape[1], 128):
            v = x[0, r : r + 128, lanes(c)]
            total += folded(v)
            squares += folded(v * v)
        stats[0, :, lanes(c)] += total
        stats[1, :, lanes(c)] += squares


def input_sums(x):
    windows, length, channels = x.shape
    tile = min(1024, length)
    per = length // tile
    return pl.pallas_call(
        sums_kernel,
        grid=(windows * per,),
        out_shape=jax.ShapeDtypeStruct((2, 8, channels), f32),
        in_specs=[pl.BlockSpec((1, tile, channels), lambda i: (i // per, i % per, 0))],
        out_specs=pl.BlockSpec((2, 8, channels), lambda i: (0, 0, 0)),
        name="input_sums",
        **params(moved=4 * x.size),
    )(x)


def conv_one_kernel(
    tile, entries, x, left, right, sums, gain, shift, w_hbm, pooled, s_out, first_out, stats,
    xs, h_buf, lhs_a, lhs_b, outs, coef, w_ref, x_sem, s_sem, f_sem, o_sem, w_sem,
):
    windows, length, channels = x.shape
    slabs = channels // LANES
    span = 2 * tile
    walk = Walk(windows, length // 2, tile)
    tiles = walk.count
    lhs = (lhs_a, lhs_b)
    center, inverse = center_inverse(sums[...], entries)
    scale = inverse * flat_row(gain)
    offset = flat_row(shift) - center * scale
    for c in range(slabs):
        coef[c, 0:1] = scale[:, lanes_of(c)]
        coef[c, 1:2] = offset[:, lanes_of(c)]
    stats[...] = jnp.zeros_like(stats)

    def load(i, slot):
        walk.fetch(i, x, left, right, xs.at[slot], x_sem.at[slot], 2)

    def s_copy(i, slot, which):
        w, _ = walk.where(i)
        return pltpu.make_async_copy(
            lhs[slot].at[:, pl.ds((2 + which) * channels, channels)], s_out.at[which, w, walk.rows(i)],
            s_sem.at[slot, which],
        )

    def first_copy(i, slot):
        w, _ = walk.where(i)
        return pltpu.make_async_copy(
            lhs[slot].at[pl.ds(0, 16), pl.ds(channels, channels)], first_out.at[w], f_sem
        )

    def o_copy(i, slot):
        w, _ = walk.where(i)
        return pltpu.make_async_copy(outs.at[slot], pooled.at[w, walk.rows(i)], o_sem.at[slot])

    def activate(i, slot, c):
        scale = coef[c, 0:1]
        offset = coef[c, 1:2]
        src = xs.at[slot]
        dst = lhs[slot]
        cols = lanes(c)

        def ends():
            head = gelu(src[0:EDGE, cols] * scale + offset)
            h_buf[c, 0:EDGE] = jnp.where(walk.hide_left(i), 0.0, head)
            tail = gelu(src[EDGE + span : 2 * EDGE + span, cols] * scale + offset)
            h_buf[c, EDGE + span : 2 * EDGE + span] = jnp.where(walk.hide_right(i), 0.0, tail)

        def rows(r):
            def run():
                for q in range(EDGE + r, EDGE + r + 2 * UNIT, 2 * SUB):
                    h_buf[c, q : q + 2 * SUB] = gelu(src[q : q + 2 * SUB, cols] * scale + offset)

            return run

        def taps(r):
            def run():
                for q in range(r, r + UNIT, SUB):
                    h = [h_buf[c, pl.ds(EDGE + 2 * q + d, SUB, stride=2)] for d in range(-2, 4)]
                    for tap in range(5):
                        at = pl.ds(pl.multiple_of(tap * channels + c * LANES, LANES), LANES)
                        dst[q : q + SUB, at] = (h[tap] + h[tap + 1]).astype(bf16)

            return run

        units = [ends, rows(0)]
        for r in range(UNIT, tile, UNIT):
            units += [rows(2 * r), taps(r - UNIT)]
        return units + [taps(tile - UNIT)]

    def matmul(slot, n):
        cols = lanes(n, 256)
        src = lhs[slot]
        held = []

        def piece(k):
            def run():
                at = slice(k * channels, (k + 1) * channels)
                part = dot(src[:, at], w_ref[at, cols])
                held[:] = [held[0] + part] if held else [part]

            return run

        def finish():
            total = 0.5 * held[0]
            outs[slot, :, cols] = total
            stats[0, :, cols] += folded(total)
            stats[1, :, cols] += folded(total * total)

        return [piece(k) for k in range(5)], finish

    load(0, 0)
    wait_for(xs.at[0], x_sem.at[0])
    w_copy = pltpu.make_async_copy(w_hbm, w_ref, w_sem)
    w_copy.start()
    load(1, 1)

    def first_slab(c, _):
        for unit in activate(0, 0, c):
            unit()
        return 0

    lax.fori_loop(0, slabs, first_slab, 0)
    for which in range(2):
        s_copy(0, 0, which).start()
    first_copy(0, 0).start()
    w_copy.wait()

    def pair(j, _):
        for slot in range(2):
            i = 2 * j + slot
            other = 1 - slot

            @pl.when(i + 1 < tiles)
            def _():
                wait_for(xs.at[other], x_sem.at[other])

            @pl.when(i + 2 < tiles)
            def _():
                load(i + 2, slot)

            @pl.when(i >= 1)
            def _():
                for which in range(2):
                    s_copy(i - 1, other, which).wait()

                @pl.when((i - 1) % walk.per == 0)
                def _():
                    first_copy(i - 1, other).wait()

            @pl.when(i >= 2)
            def _():
                o_copy(i - 2, slot).wait()

            def part(n, _):
                pieces, finish = matmul(slot, n)
                units = []
                for c in range(2):
                    units += activate(i + 1, other, 2 * n + c)
                interleave(pieces, units)
                finish()
                return 0

            lax.fori_loop(0, channels // 256, part, 0)
            o_copy(i, slot).start()

            @pl.when(i + 1 < tiles)
            def _():
                for which in range(2):
                    s_copy(i + 1, other, which).start()

                @pl.when((i + 1) % walk.per == 0)
                def _():
                    first_copy(i + 1, other).start()

        return 0

    lax.fori_loop(0, tiles // 2, pair, 0)
    for which in range(2):
        s_copy(tiles - 1, 1, which).wait()
    if walk.per == 1:
        first_copy(tiles - 1, 1).wait()
    o_copy(tiles - 2, 0).wait()
    o_copy(tiles - 1, 1).wait()


def lanes_of(c):
    return slice(c * LANES, (c + 1) * LANES)


def conv_one_forward(x, left, right, sums, gain, shift, weight, entries):
    windows, length, channels = x.shape
    half = length // 2
    tile = min(512, half)
    slabs = channels // LANES
    return pl.pallas_call(
        functools.partial(conv_one_kernel, tile, entries),
        out_shape=(
            jax.ShapeDtypeStruct((windows, half, channels), f32),
            jax.ShapeDtypeStruct((2, windows, half, channels), bf16),
            jax.ShapeDtypeStruct((windows, 16, channels), bf16),
            jax.ShapeDtypeStruct((2, 8, channels), f32),
        ),
        in_specs=[ANY, ANY, ANY, VM, VM, VM, ANY],
        out_specs=(ANY, ANY, ANY, VM),
        scratch_shapes=[
            pltpu.VMEM((2, 2 * tile + 2 * EDGE, channels), f32),
            pltpu.VMEM((slabs, 2 * tile + 2 * EDGE, LANES), f32),
            pltpu.VMEM((tile, 5 * channels), bf16),
            pltpu.VMEM((tile, 5 * channels), bf16),
            pltpu.VMEM((2, tile, channels), f32),
            pltpu.VMEM((slabs, 8, LANES), f32),
            pltpu.VMEM((5 * channels, channels), bf16),
            DMA((2,)),
            DMA((2, 2)),
            DMA,
            DMA((2,)),
            DMA,
        ],
        name="conv_one_forward",
        **params(10 * windows * half * channels * channels, 8 * x.size, x.size),
    )(x, left, right, sums, gain, shift, weight.reshape(5 * channels, channels))


def conv_two_kernel(
    tile, entries, v, left, right, sums, gain, shift, w_hbm, narrow, h_out, stats,
    vs, h_buf, lhs_a, lhs_b, outs, w_ref, v_sem, h_sem, o_sem, w_sem,
):
    windows, length, channels = v.shape
    slabs = channels // LANES
    walk = Walk(windows, length, tile)
    tiles = walk.count
    lhs = (lhs_a, lhs_b)
    center, inverse = center_inverse(sums[...], entries)
    scale = inverse * flat_row(gain)
    offset = flat_row(shift) - center * scale
    stats[...] = jnp.zeros_like(stats)

    def load(i, slot):
        walk.fetch(i, v, left, right, vs.at[slot], v_sem.at[slot])

    def h_copy(i, slot):
        w, _ = walk.where(i)
        return pltpu.make_async_copy(
            lhs[slot].at[:, pl.ds(channels, channels)], h_out.at[w, walk.rows(i)], h_sem.at[slot]
        )

    def o_copy(i, slot):
        w, _ = walk.where(i)
        return pltpu.make_async_copy(outs.at[slot], narrow.at[w, walk.rows(i)], o_sem.at[slot])

    def activate(i, slot, c):
        a, b = scale[:, lanes_of(c)], offset[:, lanes_of(c)]
        src, dst, cols = vs.at[slot], lhs[slot], lanes(c)

        def ends():
            head = gelu(src[0:EDGE, cols] * a + b)
            h_buf[c, 0:EDGE] = jnp.where(walk.hide_left(i), 0.0, head)
            tail = gelu(src[EDGE + tile : 2 * EDGE + tile, cols] * a + b)
            h_buf[c, EDGE + tile : 2 * EDGE + tile] = jnp.where(walk.hide_right(i), 0.0, tail)

        def rows(r):
            def run():
                q = EDGE + r
                h_buf[c, q : q + UNIT] = gelu(src[q : q + UNIT, cols] * a + b)

            return run

        def taps(r):
            def run():
                for tap in range(3):
                    at = EDGE + r + 5 * (tap - 1)
                    dst[r : r + UNIT, lanes(tap * slabs + c)] = h_buf[c, at : at + UNIT].astype(bf16)

            return run

        units = [ends, rows(0)]
        for r in range(UNIT, tile, UNIT):
            units += [rows(r), taps(r - UNIT)]
        return units + [taps(tile - UNIT)]

    load(0, 0)
    wait_for(vs.at[0], v_sem.at[0])
    w_copy = pltpu.make_async_copy(w_hbm, w_ref, w_sem)
    w_copy.start()
    load(1, 1)
    for c in range(slabs):
        for unit in activate(0, 0, c):
            unit()
    h_copy(0, 0).start()
    w_copy.wait()

    def pair(j, _):
        for slot in range(2):
            i = 2 * j + slot
            other = 1 - slot

            @pl.when(i + 1 < tiles)
            def _():
                wait_for(vs.at[other], v_sem.at[other])

            @pl.when(i + 2 < tiles)
            def _():
                load(i + 2, slot)

            @pl.when(i >= 1)
            def _():
                h_copy(i - 1, other).wait()

            @pl.when(i >= 2)
            def _():
                o_copy(i - 2, slot).wait()

            held = []

            def piece(k):
                def run():
                    at = slice(k * channels, (k + 1) * channels)
                    part = dot(lhs[slot][:, at], w_ref[at])
                    held[:] = [held[0] + part] if held else [part]

                return run

            units = []
            for c in range(slabs):
                units += activate(i + 1, other, c)
            interleave([piece(k) for k in range(3)], units)
            total = held[0]
            outs[slot] = total
            stats[0] += folded(total)
            stats[1] += folded(total * total)
            o_copy(i, slot).start()

            @pl.when(i + 1 < tiles)
            def _():
                h_copy(i + 1, other).start()

        return 0

    lax.fori_loop(0, tiles // 2, pair, 0)
    h_copy(tiles - 1, 1).wait()
    o_copy(tiles - 2, 0).wait()
    o_copy(tiles - 1, 1).wait()


def conv_two_forward(v, left, right, sums, gain, shift, weight, entries):
    windows, length, channels = v.shape
    tile = min(512, length)
    slabs = channels // LANES
    width = weight.shape[2]
    return pl.pallas_call(
        functools.partial(conv_two_kernel, tile, entries),
        out_shape=(
            jax.ShapeDtypeStruct((windows, length, width), f32),
            jax.ShapeDtypeStruct((windows, length, channels), bf16),
            jax.ShapeDtypeStruct((2, 8, width), f32),
        ),
        in_specs=[ANY, ANY, ANY, VM, VM, VM, ANY],
        out_specs=(ANY, ANY, VM),
        scratch_shapes=[
            pltpu.VMEM((2, tile + 2 * EDGE, channels), f32),
            pltpu.VMEM((slabs, tile + 2 * EDGE, LANES), f32),
            pltpu.VMEM((tile, 3 * channels), bf16),
            pltpu.VMEM((tile, 3 * channels), bf16),
            pltpu.VMEM((2, tile, width), f32),
            pltpu.VMEM((3 * channels, width), bf16),
            DMA((2,)),
            DMA((2,)),
            DMA((2,)),
            DMA,
        ],
        name="conv_two_forward",
        **params(6 * v.size * width, 8 * v.size, v.size),
    )(v, left, right, sums, gain, shift, weight.reshape(3 * channels, width))


def conv_three_kernel(
    entries, narrow, cotangent, pooled, sums, gain, shift, w_ref, outputs, da, stats, w_grad,
    branch, grad, hidden, total,
):
    tile = narrow.shape[1]
    step = pl.program_id(0)
    center, inverse = center_inverse(sums[...], entries)

    @pl.when(step == 0)
    def _():
        stats[...] = jnp.zeros_like(stats)
        total[...] = jnp.zeros_like(total)

    branch[...] = cotangent[0].astype(bf16)
    grad[...] = dot(branch[...], w_ref[...], NT)
    for c in range(narrow.shape[2] // LANES):
        cols = lanes(c)
        at = lanes_of(c)
        m, inv, g, s = center[:, at], inverse[:, at], gain[at][None], shift[at][None]
        gains = jnp.zeros((8, LANES), f32)
        shifts = jnp.zeros((8, LANES), f32)
        for r in range(0, tile, UNIT):
            normed = (narrow[0, r : r + UNIT, cols] - m) * inv
            value, slope = gelu_both(normed * g + s)
            hidden[r : r + UNIT, cols] = value.astype(bf16)
            back = slope * grad[r : r + UNIT, cols]
            da[0, r : r + UNIT, cols] = back
            gains += folded(back * normed)
            shifts += folded(back)
        stats[0, :, cols] += gains
        stats[1, :, cols] += shifts
    outputs[0] = pooled[0] + dot(hidden[...], w_ref[...])
    total[...] += dot(hidden[...], branch[...], TN)

    @pl.when(step == pl.num_programs(0) - 1)
    def _():
        for c in range(total.shape[1] // LANES):
            w_grad[c] = total[:, lanes_of(c)].astype(bf16)


def conv_three_both(narrow, cotangent, pooled, sums, gain, shift, weight, entries):
    windows, length, width = narrow.shape
    channels = weight.shape[1]
    tile = min(512, length)
    per = length // tile
    rows = lambda i: (i // per, i % per, 0)
    whole = lambda i: (0, 0)
    return pl.pallas_call(
        functools.partial(conv_three_kernel, entries),
        grid=(windows * per,),
        out_shape=(
            jax.ShapeDtypeStruct((windows, length, channels), f32),
            jax.ShapeDtypeStruct((windows, length, width), f32),
            jax.ShapeDtypeStruct((2, 8, width), f32),
            jax.ShapeDtypeStruct((channels // LANES, width, LANES), bf16),
        ),
        in_specs=[
            pl.BlockSpec((1, tile, width), rows),
            pl.BlockSpec((1, tile, channels), rows),
            pl.BlockSpec((1, tile, channels), rows),
            pl.BlockSpec((8, width), whole),
            pl.BlockSpec((width,), lambda i: (0,)),
            pl.BlockSpec((width,), lambda i: (0,)),
            pl.BlockSpec((width, channels), whole),
        ],
        out_specs=(
            pl.BlockSpec((1, tile, channels), rows),
            pl.BlockSpec((1, tile, width), rows),
            pl.BlockSpec((2, 8, width), lambda i: (0, 0, 0)),
            pl.BlockSpec((channels // LANES, width, LANES), lambda i: (0, 0, 0)),
        ),
        scratch_shapes=[
            pltpu.VMEM((tile, channels), bf16),
            pltpu.VMEM((tile, width), f32),
            pltpu.VMEM((tile, width), bf16),
            pltpu.VMEM((width, channels), f32),
        ],
        name="conv_three_both",
        **params(6 * narrow.size * channels, 12 * cotangent.size, narrow.size),
    )(narrow, cotangent, pooled, sums, gain, shift, weight)


def conv_two_back_kernel(
    tile, entries, da, da_left, da_right, v, v_left, v_right, sums3, grads3, gain3, pooled, sums2, gain2, shift2,
    h, w_hbm, da_out, stats, w_grad,
    das, vs, ps, hs, low_buf, low_a, low_b, g_buf, outs, total, w_ref, w_flip,
    a_sem, v_sem, p_sem, h_sem, o_sem, w_sem,
):
    windows, length, width = da.shape
    channels = pooled.shape[2]
    thin, slabs = width // LANES, channels // LANES
    walk = Walk(windows, length, tile)
    tiles = walk.count
    low = (low_a, low_b)
    center3, inverse3 = center_inverse(sums3[...], entries)
    grads = grads3[...]
    scale3 = inverse3 * flat_row(gain3)
    lean = scale3 * inverse3 * (grads[0:1] / entries)
    flat = scale3 * (grads[1:2] / entries)
    center, inverse = center_inverse(sums2[...], entries)
    stats[...] = jnp.zeros_like(stats)
    total[...] = jnp.zeros_like(total)

    def load(i, slot):
        walk.fetch(i, da, da_left, da_right, das.at[slot], a_sem.at[slot])
        walk.fetch(i, v, v_left, v_right, vs.at[slot], v_sem.at[slot])

    def wait_load(slot):
        wait_for(das.at[slot], a_sem.at[slot])
        wait_for(vs.at[slot], v_sem.at[slot])

    def late_copies(i, slot):
        w, _ = walk.where(i)
        return (
            pltpu.make_async_copy(pooled.at[w, walk.rows(i)], ps.at[slot], p_sem.at[slot]),
            pltpu.make_async_copy(h.at[w, walk.rows(i)], hs.at[slot], h_sem.at[slot]),
        )

    def o_copy(i, slot):
        w, _ = walk.where(i)
        return pltpu.make_async_copy(outs.at[slot], da_out.at[w, walk.rows(i)], o_sem.at[slot])

    def lower(i, slot, c):
        at, cols = lanes_of(c), lanes(c)
        m, s, l, f = center3[:, at], scale3[:, at], lean[:, at], flat[:, at]
        dst = low[slot]

        def value(q, size):
            return das[slot, q : q + size, cols] * s - (vs[slot, q : q + size, cols] - m) * l - f

        def ends():
            low_buf[c, 0:EDGE] = jnp.where(walk.hide_left(i), 0.0, value(0, EDGE))
            low_buf[c, EDGE + tile : 2 * EDGE + tile] = jnp.where(walk.hide_right(i), 0.0, value(EDGE + tile, EDGE))

        def rows(r):
            def run():
                low_buf[c, EDGE + r : EDGE + r + UNIT] = value(EDGE + r, UNIT)

            return run

        def taps(r):
            def run():
                for tap in range(3):
                    q = EDGE + r - 5 * (tap - 1)
                    dst[r : r + UNIT, lanes(tap * thin + c)] = low_buf[c, q : q + UNIT].astype(bf16)

            return run

        units = [ends, rows(0)]
        for r in range(UNIT, tile, UNIT):
            units += [rows(r), taps(r - UNIT)]
        return units + [taps(tile - UNIT)]

    def finish(slot, c):
        at, cols = lanes_of(c), lanes(c)
        m, inv, g, s = center[:, at], inverse[:, at], gain2[at][None], shift2[at][None]
        sums = [jnp.zeros((8, LANES), f32), jnp.zeros((8, LANES), f32)]

        def rows(r):
            def run():
                normed = (ps[slot, r : r + UNIT, cols] - m) * inv
                back = gelu_slope(normed * g + s) * g_buf[r : r + UNIT, cols]
                outs[slot, r : r + UNIT, cols] = back
                sums[0] = sums[0] + folded(back * normed)
                sums[1] = sums[1] + folded(back)

            return run

        def close():
            stats[0, :, cols] += sums[0]
            stats[1, :, cols] += sums[1]

        return [rows(r) for r in range(0, tile, UNIT)] + [close]

    load(0, 0)
    w_copy = pltpu.make_async_copy(w_hbm, w_ref, w_sem)
    w_copy.start()
    for copy in late_copies(0, 0):
        copy.start()
    wait_load(0)
    load(1, 1)
    for c in range(thin):
        for unit in lower(0, 0, c):
            unit()
    w_copy.wait()
    for k in range(3):
        w_flip[k * width : (k + 1) * width] = w_ref[k].T

    def pair(j, _):
        for slot in range(2):
            i = 2 * j + slot
            other = 1 - slot

            @pl.when(i + 1 < tiles)
            def _():
                wait_load(other)
                for copy in late_copies(i + 1, other):
                    copy.start()

            @pl.when(i + 2 < tiles)
            def _():
                load(i + 2, slot)

            for copy in late_copies(i, slot):
                copy.wait()

            @pl.when(i >= 2)
            def _():
                o_copy(i - 2, slot).wait()

            def back(n):
                def run():
                    cols = lanes(n, 256)
                    g_buf[:, cols] = dot(low[slot][...], w_flip[:, cols])

                return run

            def weigh(n):
                def run():
                    at = slice(n * 256, (n + 1) * 256)
                    total[at] += dot(hs[slot, :, at], low[slot][...], TN)

                return run

            units = []
            for c in range(thin):
                units += lower(i + 1, other, c)
            interleave([back(n) for n in range(channels // 256)], units)
            units = []
            for c in range(slabs):
                units += finish(slot, c)
            interleave([weigh(n) for n in range(channels // 256)], units)
            o_copy(i, slot).start()

        return 0

    lax.fori_loop(0, tiles // 2, pair, 0)
    for c in range(3 * thin):
        w_grad[c] = total[:, lanes_of(c)].astype(bf16)
    o_copy(tiles - 2, 0).wait()
    o_copy(tiles - 1, 1).wait()


def conv_two_back(da, da_sides, v, v_sides, sums3, grads3, gain3, pooled, sums2, gain2, shift2, h, weight, entries):
    windows, length, width = da.shape
    channels = pooled.shape[2]
    tile = min(512, length)
    thin, slabs = width // LANES, channels // LANES
    return pl.pallas_call(
        functools.partial(conv_two_back_kernel, tile, entries),
        out_shape=(
            jax.ShapeDtypeStruct((windows, length, channels), f32),
            jax.ShapeDtypeStruct((2, 8, channels), f32),
            jax.ShapeDtypeStruct((3 * thin, channels, LANES), bf16),
        ),
        in_specs=[ANY] * 6 + [VM] * 3 + [ANY] + [VM] * 3 + [ANY] * 2,
        out_specs=(ANY, VM, VM),
        scratch_shapes=[
            pltpu.VMEM((2, tile + 2 * EDGE, width), f32),
            pltpu.VMEM((2, tile + 2 * EDGE, width), f32),
            pltpu.VMEM((2, tile, channels), f32),
            pltpu.VMEM((2, tile, channels), bf16),
            pltpu.VMEM((thin, tile + 2 * EDGE, LANES), f32),
            pltpu.VMEM((tile, 3 * width), bf16),
            pltpu.VMEM((tile, 3 * width), bf16),
            pltpu.VMEM((tile, channels), f32),
            pltpu.VMEM((2, tile, channels), f32),
            pltpu.VMEM((channels, 3 * width), f32),
            pltpu.VMEM(weight.shape, bf16),
            pltpu.VMEM((3 * width, channels), bf16),
            DMA((2,)),
            DMA((2,)),
            DMA((2,)),
            DMA((2,)),
            DMA((2,)),
            DMA,
        ],
        name="conv_two_back",
        **params(12 * pooled.size * width, 16 * pooled.size, pooled.size),
    )(da, *da_sides, v, *v_sides, sums3, grads3, gain3, pooled, sums2, gain2, shift2, h, weight)


class Reduction:
    STAGES = 8
    LAG = 3

    def __init__(self, data, done, lands, send, recv):
        self.data, self.done, self.lands, self.send, self.recv = data, done, lands, send, recv
        self.chunks, self.rows = data.shape[0], data.shape[1]
        self.steps = self.chunks + self.LAG * self.STAGES
        self.planes = lax.axis_size("dp") // 4
        seq, dp = lax.axis_index("seq"), lax.axis_index("dp")
        self.seq, self.dp = seq, dp
        one, two = dp % 2, (dp // 2) % 2
        swap = seq == 1
        first_bit, second_bit = jnp.where(swap, two, one), jnp.where(swap, one, two)
        to_one, to_two = dp + 1 - 2 * one, dp + 2 - 4 * two
        first_peer, second_peer = jnp.where(swap, to_two, to_one), jnp.where(swap, to_one, to_two)
        self.peers = ({"seq": 1 - seq}, {"dp": first_peer}, {"dp": second_peer})
        self.plane = dp // 4
        rows = self.rows
        self.size = [rows // 2, rows // 4, rows // 8, rows // 8 // self.planes]
        self.base = [seq * self.size[0]]
        self.away = [(1 - seq) * self.size[0]]
        for bit, size in ((first_bit, self.size[1]), (second_bit, self.size[2])):
            self.away.append(self.base[-1] + (1 - bit) * size)
            self.base.append(self.base[-1] + bit * size)

    def part(self, ref, c, start, size):
        return ref.at[c, pl.ds(pl.multiple_of(start, 16), size)]

    def copy(self, c, number, src, dst, peer):
        return pltpu.make_async_remote_copy(
            src_ref=src, dst_ref=dst, send_sem=self.send.at[c, number], recv_sem=self.recv.at[c, number],
            device_id=peer, device_id_type=MESH,
        )

    def copies(self, c, stage):
        size, base = self.size, self.base
        if stage < 3:
            src = self.part(self.data, c, self.away[stage], size[stage])
            return [self.copy(c, stage, src, self.lands[stage].at[c], self.peers[stage])]
        if stage == 3 or stage == 4:
            out = []
            for d in range(1, self.planes):
                there = (self.plane + d) % self.planes
                peer = {"dp": self.dp + (there - self.plane) * 4}
                if stage == 3:
                    src = self.part(self.data, c, base[2] + there * size[3], size[3])
                    dst = self.lands[3].at[c, d - 1]
                else:
                    src = dst = self.part(self.done, c, base[2] + self.plane * size[3], size[3])
                out.append(self.copy(c, 3 + (stage - 3) * (self.planes - 1) + d - 1, src, dst, peer))
            return out
        level = 7 - stage
        mine = self.part(self.done, c, base[level], size[level])
        return [self.copy(c, 2 * (self.planes - 1) + stage - 2, mine, mine, self.peers[level])]

    def launch(self, c, stage):
        for copy in self.copies(c, stage):
            copy.start()

    def arrive(self, c, stage):
        for copy in self.copies(c, stage):
            copy.wait()
        size, base = self.size, self.base
        if stage < 3:
            unit = self.rows // 8

            def add(r, _):
                at = pl.ds(pl.multiple_of(base[stage] + r * unit, 16), unit)
                got = self.lands[stage][c, pl.ds(pl.multiple_of(r * unit, 16), unit)].astype(f32)
                self.data[c, at] = (self.data[c, at].astype(f32) + got).astype(bf16)
                return 0

            lax.fori_loop(0, size[stage] // unit, add, 0)
        elif stage == 3:
            at = pl.ds(pl.multiple_of(base[2] + self.plane * size[3], 16), size[3])
            total = self.data[c, at].astype(f32)
            for d in range(1, self.planes):
                total += self.lands[3][c, d - 1].astype(f32)
            self.done[c, at] = total.astype(bf16)

    def step(self, t):
        for stage in range(self.STAGES, -1, -1):
            c = t - self.LAG * stage

            @pl.when(jnp.logical_and(c >= 0, c < self.chunks))
            def _():
                if stage > 0:
                    self.arrive(c, stage - 1)
                if stage < self.STAGES:
                    self.launch(c, stage)

    @staticmethod
    def fits(rows):
        dps = lax.axis_size("dp")
        return lax.axis_size("seq") == 2 and dps % 4 == 0 and dps > 4 and rows % (128 * (dps // 4)) == 0

    @staticmethod
    def scratch(chunks, rows):
        planes = lax.axis_size("dp") // 4
        copies = 2 * (planes - 1) + 6
        shapes = [(chunks, rows, LANES)] + [(chunks, rows >> (n + 1), LANES) for n in range(3)]
        shapes += [(chunks, planes - 1, rows // 8 // planes, LANES)]
        return [pltpu.VMEM(shape, bf16) for shape in shapes] + [DMA((chunks, copies)), DMA((chunks, copies))]

    @staticmethod
    def of(data, refs):
        return Reduction(data, refs[0], refs[1:5], refs[5], refs[6])


def greet(seqs, dps):
    seq, dp = lax.axis_index("seq"), lax.axis_index("dp")
    barrier = pltpu.get_barrier_semaphore()

    def near(d, _):
        pl.semaphore_signal(barrier, inc=1, device_id={"seq": lax.rem(seq + d, seqs)}, device_id_type=MESH)
        return 0

    def far(d, _):
        pl.semaphore_signal(barrier, inc=1, device_id={"dp": lax.rem(dp + d, dps)}, device_id_type=MESH)
        return 0

    lax.fori_loop(1, seqs, near, 0)
    lax.fori_loop(1, dps, far, 0)
    pl.semaphore_wait(barrier, seqs - 1 + dps - 1)


def conv_one_weigh_kernel(
    tile, entries, joined, seqs, dps, da, da_left, da_right, v, v_left, v_right, ct, ct_left, ct_right, sums2, grads2,
    gain2, s, first, two, three, low_out, w_grad, small, das, vs, cts, ss, firsts, low_buf, low_a, low_b, coef, total,
    packed, data, a_sem, v_sem, c_sem, s_sem, f_sem, l_sem, g_sem, d_sem, *reduction,
):
    windows, length, channels = da.shape
    slabs = channels // LANES
    walk = Walk(windows, length, tile)
    tiles = walk.count
    low = (low_a, low_b)
    half_entries = entries / 2
    center2, inverse2 = center_inverse(sums2[...], half_entries)
    grads = grads2[...]
    scale2 = 0.5 * inverse2 * flat_row(gain2)
    lean = scale2 * inverse2 * (grads[0:1] / half_entries)
    flat = scale2 * (grads[1:2] / half_entries)
    for c in range(slabs):
        for row, values in enumerate((scale2, lean, center2 * lean - flat)):
            coef[c, row : row + 1] = values[:, lanes_of(c)]

    def load(i, slot):
        walk.fetch(i, da, da_left, da_right, das.at[slot], a_sem.at[slot])
        walk.fetch(i, v, v_left, v_right, vs.at[slot], v_sem.at[slot])
        walk.fetch(i, ct, ct_left, ct_right, cts.at[slot], c_sem.at[slot])

    def wait_load(slot):
        wait_for(das.at[slot], a_sem.at[slot])
        wait_for(vs.at[slot], v_sem.at[slot])
        wait_for(cts.at[slot], c_sem.at[slot])

    def s_copy(i, slot):
        w, _ = walk.where(i)
        return pltpu.make_async_copy(s.at[:, w, walk.rows(i)], ss.at[slot], s_sem.at[slot])

    def l_copy(i, slot):
        w, _ = walk.where(i)
        return pltpu.make_async_copy(low[slot], low_out.at[w, walk.rows(i)], l_sem.at[slot])

    def lower(i, slot, c):
        cols = lanes(c)
        sc, l, f = coef[c, 0:1], coef[c, 1:2], coef[c, 2:3]
        dst = low[slot]

        def value(q, size):
            rows = slice(q, q + size)
            return 0.5 * cts[slot, rows, cols] + das[slot, rows, cols] * sc - vs[slot, rows, cols] * l + f

        def ends():
            low_buf[c, 0:EDGE] = jnp.where(walk.hide_left(i), 0.0, value(0, EDGE))
            low_buf[c, EDGE + tile : 2 * EDGE + tile] = jnp.where(walk.hide_right(i), 0.0, value(EDGE + tile, EDGE))

        def rows(r):
            def run():
                low_buf[c, EDGE + r : EDGE + r + UNIT] = value(EDGE + r, UNIT)

            return run

        def taps(r):
            def run():
                for tap in range(3):
                    q = EDGE + r + 1 - tap
                    at = pl.ds(pl.multiple_of(tap * channels + c * LANES, LANES), LANES)
                    dst[r : r + UNIT, at] = low_buf[c, q : q + UNIT].astype(bf16)

            return run

        units = [ends, rows(0)]
        for r in range(UNIT, tile, UNIT):
            units += [rows(r), taps(r - UNIT)]
        return units + [taps(tile - UNIT)]

    load(0, 0)
    wait_load(0)
    s_copy(0, 0).start()
    f_copy = pltpu.make_async_copy(first, firsts, f_sem)
    f_copy.start()
    load(1, 1)
    at = 0
    for src in (two, three):
        size = src.shape[1]
        for c in range(src.shape[0]):
            chunk, start = divmod(at, data.shape[1])
            pltpu.make_async_copy(src.at[c], data.at[chunk, pl.ds(start, size)], d_sem).start()
            at += size
    if joined:
        greet(seqs, dps)
        sharing = Reduction.of(data, reduction)
    total[...] = jnp.zeros_like(total)

    def first_slab(c, _):
        for unit in lower(0, 0, c):
            unit()
        return 0

    lax.fori_loop(0, slabs, first_slab, 0)
    l_copy(0, 0).start()
    f_copy.wait()
    wait_for(data, d_sem)

    def pair(j, _):
        for slot in range(2):
            i = 2 * j + slot
            other = 1 - slot
            w, p = walk.where(i)

            @pl.when(jnp.logical_and(p == 0, walk.at_start))
            def _():
                row = lax.broadcasted_iota(jnp.int32, (16, channels), 0)
                here = jnp.where(row == 0, firsts[w].astype(f32), 0.0).astype(bf16)
                total[1] += dot(here, low[slot][0:16, channels : 2 * channels], TN)

            @pl.when(i + 1 < tiles)
            def _():
                wait_load(other)
                s_copy(i + 1, other).start()

            @pl.when(i + 2 < tiles)
            def _():
                load(i + 2, slot)

            @pl.when(i >= 1)
            def _():
                l_copy(i - 1, other).wait()

            s_copy(i, slot).wait()

            def part(n, _):
                cols = lanes(n, 256)

                def weigh(k):
                    def run():
                        at = pl.ds(pl.multiple_of((k // 2) * channels + n * 256, 256), 256)
                        total[k, :, cols] += dot(ss[slot, k % 2], low[slot][:, at], TN)

                    return run

                units = lower(i + 1, other, 2 * n) + lower(i + 1, other, 2 * n + 1)
                interleave([weigh(k) for k in range(EARLY)], units)
                if joined:
                    sharing.step(i * (channels // 256) + n)
                return 0

            lax.fori_loop(0, channels // 256, part, 0)

            @pl.when(i + 1 < tiles)
            def _():
                l_copy(i + 1, other).start()

        return 0

    lax.fori_loop(0, tiles // 2, pair, 0)
    l_copy(tiles - 1, 1).wait()
    for k in range(EARLY):
        for c in range(slabs):
            packed[k, c] = total[k, :, lanes_of(c)].astype(bf16)
    g_copy = pltpu.make_async_copy(packed, w_grad, g_sem)
    g_copy.start()
    if joined:
        def more(t, _):
            sharing.step(t)
            return 0

        lax.fori_loop(tiles * (channels // 256), sharing.steps, more, 0)
        d_copy = pltpu.make_async_copy(sharing.done, small, d_sem)
    else:
        d_copy = pltpu.make_async_copy(data, small, d_sem)
    d_copy.start()
    d_copy.wait()
    g_copy.wait()


def conv_one_weigh(da, da_sides, v, v_sides, ct, ct_sides, sums2, grads2, gain2, s, first, two, three, entries, number):
    windows, length, channels = da.shape
    tile = min(512, length)
    slabs = channels // LANES
    packed = (EARLY, slabs, channels, LANES)
    rows = 2 * channels
    chunks = (two.shape[0] * two.shape[1] + three.shape[0] * three.shape[1]) // rows
    joined = Reduction.fits(rows)
    estimate = params(4 * EARLY * da.size * channels, 24 * da.size, 0)
    if joined:
        estimate["compiler_params"] = pltpu.CompilerParams(
            vmem_limit_bytes=VMEM_LIMIT, collective_id=number, has_side_effects=True
        )
    low, parts, small = pl.pallas_call(
        functools.partial(conv_one_weigh_kernel, tile, entries, joined, lax.axis_size("seq"), lax.axis_size("dp")),
        out_shape=(
            jax.ShapeDtypeStruct((windows, length, 3 * channels), bf16),
            jax.ShapeDtypeStruct(packed, bf16),
            jax.ShapeDtypeStruct((chunks, rows, LANES), bf16),
        ),
        in_specs=[ANY] * 9 + [VM] * 3 + [ANY] * 4,
        out_specs=(ANY, ANY, ANY),
        scratch_shapes=[
            pltpu.VMEM((2, tile + 2 * EDGE, channels), f32),
            pltpu.VMEM((2, tile + 2 * EDGE, channels), f32),
            pltpu.VMEM((2, tile + 2 * EDGE, channels), f32),
            pltpu.VMEM((2, 2, tile, channels), bf16),
            pltpu.VMEM(first.shape, bf16),
            pltpu.VMEM((slabs, tile + 2 * EDGE, LANES), f32),
            pltpu.VMEM((tile, 3 * channels), bf16),
            pltpu.VMEM((tile, 3 * channels), bf16),
            pltpu.VMEM((slabs, 8, LANES), f32),
            pltpu.VMEM((EARLY, channels, channels), f32),
            pltpu.VMEM(packed, bf16),
            pltpu.VMEM((chunks, rows, LANES), bf16),
        ]
        + [DMA((2,))] * 4
        + [DMA, DMA((2,)), DMA, DMA]
        + (Reduction.scratch(chunks, rows) if joined else []),
        name="conv_one_weigh",
        **estimate,
    )(da, *da_sides, v, *v_sides, ct, *ct_sides, sums2, grads2, gain2, s, first, two, three)
    if not joined:
        small = lax.psum(small, ("dp", "seq"))
    return low, parts, small


def conv_one_spread_kernel(
    tile, entries, joined, seqs, dps, low, x, sums1, gain1, shift1, w_hbm, s, parts, da_out, stats, w_grad,
    lows, xs, g_buf, outs, coef, w_ref, total, ss, ls, data, l_sem, x_sem, o_sem, w_sem, d_sem, t_sem, *reduction,
):
    windows, length, _ = low.shape
    channels = x.shape[2]
    slabs = channels // LANES
    span = 2 * tile
    walk = Walk(windows, length, tile)
    tiles = walk.count
    center, inverse = center_inverse(sums1[...], entries)
    for c in range(slabs):
        for row, values in enumerate((center, inverse, flat_row(gain1), flat_row(shift1))):
            coef[c, row : row + 1] = values[:, lanes_of(c)]
    stats[...] = jnp.zeros_like(stats)

    def l_copy(i, slot):
        w, _ = walk.where(i)
        return pltpu.make_async_copy(low.at[w, walk.rows(i)], lows.at[slot], l_sem.at[slot])

    def x_copy(i, slot):
        w, _ = walk.where(i)
        return pltpu.make_async_copy(x.at[w, walk.rows(i, 2)], xs.at[slot], x_sem.at[slot])

    def o_copy(i, slot):
        w, _ = walk.where(i)
        return pltpu.make_async_copy(outs.at[slot], da_out.at[w, walk.rows(i, 2)], o_sem.at[slot])

    def t_copies(g, slot):
        k = EARLY + g // tiles
        w, _ = walk.where(g % tiles)
        rows = walk.rows(g % tiles)
        at = pl.ds(pl.multiple_of((k // 2) * channels, channels), channels)
        return (
            pltpu.make_async_copy(s.at[k % 2, w, rows], ss.at[slot], t_sem.at[slot, 0]),
            pltpu.make_async_copy(low.at[w, rows, at], ls.at[slot], t_sem.at[slot, 1]),
        )

    d_copy = pltpu.make_async_copy(parts, data.at[pl.ds(0, EARLY * slabs // 2)], d_sem)
    d_copy.start()
    for copy in t_copies(0, 0):
        copy.start()
    if joined:
        greet(seqs, dps)
    d_copy.wait()
    l_copy(0, 0).start()
    w_copy = pltpu.make_async_copy(w_hbm, w_ref, w_sem)
    w_copy.start()
    if joined:
        sharing = Reduction.of(data, reduction)
        sharing.step(0)

    late = (5 - EARLY) * tiles
    triple = slabs // 2

    def due(g):
        whole, part = g // tiles, g % tiles
        first = jnp.where(whole == 0, 1, (EARLY + whole - 1) * triple)
        count = jnp.where(whole == 0, EARLY * triple - 1, triple)
        return first + count * part // tiles, first + count * (part + 1) // tiles

    def weigh(g, _):
        slot = g % 2
        for copy in t_copies(g, slot):
            copy.wait()

        @pl.when(g + 1 < late)
        def _():
            for copy in t_copies(g + 1, 1 - slot):
                copy.start()

        @pl.when(g % tiles == 0)
        def _():
            total[...] = dot(ss[slot], ls[slot], TN)

        @pl.when(g % tiles > 0)
        def _():
            total[...] += dot(ss[slot], ls[slot], TN)

        @pl.when(g % tiles == tiles - 1)
        def _():
            for c in range(slabs):
                at = slice((c % 2) * channels, (c % 2 + 1) * channels)
                data[(EARLY + g // tiles) * triple + c // 2, at] = total[:, lanes_of(c)].astype(bf16)

        if joined:
            def take(t, _):
                sharing.step(t)
                return 0

            lax.fori_loop(*due(g), take, 0)

        return 0

    lax.fori_loop(0, late, weigh, 0)
    w_copy.wait()

    def finish(slot, c):
        cols = lanes(c)
        m, inv, g, sh = (coef[c, row : row + 1] for row in range(4))
        held = [jnp.zeros((8, LANES), f32), jnp.zeros((8, LANES), f32)]

        def rows(r):
            def run():
                normed = (xs[slot, r : r + UNIT, cols] - m) * inv
                incoming = g_buf[slot, c, EDGE + r : EDGE + r + UNIT] + g_buf[slot, c, EDGE + r - 1 : EDGE + r - 1 + UNIT]
                back = gelu_slope(normed * g + sh) * incoming
                outs[slot, r : r + UNIT, cols] = back.astype(bf16)
                held[0] = held[0] + folded(back * normed)
                held[1] = held[1] + folded(back)

            return run

        def close():
            stats[0, :, cols] += held[0]
            stats[1, :, cols] += held[1]

        return [rows(r) for r in range(0, span, UNIT)] + [close]

    def spread(slot, n):
        at = lanes(n, 256)

        def even():
            part = dot(lows[slot, :, 0:channels], w_ref[0, at], NT)
            part += dot(lows[slot, :, channels : 2 * channels], w_ref[2, at], NT)
            part += dot(lows[slot, :, 2 * channels : 3 * channels], w_ref[4, at], NT)
            for c in range(2):
                g_buf[slot, 2 * n + c, pl.ds(EDGE, tile, stride=2)] = part[:, lanes_of(c)]

        def odd():
            part = dot(lows[slot, :, 0:channels], w_ref[1, at], NT)
            part += dot(lows[slot, :, channels : 2 * channels], w_ref[3, at], NT)
            for c in range(2):
                g_buf[slot, 2 * n + c, pl.ds(EDGE + 1, tile, stride=2)] = part[:, lanes_of(c)]

        return [even, odd]

    def turn(i, slot, last):
        other = 1 - slot
        w, p = walk.where(i)
        if not last:
            l_copy(i, slot).wait()

            @pl.when(i + 1 < tiles)
            def _():
                l_copy(i + 1, other).start()

            @pl.when(p == 0)
            def _():
                edge = lows[slot, 0:16]
                part = dot(edge[:, channels : 2 * channels], w_ref[1], NT) + dot(edge[:, 2 * channels :], w_ref[3], NT)
                for c in range(slabs):
                    g_buf[slot, c, EDGE - 1 : EDGE] = part[0:1, lanes_of(c)]

            @pl.when(p > 0)
            def _():
                for c in range(slabs):
                    g_buf[slot, c, EDGE - 1 : EDGE] = g_buf[other, c, EDGE + span - 1 : EDGE + span]

        @pl.when(i >= 1)
        def _():
            x_copy(i - 1, other).wait()

        @pl.when(i >= 3)
        def _():
            o_copy(i - 3, other).wait()

        if not last:
            x_copy(i, slot).start()

        def part(n, _):
            units = finish(other, 2 * n) + finish(other, 2 * n + 1)
            interleave([] if last else spread(slot, n), units)
            if last:
                for unit in units:
                    unit()
            elif joined:
                sharing.step(4 * triple + i * (channels // 256) + n)
            return 0

        lax.fori_loop(0, channels // 256, part, 0)

        @pl.when(i >= 1)
        def _():
            o_copy(i - 1, other).start()

    xs[1] = jnp.zeros(xs.shape[1:], f32)
    g_buf[1] = jnp.zeros(g_buf.shape[1:], f32)

    def pair(j, _):
        for slot in range(2):
            turn(2 * j + slot, slot, False)
        return 0

    lax.fori_loop(0, tiles // 2, pair, 0)
    turn(tiles, 0, True)
    o_copy(tiles - 2, 0).wait()
    o_copy(tiles - 1, 1).wait()
    if joined:
        def more(t, _):
            sharing.step(t)
            return 0

        lax.fori_loop(4 * triple + tiles * (channels // 256), sharing.steps, more, 0)
    d_copy = pltpu.make_async_copy(sharing.done if joined else data, w_grad, d_sem)
    d_copy.start()
    d_copy.wait()


def conv_one_spread(low, x, sums1, gain1, shift1, weight, s, parts, entries, number):
    windows, length, _ = low.shape
    channels = x.shape[2]
    tile = min(512, length)
    slabs = channels // LANES
    rows, chunks = 2 * channels, 5 * slabs // 2
    parts = parts.reshape(EARLY * slabs // 2, rows, LANES)
    joined = Reduction.fits(rows)
    estimate = params(10 * low.size * channels // 3, 12 * x.size, x.size)
    if joined:
        estimate["compiler_params"] = pltpu.CompilerParams(
            vmem_limit_bytes=VMEM_LIMIT, collective_id=number, has_side_effects=True
        )
    da, stats, grad = pl.pallas_call(
        functools.partial(conv_one_spread_kernel, tile, entries, joined, lax.axis_size("seq"), lax.axis_size("dp")),
        out_shape=(
            jax.ShapeDtypeStruct((windows, 2 * length, channels), bf16),
            jax.ShapeDtypeStruct((2, 8, channels), f32),
            jax.ShapeDtypeStruct((chunks, rows, LANES), bf16),
        ),
        in_specs=[ANY] * 2 + [VM] * 3 + [ANY] * 3,
        out_specs=(ANY, VM, ANY),
        scratch_shapes=[
            pltpu.VMEM((2, tile, 3 * channels), bf16),
            pltpu.VMEM((2, 2 * tile, channels), f32),
            pltpu.VMEM((2, slabs, 2 * tile + 2 * EDGE, LANES), f32),
            pltpu.VMEM((2, 2 * tile, channels), bf16),
            pltpu.VMEM((slabs, 8, LANES), f32),
            pltpu.VMEM(weight.shape, bf16),
            pltpu.VMEM((channels, channels), f32),
            pltpu.VMEM((2, tile, channels), bf16),
            pltpu.VMEM((2, tile, channels), bf16),
            pltpu.VMEM((chunks, rows, LANES), bf16),
            DMA((2,)),
            DMA((2,)),
            DMA((2,)),
            DMA,
            DMA,
            DMA((2, 2)),
        ]
        + (Reduction.scratch(chunks, rows) if joined else []),
        name="conv_one_spread",
        **estimate,
    )(low, x, sums1, gain1, shift1, weight, s, parts)
    if not joined:
        grad = lax.psum(grad, ("dp", "seq"))
    return da, stats, grad


def widen_kernel(one, small, grads1, grads2, grads3, one_out, two_out, three_out, *vectors):
    for c in range(one.shape[1]):
        one_out[0, :, lanes_of(c)] = one[0, c].astype(f32)

    @pl.when(pl.program_id(0) == 0)
    def _():
        taps, rows, width = two_out.shape
        at = 0
        for k in range(taps):
            for c in range(width // LANES):
                two_out[k, :, lanes_of(c)] = small[at : at + rows].astype(f32)
                at += rows
        rows = three_out.shape[0]
        for c in range(three_out.shape[1] // LANES):
            three_out[:, lanes_of(c)] = small[at : at + rows].astype(f32)
            at += rows
        for n, grads in enumerate((grads1, grads2, grads3)):
            vectors[2 * n][...] = grads[0]
            vectors[2 * n + 1][...] = grads[1]


def widen(one, small, two_shape, three_shape, grads):
    channels = two_shape[1]
    slabs = channels // LANES
    one = one.reshape(5, slabs, channels, LANES)
    small = small.reshape(-1, LANES)
    flat = lambda k: (0, 0)
    lengths = [g.shape[1] for g in grads for _ in range(2)]
    return pl.pallas_call(
        widen_kernel,
        grid=(5,),
        out_shape=[
            jax.ShapeDtypeStruct((5, channels, channels), f32),
            jax.ShapeDtypeStruct(two_shape, f32),
            jax.ShapeDtypeStruct(three_shape, f32),
        ]
        + [jax.ShapeDtypeStruct((n,), f32) for n in lengths],
        in_specs=[pl.BlockSpec((1, slabs, channels, LANES), lambda k: (k, 0, 0, 0)), pl.BlockSpec(small.shape, flat)]
        + [pl.BlockSpec(g.shape, flat) for g in grads],
        out_specs=[
            pl.BlockSpec((1, channels, channels), lambda k: (k, 0, 0)),
            pl.BlockSpec(two_shape, lambda k: (0, 0, 0)),
            pl.BlockSpec(three_shape, flat),
        ]
        + [pl.BlockSpec((n,), lambda k: (0,)) for n in lengths],
        name="widen",
        **params(moved=6 * one.size),
    )(one, small, *grads)


def last_kernel(entries, x, da, sums, grads, gain, out):
    center, inverse = center_inverse(sums[...], entries)
    both = grads[...]
    scale = inverse * flat_row(gain)
    lean = scale * inverse * (both[0:1] / entries)
    flat = scale * (both[1:2] / entries)
    for c in range(x.shape[2] // LANES):
        cols, at = lanes(c), lanes_of(c)
        m, s, l, f = center[:, at], scale[:, at], lean[:, at], flat[:, at]
        for r in range(0, x.shape[1], 128):
            rows = slice(r, r + 128)
            out[0, rows, cols] = da[0, rows, cols].astype(f32) * s - (x[0, rows, cols] - m) * l - f


def input_back(x, da, sums, grads, gain, entries):
    windows, length, channels = x.shape
    tile = min(512, length)
    per = length // tile
    rows = pl.BlockSpec((1, tile, channels), lambda i: (i // per, i % per, 0))
    whole = lambda i: (0, 0)
    return pl.pallas_call(
        functools.partial(last_kernel, entries),
        grid=(windows * per,),
        out_shape=jax.ShapeDtypeStruct(x.shape, f32),
        in_specs=[
            rows,
            rows,
            pl.BlockSpec((8, channels), whole),
            pl.BlockSpec((8, channels), whole),
            pl.BlockSpec((channels,), lambda i: (0,)),
        ],
        out_specs=rows,
        name="input_back",
        **params(moved=10 * x.size),
    )(x, da, sums, grads, gain)


def on_device(
    inputs,
    conv_one,
    conv_two,
    conv_three,
    gain_one,
    shift_one,
    gain_two,
    shift_two,
    gain_three,
    shift_three,
    cotangent,
):
    windows, length, channels = inputs.shape
    entries = float(windows * length * lax.axis_size("dp") * lax.axis_size("seq"))
    half = entries / 2
    sums1, (x_left, x_right, c_left, c_right) = exchange(input_sums(inputs), [inputs, cotangent], 0)
    pooled, s, first, stats = conv_one_forward(
        inputs, x_left, x_right, sums1, gain_one, shift_one, conv_one, entries
    )
    sums2, p_sides = exchange(stats, [pooled], 1)
    narrow, hidden_two, stats = conv_two_forward(pooled, *p_sides, sums2, gain_two, shift_two, conv_two, half)
    sums3, n_sides = exchange(stats, [narrow], 2)
    outputs, da3, stats, three_grad = conv_three_both(
        narrow, cotangent, pooled, sums3, gain_three, shift_three, conv_three, half
    )
    grads3, a_sides = exchange(stats, [da3], 3)
    da2, stats, two_grad = conv_two_back(
        da3, a_sides, narrow, n_sides, sums3, grads3, gain_three, pooled, sums2, gain_two, shift_two,
        hidden_two, conv_two, half,
    )
    grads2, b_sides = exchange(stats, [da2], 4)
    low, parts, small = conv_one_weigh(
        da2, b_sides, pooled, p_sides, cotangent, (c_left, c_right), sums2, grads2, gain_two, s, first,
        two_grad, three_grad, entries, 7,
    )
    da1, stats, one_grad = conv_one_spread(
        low, inputs, sums1, gain_one, shift_one, conv_one, s, parts, entries, 6
    )
    grads1, _ = exchange(stats, [], 5)
    input_grad = input_back(inputs, da1, sums1, grads1, gain_one, entries)
    small_grads = widen(one_grad, small, conv_two.shape, conv_three.shape, (grads1, grads2, grads3))
    return (outputs, input_grad, *small_grads)


def solution(mesh):
    rows = P("dp", "seq", None)
    in_specs = (rows,) + (P(),) * 9 + (rows,)
    out_specs = (rows, rows) + (P(),) * 9
    return jax.shard_map(on_device, mesh=mesh, in_specs=in_specs, out_specs=out_specs, check_vma=False)
```

```python
import functools

import jax
import jax.numpy as jnp
from jax import lax
from jax.experimental import pallas as pl
from jax.experimental.pallas import tpu as pltpu
from jax.sharding import PartitionSpec as P

epsilon = 1e-05
bf16 = jnp.bfloat16
f32 = jnp.float32
LANES = 128
UNIT = 64
SUB = 32
EDGE = 8
MESH = pl.DeviceIdType.MESH
LINEAR = 0.7978845608028654
CUBIC = 0.7978845608028654 * 0.044715
VMEM_LIMIT = 60 << 20
EARLY = 3
AHEAD = 3
NN = (((1,), (0,)), ((), ()))
NT = (((1,), (1,)), ((), ()))
TN = (((0,), (0,)), ((), ()))


def dot(a, b, dims=NN):
    return lax.dot_general(a, b, dims, preferred_element_type=f32)


def gelu(v):
    half = 0.5 * v
    return half + half * jnp.tanh(v * (LINEAR + CUBIC * (v * v)))


ROOT = CUBIC ** (1.0 / 3.0)
BEND = LINEAR / ROOT


def gelu_scaled(q):
    return q * (1.0 + jnp.tanh(q * (BEND + q * q)))


def slope_scaled(q):
    square = q * q
    th = jnp.tanh(q * (BEND + square))
    return (1.0 + th) * (1.0 + (1.0 - th) * (q * (BEND + 3.0 * square)))


def gelu_both(v):
    square = v * v
    up = 0.5 + 0.5 * jnp.tanh(v * (LINEAR + CUBIC * square))
    value = v * up
    slope = up + value * (1.0 - up) * (2.0 * LINEAR + (6.0 * CUBIC) * square)
    return value, slope


def gelu_slope(v):
    square = v * v
    up = 0.5 + 0.5 * jnp.tanh(v * (LINEAR + CUBIC * square))
    return up + (v * up) * (1.0 - up) * (2.0 * LINEAR + (6.0 * CUBIC) * square)


def center_inverse(sums, entries):
    center = sums[0:1] / entries
    return center, lax.rsqrt(sums[1:2] / entries - center * center + epsilon)


def flat_row(v):
    return v[...].reshape(1, v.shape[0])


def lanes(c, width=LANES):
    if isinstance(c, int):
        return pl.ds(c * width, width)
    return pl.ds(pl.multiple_of(c * width, width), width)


def folded(values):
    return jnp.sum(values.reshape(values.shape[0] // 8, 8, values.shape[1]), axis=0)


def interleave(pieces, units):
    done = 0
    for k, piece in enumerate(pieces):
        piece()
        until = (k + 1) * len(units) // len(pieces)
        for unit in units[done:until]:
            unit()
        done = until


def place_flags():
    return lax.axis_index("seq") == 0, lax.axis_index("seq") == lax.axis_size("seq") - 1


class Walk:
    def __init__(self, windows, length, tile):
        self.tile = tile
        self.per = length // tile
        self.count = windows * self.per
        self.at_start, self.at_end = place_flags()

    def where(self, i):
        return i // self.per, i % self.per

    def hide_left(self, i):
        return jnp.logical_and(i % self.per == 0, self.at_start)

    def hide_right(self, i):
        return jnp.logical_and(i % self.per == self.per - 1, self.at_end)

    def rows(self, i, scale=1):
        span = self.tile * scale
        return pl.ds(pl.multiple_of((i % self.per) * span, span), span)

    def fetch(self, i, src, left, right, dst, sem, scale=1):
        w, p = self.where(i)
        span = self.tile * scale
        low = pl.multiple_of(p * span, span)
        first, last = p == 0, p == self.per - 1
        pltpu.make_async_copy(src.at[w, pl.ds(low, span)], dst.at[pl.ds(EDGE, span)], sem).start()
        head, tail = dst.at[pl.ds(0, EDGE)], dst.at[pl.ds(EDGE + span, EDGE)]

        @pl.when(first)
        def _():
            pltpu.make_async_copy(left.at[w], head, sem).start()

        @pl.when(jnp.logical_not(first))
        def _():
            pltpu.make_async_copy(src.at[w, pl.ds(pl.multiple_of(low - EDGE, EDGE), EDGE)], head, sem).start()

        @pl.when(last)
        def _():
            pltpu.make_async_copy(right.at[w], tail, sem).start()

        @pl.when(jnp.logical_not(last))
        def _():
            pltpu.make_async_copy(src.at[w, pl.ds(pl.multiple_of(low + span, EDGE), EDGE)], tail, sem).start()


def wait_for(dst, sem):
    pltpu.make_async_copy(dst, dst, sem).wait()


ANY = pl.BlockSpec(memory_space=pl.ANY)
VM = pl.BlockSpec(memory_space=pltpu.VMEM)
DMA = pltpu.SemaphoreType.DMA


def params(flops=0, moved=0, waved=0):
    return dict(
        compiler_params=pltpu.CompilerParams(vmem_limit_bytes=VMEM_LIMIT),
        cost_estimate=pl.CostEstimate(flops=flops, bytes_accessed=moved, transcendentals=waved),
    )


def greet(seqs, dps):
    seq, dp = lax.axis_index("seq"), lax.axis_index("dp")
    barrier = pltpu.get_barrier_semaphore()

    def near(d, _):
        pl.semaphore_signal(barrier, inc=1, device_id={"seq": lax.rem(seq + d, seqs)}, device_id_type=MESH)
        return 0

    def far(d, _):
        pl.semaphore_signal(barrier, inc=1, device_id={"dp": lax.rem(dp + d, dps)}, device_id_type=MESH)
        return 0

    lax.fori_loop(1, seqs, near, 0)
    lax.fori_loop(1, dps, far, 0)
    pl.semaphore_wait(barrier, seqs - 1 + dps - 1)


class Exchange:
    SUMS = 7

    def __init__(self, refs, edge_refs=()):
        self.message, self.near, self.far, self.near_send, self.near_recv, self.far_send, self.far_recv = refs
        self.seqs, self.dps = self.near.shape[0], self.far.shape[0]
        self.seq, self.dp = lax.axis_index("seq"), lax.axis_index("dp")
        if edge_refs:
            self.lands, (self.edge_send, self.edge_recv) = edge_refs[:-2], edge_refs[-2:]

    @staticmethod
    def scratch(channels):
        seqs, dps = lax.axis_size("seq"), lax.axis_size("dp")
        rows = -(-2 * (channels // LANES) // 8) * 8
        return [
            pltpu.VMEM((rows, LANES), f32),
            pltpu.VMEM((seqs, rows, LANES), f32),
            pltpu.VMEM((dps, rows, LANES), f32),
            DMA((seqs,)),
            DMA((seqs,)),
            DMA((dps,)),
            DMA((dps,)),
        ]

    @staticmethod
    def edges(arrays):
        return [jax.ShapeDtypeStruct((a.shape[0], EDGE, a.shape[2]), a.dtype) for a in arrays for _ in range(2)]

    @staticmethod
    def edge_scratch(arrays):
        edges = Exchange.edges(arrays)
        return [pltpu.VMEM(e.shape, e.dtype) for e in edges] + [DMA((len(edges),)), DMA((len(edges),))]

    def edge_copy(self, n, src):
        length = src.shape[1]
        part = src.at[:, pl.ds(length - EDGE, EDGE)] if n % 2 == 0 else src.at[:, pl.ds(0, EDGE)]
        to = self.seq + 1 if n % 2 == 0 else self.seq - 1
        return pltpu.make_async_remote_copy(
            src_ref=part, dst_ref=self.lands[n], send_sem=self.edge_send.at[n], recv_sem=self.edge_recv.at[n],
            device_id={"seq": to}, device_id_type=MESH,
        )

    def start_edges(self, sources):
        for a, src in enumerate(sources):
            @pl.when(self.seq < self.seqs - 1)
            def _():
                self.edge_copy(2 * a, src).start()

            @pl.when(self.seq > 0)
            def _():
                self.edge_copy(2 * a + 1, src).start()

    def finish_edges(self, sources):
        for a, src in enumerate(sources):
            @pl.when(self.seq < self.seqs - 1)
            def _():
                self.edge_copy(2 * a, src).wait_send()
                self.edge_copy(2 * a + 1, src).wait_recv()

            @pl.when(self.seq > 0)
            def _():
                self.edge_copy(2 * a + 1, src).wait_send()
                self.edge_copy(2 * a, src).wait_recv()

    def near_copy(self, d):
        return pltpu.make_async_remote_copy(
            src_ref=self.message, dst_ref=self.near.at[self.seq], send_sem=self.near_send.at[d],
            recv_sem=self.near_recv.at[d], device_id={"seq": lax.rem(self.seq + d, self.seqs)}, device_id_type=MESH,
        )

    def far_copy(self, d):
        mine = self.far.at[self.dp]
        return pltpu.make_async_remote_copy(
            src_ref=mine, dst_ref=mine, send_sem=self.far_send.at[d], recv_sem=self.far_recv.at[d],
            device_id={"dp": lax.rem(self.dp + d, self.dps)}, device_id_type=MESH,
        )

    def each(self, count, run):
        def body(d, _):
            run(d)
            return 0

        lax.fori_loop(1, count, body, 0)

    def start_sums(self, stats):
        slabs = stats.shape[2] // LANES
        self.message[...] = jnp.zeros_like(self.message)
        for row in range(2):
            total = jnp.sum(stats[row], axis=0, keepdims=True)
            for c in range(slabs):
                self.message[row * slabs + c : row * slabs + c + 1] = total[:, lanes_of(c)]
        self.each(self.seqs, lambda d: self.near_copy(d).start())
        self.near[self.seq] = self.message[...]
        self.each(self.seqs, lambda d: self.near_copy(d).wait())
        self.far[self.dp] = lax.fori_loop(1, self.seqs, lambda n, t: t + self.near[n], self.near[0])
        self.each(self.dps, lambda d: self.far_copy(d).start())

    def finish_sums(self, sums):
        slabs = sums.shape[1] // LANES
        self.each(self.dps, lambda d: self.far_copy(d).wait())
        total = lax.fori_loop(1, self.dps, lambda n, t: t + self.far[n], self.far[0])
        sums[...] = jnp.zeros_like(sums)
        for row in range(2):
            for c in range(slabs):
                sums[row : row + 1, lanes_of(c)] = total[row * slabs + c : row * slabs + c + 1]


def lanes_of(c):
    return slice(c * LANES, (c + 1) * LANES)


def exchange_kernel(arrays, *refs):
    stats, sources, sums = refs[0], refs[1 : 1 + arrays], refs[1 + arrays]
    outs, scratch = refs[2 + arrays : 2 + 3 * arrays], refs[2 + 3 * arrays :]
    talk = Exchange(scratch[: Exchange.SUMS], scratch[Exchange.SUMS :])
    greet(talk.seqs, talk.dps)
    talk.start_edges(sources)
    talk.start_sums(stats)
    talk.finish_edges(sources)
    for out, land in zip(outs, talk.lands):
        out[...] = land[...]
    talk.finish_sums(sums)


def exchange(stats, arrays, number):
    channels = stats.shape[2]
    edges = Exchange.edges(arrays)
    got = pl.pallas_call(
        functools.partial(exchange_kernel, len(arrays)),
        out_shape=[jax.ShapeDtypeStruct((8, channels), f32)] + edges,
        in_specs=[VM] + [ANY] * len(arrays),
        out_specs=[VM] * (1 + len(edges)),
        scratch_shapes=Exchange.scratch(channels) + Exchange.edge_scratch(arrays),
        compiler_params=pltpu.CompilerParams(collective_id=number, has_side_effects=True),
        name=f"exchange_{number}",
    )(stats, *arrays)
    return got[0], got[1:]


def joining(estimate, number):
    return dict(
        estimate,
        compiler_params=pltpu.CompilerParams(
            vmem_limit_bytes=VMEM_LIMIT, collective_id=number, has_side_effects=True
        ),
    )


def conv_one_kernel(
    tile, entries, x, cotangent, gain, shift, w_hbm,
    pooled, s_out, first_out, sums1, sums2, c_left, c_right, p_left, p_right,
    xs, h_buf, lhs_a, lhs_b, outs, coef, w_ref, stats, x_sem, s_sem, f_sem, o_sem, w_sem, *talks,
):
    windows, length, channels = x.shape
    slabs = channels // LANES
    span = 2 * tile
    walk = Walk(windows, length // 2, tile)
    tiles = walk.count
    lhs = (lhs_a, lhs_b)
    n = Exchange.SUMS
    talk1 = Exchange(talks[:n], talks[2 * n : 2 * n + 6])
    talk2 = Exchange(talks[n : 2 * n], talks[2 * n + 6 :])
    left, right = talk1.lands[:2]

    def scan_copy(i, slot):
        w, _ = walk.where(i)
        return pltpu.make_async_copy(x.at[w, walk.rows(i, 2)], xs.at[slot, pl.ds(EDGE, span)], x_sem.at[slot])

    scan_copy(0, 0).start()
    scan_copy(1, 1).start()
    greet(talk1.seqs, talk1.dps)
    talk1.start_edges((x, cotangent))
    stats[...] = jnp.zeros_like(stats)

    def scan(i, _):
        slot = i % 2
        scan_copy(i, slot).wait()

        def slab(c, _):
            cols = lanes(c)
            total = jnp.zeros((8, LANES), f32)
            squares = jnp.zeros((8, LANES), f32)
            for r in range(EDGE, EDGE + span, 128):
                v = xs[slot, r : r + 128, cols]
                total += folded(v)
                squares += folded(v * v)
            stats[0, :, cols] += total
            stats[1, :, cols] += squares
            return 0

        lax.fori_loop(0, slabs, slab, 0)

        @pl.when(i + 2 < tiles)
        def _():
            scan_copy(i + 2, slot).start()

        return 0

    lax.fori_loop(0, tiles, scan, 0)
    talk1.start_sums(stats)
    w_copy = pltpu.make_async_copy(w_hbm, w_ref, w_sem)

    def load(i, slot):
        walk.fetch(i, x, left, right, xs.at[slot], x_sem.at[slot], 2)

    def s_copy(i, slot, which):
        w, _ = walk.where(i)
        return pltpu.make_async_copy(
            lhs[slot].at[:, pl.ds((2 + which) * channels, channels)], s_out.at[which, w, walk.rows(i)],
            s_sem.at[slot, which],
        )

    def first_copy(i, slot):
        w, _ = walk.where(i)
        return pltpu.make_async_copy(
            lhs[slot].at[pl.ds(0, 16), pl.ds(channels, channels)], first_out.at[w], f_sem
        )

    def o_copy(i, slot):
        w, _ = walk.where(i)
        return pltpu.make_async_copy(outs.at[slot], pooled.at[w, walk.rows(i)], o_sem.at[slot])

    def activate(i, slot, c):
        scale = coef[c, 0:1]
        offset = coef[c, 1:2]
        src = xs.at[slot]
        dst = lhs[slot]
        cols = lanes(c)

        def ends():
            head = gelu_scaled(src[0:EDGE, cols] * scale + offset)
            h_buf[c, 0:EDGE] = jnp.where(walk.hide_left(i), 0.0, head)
            tail = gelu_scaled(src[EDGE + span : 2 * EDGE + span, cols] * scale + offset)
            h_buf[c, EDGE + span : 2 * EDGE + span] = jnp.where(walk.hide_right(i), 0.0, tail)

        def rows(r):
            def run():
                for q in range(EDGE + r, EDGE + r + 2 * UNIT, 2 * SUB):
                    h_buf[c, q : q + 2 * SUB] = gelu_scaled(src[q : q + 2 * SUB, cols] * scale + offset)

            return run

        def taps(r):
            def run():
                for q in range(r, r + UNIT, SUB):
                    h = [h_buf[c, pl.ds(EDGE + 2 * q + d, SUB, stride=2)] for d in range(-2, 4)]
                    for tap in range(5):
                        at = pl.ds(pl.multiple_of(tap * channels + c * LANES, LANES), LANES)
                        dst[q : q + SUB, at] = (h[tap] + h[tap + 1]).astype(bf16)

            return run

        units = [ends, rows(0)]
        for r in range(UNIT, tile, UNIT):
            units += [rows(2 * r), taps(r - UNIT)]
        return units + [taps(tile - UNIT)]

    def matmul(slot, n):
        cols = lanes(n, 256)
        src = lhs[slot]
        held = []

        def piece(k):
            def run():
                at = slice(k * channels, (k + 1) * channels)
                part = dot(src[:, at], w_ref[at, cols])
                held[:] = [held[0] + part] if held else [part]

            return run

        def finish():
            total = (0.25 / ROOT) * held[0]
            outs[slot, :, cols] = total
            stats[0, :, cols] += folded(total)
            stats[1, :, cols] += folded(total * total)

        return [piece(k) for k in range(5)], finish

    talk1.finish_edges((x, cotangent))
    c_left[...] = talk1.lands[2][...]
    c_right[...] = talk1.lands[3][...]
    load(0, 0)
    load(1, 1)
    w_copy.start()
    talk1.finish_sums(sums1)
    center, inverse = center_inverse(sums1[...], entries)
    scale = inverse * flat_row(gain)
    offset = flat_row(shift) - center * scale
    for c in range(slabs):
        coef[c, 0:1] = ROOT * scale[:, lanes_of(c)]
        coef[c, 1:2] = ROOT * offset[:, lanes_of(c)]
    stats[...] = jnp.zeros_like(stats)
    wait_for(xs.at[0], x_sem.at[0])

    def first_slab(c, _):
        for unit in activate(0, 0, c):
            unit()
        return 0

    lax.fori_loop(0, slabs, first_slab, 0)
    for which in range(2):
        s_copy(0, 0, which).start()
    first_copy(0, 0).start()
    w_copy.wait()

    def pair(j, _):
        for slot in range(2):
            i = 2 * j + slot
            other = 1 - slot

            @pl.when(i + 1 < tiles)
            def _():
                wait_for(xs.at[other], x_sem.at[other])

            @pl.when(i + 2 < tiles)
            def _():
                load(i + 2, slot)

            @pl.when(i >= 1)
            def _():
                for which in range(2):
                    s_copy(i - 1, other, which).wait()

                @pl.when((i - 1) % walk.per == 0)
                def _():
                    first_copy(i - 1, other).wait()

            @pl.when(i >= 2)
            def _():
                o_copy(i - 2, slot).wait()

            def part(n, _):
                pieces, finish = matmul(slot, n)
                units = []
                for c in range(2):
                    units += activate(i + 1, other, 2 * n + c)
                interleave(pieces, units)
                finish()
                return 0

            lax.fori_loop(0, channels // 256, part, 0)
            o_copy(i, slot).start()

            @pl.when(i + 1 < tiles)
            def _():
                for which in range(2):
                    s_copy(i + 1, other, which).start()

                @pl.when((i + 1) % walk.per == 0)
                def _():
                    first_copy(i + 1, other).start()

        return 0

    lax.fori_loop(0, tiles // 2, pair, 0)
    for which in range(2):
        s_copy(tiles - 1, 1, which).wait()
    if walk.per == 1:
        first_copy(tiles - 1, 1).wait()
    o_copy(tiles - 2, 0).wait()
    o_copy(tiles - 1, 1).wait()
    talk2.start_edges((pooled,))
    talk2.start_sums(stats)
    talk2.finish_edges((pooled,))
    p_left[...] = talk2.lands[0][...]
    p_right[...] = talk2.lands[1][...]
    talk2.finish_sums(sums2)


def conv_one_forward(x, cotangent, gain, shift, weight, entries, number):
    windows, length, channels = x.shape
    half = length // 2
    tile = min(512, half)
    slabs = channels // LANES
    pooled = jax.ShapeDtypeStruct((windows, half, channels), f32)
    edges = Exchange.edges([cotangent, pooled])
    got = pl.pallas_call(
        functools.partial(conv_one_kernel, tile, entries),
        out_shape=[
            pooled,
            jax.ShapeDtypeStruct((2, windows, half, channels), bf16),
            jax.ShapeDtypeStruct((windows, 16, channels), bf16),
            jax.ShapeDtypeStruct((8, channels), f32),
            jax.ShapeDtypeStruct((8, channels), f32),
        ]
        + edges,
        in_specs=[ANY, ANY, VM, VM, ANY],
        out_specs=[ANY] * 3 + [VM] * 6,
        scratch_shapes=[
            pltpu.VMEM((2, 2 * tile + 2 * EDGE, channels), f32),
            pltpu.VMEM((slabs, 2 * tile + 2 * EDGE, LANES), f32),
            pltpu.VMEM((tile, 5 * channels), bf16),
            pltpu.VMEM((tile, 5 * channels), bf16),
            pltpu.VMEM((2, tile, channels), f32),
            pltpu.VMEM((slabs, 8, LANES), f32),
            pltpu.VMEM((5 * channels, channels), bf16),
            pltpu.VMEM((2, 8, channels), f32),
            DMA((2,)),
            DMA((2, 2)),
            DMA,
            DMA((2,)),
            DMA,
        ]
        + Exchange.scratch(channels) * 2
        + Exchange.edge_scratch([x, cotangent])
        + Exchange.edge_scratch([pooled]),
        name="conv_one_forward",
        **joining(params(10 * windows * half * channels * channels, 12 * x.size, x.size), number),
    )(x, cotangent, gain, shift, weight.reshape(5 * channels, channels))
    return got[:5], got[5:7], got[7:9]


def conv_two_kernel(
    tile, entries, v, left, right, sums, gain, shift, w_hbm, narrow, h_out, sums3, n_left, n_right,
    vs, h_buf, lhs_a, lhs_b, outs, w_ref, stats, v_sem, h_sem, o_sem, w_sem, *talks,
):
    windows, length, channels = v.shape
    slabs = channels // LANES
    walk = Walk(windows, length, tile)
    tiles = walk.count
    lhs = (lhs_a, lhs_b)
    center, inverse = center_inverse(sums[...], entries)
    scale = inverse * flat_row(gain)
    offset = flat_row(shift) - center * scale
    scale, offset = ROOT * scale, ROOT * offset
    stats[...] = jnp.zeros_like(stats)

    def load(i, slot):
        walk.fetch(i, v, left, right, vs.at[slot], v_sem.at[slot])

    def h_copy(i, slot):
        w, _ = walk.where(i)
        return pltpu.make_async_copy(
            lhs[slot].at[:, pl.ds(channels, channels)], h_out.at[w, walk.rows(i)], h_sem.at[slot]
        )

    def o_copy(i, slot):
        w, _ = walk.where(i)
        return pltpu.make_async_copy(outs.at[slot], narrow.at[w, walk.rows(i)], o_sem.at[slot])

    def activate(i, slot, c):
        a, b = scale[:, lanes_of(c)], offset[:, lanes_of(c)]
        src, dst, cols = vs.at[slot], lhs[slot], lanes(c)

        def ends():
            head = gelu_scaled(src[0:EDGE, cols] * a + b)
            h_buf[c, 0:EDGE] = jnp.where(walk.hide_left(i), 0.0, head)
            tail = gelu_scaled(src[EDGE + tile : 2 * EDGE + tile, cols] * a + b)
            h_buf[c, EDGE + tile : 2 * EDGE + tile] = jnp.where(walk.hide_right(i), 0.0, tail)

        def rows(r):
            def run():
                q = EDGE + r
                h_buf[c, q : q + UNIT] = gelu_scaled(src[q : q + UNIT, cols] * a + b)

            return run

        def taps(r):
            def run():
                for tap in range(3):
                    at = EDGE + r + 5 * (tap - 1)
                    dst[r : r + UNIT, lanes(tap * slabs + c)] = h_buf[c, at : at + UNIT].astype(bf16)

            return run

        units = [ends, rows(0)]
        for r in range(UNIT, tile, UNIT):
            units += [rows(r), taps(r - UNIT)]
        return units + [taps(tile - UNIT)]

    load(0, 0)
    talk = Exchange(talks[: Exchange.SUMS], talks[Exchange.SUMS :])
    greet(talk.seqs, talk.dps)
    wait_for(vs.at[0], v_sem.at[0])
    w_copy = pltpu.make_async_copy(w_hbm, w_ref, w_sem)
    w_copy.start()
    load(1, 1)
    for c in range(slabs):
        for unit in activate(0, 0, c):
            unit()
    h_copy(0, 0).start()
    w_copy.wait()

    def pair(j, _):
        for slot in range(2):
            i = 2 * j + slot
            other = 1 - slot

            @pl.when(i + 1 < tiles)
            def _():
                wait_for(vs.at[other], v_sem.at[other])

            @pl.when(i + 2 < tiles)
            def _():
                load(i + 2, slot)

            @pl.when(i >= 1)
            def _():
                h_copy(i - 1, other).wait()

            @pl.when(i >= 2)
            def _():
                o_copy(i - 2, slot).wait()

            held = []

            def piece(k):
                def run():
                    at = slice(k * channels, (k + 1) * channels)
                    part = dot(lhs[slot][:, at], w_ref[at])
                    held[:] = [held[0] + part] if held else [part]

                return run

            units = []
            for c in range(slabs):
                units += activate(i + 1, other, c)
            interleave([piece(k) for k in range(3)], units)
            total = (0.5 / ROOT) * held[0]
            outs[slot] = total
            stats[0] += folded(total)
            stats[1] += folded(total * total)
            o_copy(i, slot).start()

            @pl.when(i + 1 < tiles)
            def _():
                h_copy(i + 1, other).start()

        return 0

    lax.fori_loop(0, tiles // 2, pair, 0)
    h_copy(tiles - 1, 1).wait()
    o_copy(tiles - 2, 0).wait()
    o_copy(tiles - 1, 1).wait()
    talk.start_edges((narrow,))
    talk.start_sums(stats)
    talk.finish_edges((narrow,))
    n_left[...] = talk.lands[0][...]
    n_right[...] = talk.lands[1][...]
    talk.finish_sums(sums3)


def conv_two_forward(v, left, right, sums, gain, shift, weight, entries, number):
    windows, length, channels = v.shape
    tile = min(512, length)
    slabs = channels // LANES
    width = weight.shape[2]
    narrow = jax.ShapeDtypeStruct((windows, length, width), f32)
    got = pl.pallas_call(
        functools.partial(conv_two_kernel, tile, entries),
        out_shape=[
            narrow,
            jax.ShapeDtypeStruct((windows, length, channels), bf16),
            jax.ShapeDtypeStruct((8, width), f32),
        ]
        + Exchange.edges([narrow]),
        in_specs=[ANY, ANY, ANY, VM, VM, VM, ANY],
        out_specs=[ANY, ANY, VM, VM, VM],
        scratch_shapes=[
            pltpu.VMEM((2, tile + 2 * EDGE, channels), f32),
            pltpu.VMEM((slabs, tile + 2 * EDGE, LANES), f32),
            pltpu.VMEM((tile, 3 * channels), bf16),
            pltpu.VMEM((tile, 3 * channels), bf16),
            pltpu.VMEM((2, tile, width), f32),
            pltpu.VMEM((3 * channels, width), bf16),
            pltpu.VMEM((2, 8, width), f32),
            DMA((2,)),
            DMA((2,)),
            DMA((2,)),
            DMA,
        ]
        + Exchange.scratch(width)
        + Exchange.edge_scratch([narrow]),
        name="conv_two_forward",
        **joining(params(6 * v.size * width, 8 * v.size, v.size), number),
    )(v, left, right, sums, gain, shift, weight.reshape(3 * channels, width))
    return got[:3], got[3:]


def conv_three_kernel(
    entries, narrow, cotangent, pooled, sums, gain, shift, w_ref, outputs, da, stats, w_grad,
    branch, grad, hidden, total,
):
    tile = narrow.shape[1]
    step = pl.program_id(0)
    center, inverse = center_inverse(sums[...], entries)

    @pl.when(step == 0)
    def _():
        stats[...] = jnp.zeros_like(stats)
        total[...] = jnp.zeros_like(total)

    branch[...] = cotangent[0].astype(bf16)
    grad[...] = dot(branch[...], w_ref[...], NT)
    for c in range(narrow.shape[2] // LANES):
        cols = lanes(c)
        at = lanes_of(c)
        m, inv, g, s = center[:, at], inverse[:, at], gain[at][None], shift[at][None]
        gains = jnp.zeros((8, LANES), f32)
        shifts = jnp.zeros((8, LANES), f32)
        for r in range(0, tile, UNIT):
            normed = (narrow[0, r : r + UNIT, cols] - m) * inv
            value, slope = gelu_both(normed * g + s)
            hidden[r : r + UNIT, cols] = value.astype(bf16)
            back = slope * grad[r : r + UNIT, cols]
            da[0, r : r + UNIT, cols] = back
            gains += folded(back * normed)
            shifts += folded(back)
        stats[0, :, cols] += gains
        stats[1, :, cols] += shifts
    outputs[0] = pooled[0] + dot(hidden[...], w_ref[...])
    total[...] += dot(hidden[...], branch[...], TN)

    @pl.when(step == pl.num_programs(0) - 1)
    def _():
        for c in range(total.shape[1] // LANES):
            w_grad[c] = total[:, lanes_of(c)].astype(bf16)


def conv_three_both(narrow, cotangent, pooled, sums, gain, shift, weight, entries):
    windows, length, width = narrow.shape
    channels = weight.shape[1]
    tile = min(512, length)
    per = length // tile
    rows = lambda i: (i // per, i % per, 0)
    whole = lambda i: (0, 0)
    return pl.pallas_call(
        functools.partial(conv_three_kernel, entries),
        grid=(windows * per,),
        out_shape=(
            jax.ShapeDtypeStruct((windows, length, channels), f32),
            jax.ShapeDtypeStruct((windows, length, width), f32),
            jax.ShapeDtypeStruct((2, 8, width), f32),
            jax.ShapeDtypeStruct((channels // LANES, width, LANES), bf16),
        ),
        in_specs=[
            pl.BlockSpec((1, tile, width), rows),
            pl.BlockSpec((1, tile, channels), rows),
            pl.BlockSpec((1, tile, channels), rows),
            pl.BlockSpec((8, width), whole),
            pl.BlockSpec((width,), lambda i: (0,)),
            pl.BlockSpec((width,), lambda i: (0,)),
            pl.BlockSpec((width, channels), whole),
        ],
        out_specs=(
            pl.BlockSpec((1, tile, channels), rows),
            pl.BlockSpec((1, tile, width), rows),
            pl.BlockSpec((2, 8, width), lambda i: (0, 0, 0)),
            pl.BlockSpec((channels // LANES, width, LANES), lambda i: (0, 0, 0)),
        ),
        scratch_shapes=[
            pltpu.VMEM((tile, channels), bf16),
            pltpu.VMEM((tile, width), f32),
            pltpu.VMEM((tile, width), bf16),
            pltpu.VMEM((width, channels), f32),
        ],
        name="conv_three_both",
        **params(6 * narrow.size * channels, 12 * cotangent.size, narrow.size),
    )(narrow, cotangent, pooled, sums, gain, shift, weight)


def conv_two_back_kernel(
    tile, entries, da, da_left, da_right, v, v_left, v_right, sums3, grads3, gain3, pooled, sums2, gain2, shift2,
    h, w_hbm, da_out, w_grad, grads2, b_left, b_right,
    das, vs, ps, hs, low_buf, low_a, low_b, g_buf, outs, total, w_ref, w_flip, stats,
    a_sem, v_sem, p_sem, h_sem, o_sem, w_sem, *talks,
):
    windows, length, width = da.shape
    channels = pooled.shape[2]
    thin, slabs = width // LANES, channels // LANES
    walk = Walk(windows, length, tile)
    tiles = walk.count
    low = (low_a, low_b)
    center3, inverse3 = center_inverse(sums3[...], entries)
    grads = grads3[...]
    scale3 = inverse3 * flat_row(gain3)
    lean = scale3 * inverse3 * (grads[0:1] / entries)
    flat = scale3 * (grads[1:2] / entries)
    center, inverse = center_inverse(sums2[...], entries)
    scale = inverse * flat_row(gain2)
    offset = ROOT * (flat_row(shift2) - center * scale)
    scale = ROOT * scale
    stats[...] = jnp.zeros_like(stats)
    total[...] = jnp.zeros_like(total)

    def load(i, slot):
        walk.fetch(i, da, da_left, da_right, das.at[slot], a_sem.at[slot])
        walk.fetch(i, v, v_left, v_right, vs.at[slot], v_sem.at[slot])

    def wait_load(slot):
        wait_for(das.at[slot], a_sem.at[slot])
        wait_for(vs.at[slot], v_sem.at[slot])

    def late_copies(i, slot):
        w, _ = walk.where(i)
        return (
            pltpu.make_async_copy(pooled.at[w, walk.rows(i)], ps.at[slot], p_sem.at[slot]),
            pltpu.make_async_copy(h.at[w, walk.rows(i)], hs.at[slot], h_sem.at[slot]),
        )

    def o_copy(i, slot):
        w, _ = walk.where(i)
        return pltpu.make_async_copy(outs.at[slot], da_out.at[w, walk.rows(i)], o_sem.at[slot])

    def lower(i, slot, c):
        at, cols = lanes_of(c), lanes(c)
        m, s, l, f = center3[:, at], scale3[:, at], lean[:, at], flat[:, at]
        dst = low[slot]

        def value(q, size):
            return das[slot, q : q + size, cols] * s - (vs[slot, q : q + size, cols] - m) * l - f

        def ends():
            low_buf[c, 0:EDGE] = jnp.where(walk.hide_left(i), 0.0, value(0, EDGE))
            low_buf[c, EDGE + tile : 2 * EDGE + tile] = jnp.where(walk.hide_right(i), 0.0, value(EDGE + tile, EDGE))

        def rows(r):
            def run():
                low_buf[c, EDGE + r : EDGE + r + UNIT] = value(EDGE + r, UNIT)

            return run

        def taps(r):
            def run():
                for tap in range(3):
                    q = EDGE + r - 5 * (tap - 1)
                    dst[r : r + UNIT, lanes(tap * thin + c)] = low_buf[c, q : q + UNIT].astype(bf16)

            return run

        units = [ends, rows(0)]
        for r in range(UNIT, tile, UNIT):
            units += [rows(r), taps(r - UNIT)]
        return units + [taps(tile - UNIT)]

    def finish(slot, c):
        at, cols = lanes_of(c), lanes(c)
        a, b = scale[:, at], offset[:, at]
        sums = [jnp.zeros((8, LANES), f32), jnp.zeros((8, LANES), f32)]

        def rows(r):
            def run():
                q = ps[slot, r : r + UNIT, cols] * a + b
                back = slope_scaled(q) * g_buf[r : r + UNIT, cols]
                outs[slot, r : r + UNIT, cols] = back
                sums[0] = sums[0] + folded(back * q)
                sums[1] = sums[1] + folded(back)

            return run

        def close():
            stats[0, :, cols] += sums[0]
            stats[1, :, cols] += sums[1]

        return [rows(r) for r in range(0, tile, UNIT)] + [close]

    load(0, 0)
    w_copy = pltpu.make_async_copy(w_hbm, w_ref, w_sem)
    w_copy.start()
    for copy in late_copies(0, 0):
        copy.start()
    talk = Exchange(talks[: Exchange.SUMS], talks[Exchange.SUMS :])
    greet(talk.seqs, talk.dps)
    wait_load(0)
    load(1, 1)
    for c in range(thin):
        for unit in lower(0, 0, c):
            unit()
    w_copy.wait()
    for k in range(3):
        w_flip[k * width : (k + 1) * width] = w_ref[k].T

    def pair(j, _):
        for slot in range(2):
            i = 2 * j + slot
            other = 1 - slot

            @pl.when(i + 1 < tiles)
            def _():
                wait_load(other)
                for copy in late_copies(i + 1, other):
                    copy.start()

            @pl.when(i + 2 < tiles)
            def _():
                load(i + 2, slot)

            for copy in late_copies(i, slot):
                copy.wait()

            @pl.when(i >= 2)
            def _():
                o_copy(i - 2, slot).wait()

            def back(n):
                def run():
                    cols = lanes(n, 256)
                    g_buf[:, cols] = dot(low[slot][...], w_flip[:, cols])

                return run

            def weigh(n):
                def run():
                    at = slice(n * 256, (n + 1) * 256)
                    total[at] += dot(hs[slot, :, at], low[slot][...], TN)

                return run

            units = []
            for c in range(thin):
                units += lower(i + 1, other, c)
            interleave([back(n) for n in range(channels // 256)], units)
            units = []
            for c in range(slabs):
                units += finish(slot, c)
            interleave([weigh(n) for n in range(channels // 256)], units)
            o_copy(i, slot).start()

        return 0

    lax.fori_loop(0, tiles // 2, pair, 0)
    shifts = 0.5 * stats[1]
    stats[0] = (0.5 / ROOT * stats[0] - shifts * flat_row(shift2)) / flat_row(gain2)
    stats[1] = shifts
    o_copy(tiles - 2, 0).wait()
    o_copy(tiles - 1, 1).wait()
    talk.start_edges((da_out,))
    talk.start_sums(stats)
    for c in range(3 * thin):
        w_grad[c] = ((0.5 / ROOT) * total[:, lanes_of(c)]).astype(bf16)
    talk.finish_edges((da_out,))
    b_left[...] = talk.lands[0][...]
    b_right[...] = talk.lands[1][...]
    talk.finish_sums(grads2)


def conv_two_back(da, da_sides, v, v_sides, sums3, grads3, gain3, pooled, sums2, gain2, shift2, h, weight, entries, number):
    windows, length, width = da.shape
    channels = pooled.shape[2]
    tile = min(512, length)
    thin, slabs = width // LANES, channels // LANES
    back = jax.ShapeDtypeStruct((windows, length, channels), f32)
    got = pl.pallas_call(
        functools.partial(conv_two_back_kernel, tile, entries),
        out_shape=[
            back,
            jax.ShapeDtypeStruct((3 * thin, channels, LANES), bf16),
            jax.ShapeDtypeStruct((8, channels), f32),
        ]
        + Exchange.edges([back]),
        in_specs=[ANY] * 6 + [VM] * 3 + [ANY] + [VM] * 3 + [ANY] * 2,
        out_specs=[ANY] + [VM] * 4,
        scratch_shapes=[
            pltpu.VMEM((2, tile + 2 * EDGE, width), f32),
            pltpu.VMEM((2, tile + 2 * EDGE, width), f32),
            pltpu.VMEM((2, tile, channels), f32),
            pltpu.VMEM((2, tile, channels), bf16),
            pltpu.VMEM((thin, tile + 2 * EDGE, LANES), f32),
            pltpu.VMEM((tile, 3 * width), bf16),
            pltpu.VMEM((tile, 3 * width), bf16),
            pltpu.VMEM((tile, channels), f32),
            pltpu.VMEM((2, tile, channels), f32),
            pltpu.VMEM((channels, 3 * width), f32),
            pltpu.VMEM(weight.shape, bf16),
            pltpu.VMEM((3 * width, channels), bf16),
            pltpu.VMEM((2, 8, channels), f32),
            DMA((2,)),
            DMA((2,)),
            DMA((2,)),
            DMA((2,)),
            DMA((2,)),
            DMA,
        ]
        + Exchange.scratch(channels)
        + Exchange.edge_scratch([back]),
        name="conv_two_back",
        **joining(params(12 * pooled.size * width, 16 * pooled.size, pooled.size), number),
    )(da, *da_sides, v, *v_sides, sums3, grads3, gain3, pooled, sums2, gain2, shift2, h, weight)
    return got[:3], got[3:]


class Reduction:
    STAGES = 8
    LAG = 3

    def __init__(self, data, done, lands, send, recv):
        self.data, self.done, self.lands, self.send, self.recv = data, done, lands, send, recv
        self.chunks, self.rows = data.shape[0], data.shape[1]
        self.steps = self.chunks + self.LAG * self.STAGES
        self.planes = lax.axis_size("dp") // 4
        seq, dp = lax.axis_index("seq"), lax.axis_index("dp")
        self.seq, self.dp = seq, dp
        one, two = dp % 2, (dp // 2) % 2
        swap = seq == 1
        first_bit, second_bit = jnp.where(swap, two, one), jnp.where(swap, one, two)
        to_one, to_two = dp + 1 - 2 * one, dp + 2 - 4 * two
        first_peer, second_peer = jnp.where(swap, to_two, to_one), jnp.where(swap, to_one, to_two)
        self.peers = ({"seq": 1 - seq}, {"dp": first_peer}, {"dp": second_peer})
        self.plane = dp // 4
        rows = self.rows
        self.size = [rows // 2, rows // 4, rows // 8, rows // 8 // self.planes]
        self.base = [seq * self.size[0]]
        self.away = [(1 - seq) * self.size[0]]
        for bit, size in ((first_bit, self.size[1]), (second_bit, self.size[2])):
            self.away.append(self.base[-1] + (1 - bit) * size)
            self.base.append(self.base[-1] + bit * size)

    def part(self, ref, c, start, size):
        return ref.at[c, pl.ds(pl.multiple_of(start, 16), size)]

    def copy(self, c, number, src, dst, peer):
        return pltpu.make_async_remote_copy(
            src_ref=src, dst_ref=dst, send_sem=self.send.at[c, number], recv_sem=self.recv.at[c, number],
            device_id=peer, device_id_type=MESH,
        )

    def copies(self, c, stage):
        size, base = self.size, self.base
        if stage < 3:
            src = self.part(self.data, c, self.away[stage], size[stage])
            return [self.copy(c, stage, src, self.lands[stage].at[c], self.peers[stage])]
        if stage == 3 or stage == 4:
            out = []
            for d in range(1, self.planes):
                there = (self.plane + d) % self.planes
                peer = {"dp": self.dp + (there - self.plane) * 4}
                if stage == 3:
                    src = self.part(self.data, c, base[2] + there * size[3], size[3])
                    dst = self.lands[3].at[c, d - 1]
                else:
                    src = dst = self.part(self.done, c, base[2] + self.plane * size[3], size[3])
                out.append(self.copy(c, 3 + (stage - 3) * (self.planes - 1) + d - 1, src, dst, peer))
            return out
        level = 7 - stage
        mine = self.part(self.done, c, base[level], size[level])
        return [self.copy(c, 2 * (self.planes - 1) + stage - 2, mine, mine, self.peers[level])]

    def launch(self, c, stage):
        for copy in self.copies(c, stage):
            copy.start()

    def arrive(self, c, stage):
        for copy in self.copies(c, stage):
            copy.wait()
        size, base = self.size, self.base
        if stage < 3:
            unit = self.rows // 8

            def add(r, _):
                at = pl.ds(pl.multiple_of(base[stage] + r * unit, 16), unit)
                got = self.lands[stage][c, pl.ds(pl.multiple_of(r * unit, 16), unit)].astype(f32)
                self.data[c, at] = (self.data[c, at].astype(f32) + got).astype(bf16)
                return 0

            lax.fori_loop(0, size[stage] // unit, add, 0)
        elif stage == 3:
            at = pl.ds(pl.multiple_of(base[2] + self.plane * size[3], 16), size[3])
            total = self.data[c, at].astype(f32)
            for d in range(1, self.planes):
                total += self.lands[3][c, d - 1].astype(f32)
            self.done[c, at] = total.astype(bf16)

    def step(self, t):
        for stage in range(self.STAGES, -1, -1):
            c = t - self.LAG * stage

            @pl.when(jnp.logical_and(c >= 0, c < self.chunks))
            def _():
                if stage > 0:
                    self.arrive(c, stage - 1)
                if stage < self.STAGES:
                    self.launch(c, stage)

    @staticmethod
    def fits(rows):
        dps = lax.axis_size("dp")
        return lax.axis_size("seq") == 2 and dps % 4 == 0 and dps > 4 and rows % (128 * (dps // 4)) == 0

    @staticmethod
    def scratch(chunks, rows):
        planes = lax.axis_size("dp") // 4
        copies = 2 * (planes - 1) + 6
        shapes = [(chunks, rows, LANES)] + [(chunks, rows >> (n + 1), LANES) for n in range(3)]
        shapes += [(chunks, planes - 1, rows // 8 // planes, LANES)]
        return [pltpu.VMEM(shape, bf16) for shape in shapes] + [DMA((chunks, copies)), DMA((chunks, copies))]

    @staticmethod
    def of(data, refs):
        return Reduction(data, refs[0], refs[1:5], refs[5], refs[6])


def conv_one_weigh_kernel(
    tile, entries, joined, seqs, dps, da, da_left, da_right, v, v_left, v_right, ct, ct_left, ct_right, sums2, grads2,
    gain2, s, first, two, three, low_out, w_grad, small, das, vs, cts, ss, firsts, low_buf, low_a, low_b, coef, total,
    packed, data, a_sem, v_sem, c_sem, s_sem, f_sem, l_sem, g_sem, d_sem, *reduction,
):
    windows, length, channels = da.shape
    slabs = channels // LANES
    walk = Walk(windows, length, tile)
    tiles = walk.count
    low = (low_a, low_b)
    half_entries = entries / 2
    center2, inverse2 = center_inverse(sums2[...], half_entries)
    grads = grads2[...]
    scale2 = 0.5 * inverse2 * flat_row(gain2)
    lean = scale2 * inverse2 * (grads[0:1] / half_entries)
    flat = scale2 * (grads[1:2] / half_entries)
    for c in range(slabs):
        for row, values in enumerate((0.5 * scale2, lean, center2 * lean - flat)):
            coef[c, row : row + 1] = values[:, lanes_of(c)]

    def load(i, slot):
        walk.fetch(i, da, da_left, da_right, das.at[slot], a_sem.at[slot])
        walk.fetch(i, v, v_left, v_right, vs.at[slot], v_sem.at[slot])
        walk.fetch(i, ct, ct_left, ct_right, cts.at[slot], c_sem.at[slot])

    def wait_load(slot):
        wait_for(das.at[slot], a_sem.at[slot])
        wait_for(vs.at[slot], v_sem.at[slot])
        wait_for(cts.at[slot], c_sem.at[slot])

    def s_copy(i, slot):
        w, _ = walk.where(i)
        return pltpu.make_async_copy(s.at[:, w, walk.rows(i)], ss.at[slot], s_sem.at[slot])

    def l_copy(i, slot):
        w, _ = walk.where(i)
        return pltpu.make_async_copy(low[slot], low_out.at[w, walk.rows(i)], l_sem.at[slot])

    def lower(i, slot, c):
        cols = lanes(c)
        sc, l, f = coef[c, 0:1], coef[c, 1:2], coef[c, 2:3]
        dst = low[slot]

        def value(q, size):
            rows = slice(q, q + size)
            return 0.5 * cts[slot, rows, cols] + das[slot, rows, cols] * sc - vs[slot, rows, cols] * l + f

        def ends():
            low_buf[c, 0:EDGE] = jnp.where(walk.hide_left(i), 0.0, value(0, EDGE))
            low_buf[c, EDGE + tile : 2 * EDGE + tile] = jnp.where(walk.hide_right(i), 0.0, value(EDGE + tile, EDGE))

        def rows(r):
            def run():
                low_buf[c, EDGE + r : EDGE + r + UNIT] = value(EDGE + r, UNIT)

            return run

        def taps(r):
            def run():
                for tap in range(3):
                    q = EDGE + r + 1 - tap
                    at = pl.ds(pl.multiple_of(tap * channels + c * LANES, LANES), LANES)
                    dst[r : r + UNIT, at] = low_buf[c, q : q + UNIT].astype(bf16)

            return run

        units = [ends, rows(0)]
        for r in range(UNIT, tile, UNIT):
            units += [rows(r), taps(r - UNIT)]
        return units + [taps(tile - UNIT)]

    load(0, 0)
    wait_load(0)
    s_copy(0, 0).start()
    f_copy = pltpu.make_async_copy(first, firsts, f_sem)
    f_copy.start()
    load(1, 1)
    at = 0
    for src in (two, three):
        size = src.shape[1]
        for c in range(src.shape[0]):
            chunk, start = divmod(at, data.shape[1])
            pltpu.make_async_copy(src.at[c], data.at[chunk, pl.ds(start, size)], d_sem).start()
            at += size
    if joined:
        greet(seqs, dps)
        sharing = Reduction.of(data, reduction)
    total[...] = jnp.zeros_like(total)

    def first_slab(c, _):
        for unit in lower(0, 0, c):
            unit()
        return 0

    lax.fori_loop(0, slabs, first_slab, 0)
    l_copy(0, 0).start()
    f_copy.wait()
    wait_for(data, d_sem)

    def pair(j, _):
        for slot in range(2):
            i = 2 * j + slot
            other = 1 - slot
            w, p = walk.where(i)

            @pl.when(jnp.logical_and(p == 0, walk.at_start))
            def _():
                row = lax.broadcasted_iota(jnp.int32, (16, channels), 0)
                here = jnp.where(row == 0, firsts[w].astype(f32), 0.0).astype(bf16)
                total[1] += dot(here, low[slot][0:16, channels : 2 * channels], TN)

            @pl.when(i + 1 < tiles)
            def _():
                wait_load(other)
                s_copy(i + 1, other).start()

            @pl.when(i + 2 < tiles)
            def _():
                load(i + 2, slot)

            @pl.when(i >= 1)
            def _():
                l_copy(i - 1, other).wait()

            s_copy(i, slot).wait()

            def part(n, _):
                cols = lanes(n, 256)

                def weigh(k):
                    def run():
                        at = pl.ds(pl.multiple_of((k // 2) * channels + n * 256, 256), 256)
                        total[k, :, cols] += dot(ss[slot, k % 2], low[slot][:, at], TN)

                    return run

                units = lower(i + 1, other, 2 * n) + lower(i + 1, other, 2 * n + 1)
                interleave([weigh(k) for k in range(EARLY)], units)
                if joined:
                    sharing.step(i * (channels // 256) + n)
                return 0

            lax.fori_loop(0, channels // 256, part, 0)

            @pl.when(i + 1 < tiles)
            def _():
                l_copy(i + 1, other).start()

        return 0

    lax.fori_loop(0, tiles // 2, pair, 0)
    l_copy(tiles - 1, 1).wait()
    for k in range(EARLY):
        for c in range(slabs):
            packed[k, c] = ((0.5 / ROOT) * total[k, :, lanes_of(c)]).astype(bf16)
    g_copy = pltpu.make_async_copy(packed, w_grad, g_sem)
    g_copy.start()
    if joined:
        def more(t, _):
            sharing.step(t)
            return 0

        lax.fori_loop(tiles * (channels // 256), sharing.steps, more, 0)
        d_copy = pltpu.make_async_copy(sharing.done, small, d_sem)
    else:
        d_copy = pltpu.make_async_copy(data, small, d_sem)
    d_copy.start()
    d_copy.wait()
    g_copy.wait()


def conv_one_weigh(da, da_sides, v, v_sides, ct, ct_sides, sums2, grads2, gain2, s, first, two, three, entries, number):
    windows, length, channels = da.shape
    tile = min(512, length)
    slabs = channels // LANES
    packed = (EARLY, slabs, channels, LANES)
    rows = 2 * channels
    chunks = (two.shape[0] * two.shape[1] + three.shape[0] * three.shape[1]) // rows
    joined = Reduction.fits(rows)
    estimate = params(4 * EARLY * da.size * channels, 24 * da.size, 0)
    if joined:
        estimate = joining(estimate, number)
    low, parts, small = pl.pallas_call(
        functools.partial(conv_one_weigh_kernel, tile, entries, joined, lax.axis_size("seq"), lax.axis_size("dp")),
        out_shape=(
            jax.ShapeDtypeStruct((windows, length, 3 * channels), bf16),
            jax.ShapeDtypeStruct(packed, bf16),
            jax.ShapeDtypeStruct((chunks, rows, LANES), bf16),
        ),
        in_specs=[ANY] * 9 + [VM] * 3 + [ANY] * 4,
        out_specs=(ANY, ANY, ANY),
        scratch_shapes=[
            pltpu.VMEM((2, tile + 2 * EDGE, channels), f32),
            pltpu.VMEM((2, tile + 2 * EDGE, channels), f32),
            pltpu.VMEM((2, tile + 2 * EDGE, channels), f32),
            pltpu.VMEM((2, 2, tile, channels), bf16),
            pltpu.VMEM(first.shape, bf16),
            pltpu.VMEM((slabs, tile + 2 * EDGE, LANES), f32),
            pltpu.VMEM((tile, 3 * channels), bf16),
            pltpu.VMEM((tile, 3 * channels), bf16),
            pltpu.VMEM((slabs, 8, LANES), f32),
            pltpu.VMEM((EARLY, channels, channels), f32),
            pltpu.VMEM(packed, bf16),
            pltpu.VMEM((chunks, rows, LANES), bf16),
        ]
        + [DMA((2,))] * 4
        + [DMA, DMA((2,)), DMA, DMA]
        + (Reduction.scratch(chunks, rows) if joined else []),
        name="conv_one_weigh",
        **estimate,
    )(da, *da_sides, v, *v_sides, ct, *ct_sides, sums2, grads2, gain2, s, first, two, three)
    if not joined:
        small = lax.psum(small, ("dp", "seq"))
    return low, parts, small


def conv_one_spread_kernel(
    tile, entries, joined, low, x, sums1, gain1, shift1, w_hbm, s, parts, da_out, w_grad, grads1,
    lows, xs, g_buf, outs, coef, w_ref, total, ss, ls, data, stats, l_sem, x_sem, o_sem, w_sem, d_sem, t_sem, *refs,
):
    windows, length, _ = low.shape
    channels = x.shape[2]
    slabs = channels // LANES
    span = 2 * tile
    walk = Walk(windows, length, tile)
    tiles = walk.count
    center, inverse = center_inverse(sums1[...], entries)
    scale = inverse * flat_row(gain1)
    offset = flat_row(shift1) - center * scale
    for c in range(slabs):
        for row, values in enumerate((ROOT * scale, ROOT * offset)):
            coef[c, row : row + 1] = values[:, lanes_of(c)]
    stats[...] = jnp.zeros_like(stats)

    def l_copy(i, slot):
        w, _ = walk.where(i)
        return pltpu.make_async_copy(low.at[w, walk.rows(i)], lows.at[slot], l_sem.at[slot])

    def x_copy(i, slot):
        w, _ = walk.where(i)
        return pltpu.make_async_copy(x.at[w, walk.rows(i, 2)], xs.at[slot], x_sem.at[slot])

    def o_copy(i, slot):
        w, _ = walk.where(i)
        return pltpu.make_async_copy(outs.at[slot], da_out.at[w, walk.rows(i, 2)], o_sem.at[slot])

    def t_copies(g, slot):
        k = EARLY + g // tiles
        w, _ = walk.where(g % tiles)
        rows = walk.rows(g % tiles)
        at = pl.ds(pl.multiple_of((k // 2) * channels, channels), channels)
        return (
            pltpu.make_async_copy(s.at[k % 2, w, rows], ss.at[slot], t_sem.at[slot, 0]),
            pltpu.make_async_copy(low.at[w, rows, at], ls.at[slot], t_sem.at[slot, 1]),
        )

    d_copy = pltpu.make_async_copy(parts, data.at[pl.ds(0, EARLY * slabs // 2)], d_sem)
    d_copy.start()
    for g in range(AHEAD):
        for copy in t_copies(g, g):
            copy.start()
    talk, reduction = Exchange(refs[: Exchange.SUMS]), refs[Exchange.SUMS :]
    greet(talk.seqs, talk.dps)
    d_copy.wait()
    l_copy(0, 0).start()
    w_copy = pltpu.make_async_copy(w_hbm, w_ref, w_sem)
    w_copy.start()
    if joined:
        sharing = Reduction.of(data, reduction)
        sharing.step(0)

    late = (5 - EARLY) * tiles
    triple = slabs // 2

    def due(g):
        whole, part = g // tiles, g % tiles
        first = jnp.where(whole == 0, 1, (EARLY + whole - 1) * triple)
        count = jnp.where(whole == 0, EARLY * triple - 1, triple)
        return first + count * part // tiles, first + count * (part + 1) // tiles

    def weigh(g, _):
        slot = g % (AHEAD + 1)
        for copy in t_copies(g, slot):
            copy.wait()

        @pl.when(g + AHEAD < late)
        def _():
            for copy in t_copies(g + AHEAD, (g + AHEAD) % (AHEAD + 1)):
                copy.start()

        @pl.when(g % tiles == 0)
        def _():
            total[...] = dot(ss[slot], ls[slot], TN)

        @pl.when(g % tiles > 0)
        def _():
            total[...] += dot(ss[slot], ls[slot], TN)

        @pl.when(g % tiles == tiles - 1)
        def _():
            for c in range(slabs):
                at = slice((c % 2) * channels, (c % 2 + 1) * channels)
                data[(EARLY + g // tiles) * triple + c // 2, at] = ((0.5 / ROOT) * total[:, lanes_of(c)]).astype(bf16)

        if joined:
            def take(t, _):
                sharing.step(t)
                return 0

            lax.fori_loop(*due(g), take, 0)

        return 0

    lax.fori_loop(0, late, weigh, 0)
    w_copy.wait()

    def finish(slot, c):
        cols = lanes(c)
        a, b = coef[c, 0:1], coef[c, 1:2]
        held = [jnp.zeros((8, LANES), f32), jnp.zeros((8, LANES), f32)]

        def rows(r):
            def run():
                q = xs[slot, r : r + UNIT, cols] * a + b
                incoming = g_buf[slot, c, EDGE + r : EDGE + r + UNIT] + g_buf[slot, c, EDGE + r - 1 : EDGE + r - 1 + UNIT]
                back = slope_scaled(q) * incoming
                outs[slot, r : r + UNIT, cols] = back.astype(bf16)
                held[0] = held[0] + folded(back * q)
                held[1] = held[1] + folded(back)

            return run

        def close():
            stats[0, :, cols] += held[0]
            stats[1, :, cols] += held[1]

        return [rows(r) for r in range(0, span, UNIT)] + [close]

    def settle():
        shifts = 0.5 * stats[1]
        stats[0] = (0.5 / ROOT * stats[0] - shifts * flat_row(shift1)) / flat_row(gain1)
        stats[1] = shifts

    def spread(slot, n):
        at = lanes(n, 256)

        def even():
            part = dot(lows[slot, :, 0:channels], w_ref[0, at], NT)
            part += dot(lows[slot, :, channels : 2 * channels], w_ref[2, at], NT)
            part += dot(lows[slot, :, 2 * channels : 3 * channels], w_ref[4, at], NT)
            for c in range(2):
                g_buf[slot, 2 * n + c, pl.ds(EDGE, tile, stride=2)] = part[:, lanes_of(c)]

        def odd():
            part = dot(lows[slot, :, 0:channels], w_ref[1, at], NT)
            part += dot(lows[slot, :, channels : 2 * channels], w_ref[3, at], NT)
            for c in range(2):
                g_buf[slot, 2 * n + c, pl.ds(EDGE + 1, tile, stride=2)] = part[:, lanes_of(c)]

        return [even, odd]

    def turn(i, slot, last):
        other = 1 - slot
        w, p = walk.where(i)
        if not last:
            l_copy(i, slot).wait()

            @pl.when(i + 1 < tiles)
            def _():
                l_copy(i + 1, other).start()

            @pl.when(p == 0)
            def _():
                edge = lows[slot, 0:16]
                part = dot(edge[:, channels : 2 * channels], w_ref[1], NT) + dot(edge[:, 2 * channels :], w_ref[3], NT)
                for c in range(slabs):
                    g_buf[slot, c, EDGE - 1 : EDGE] = part[0:1, lanes_of(c)]

            @pl.when(p > 0)
            def _():
                for c in range(slabs):
                    g_buf[slot, c, EDGE - 1 : EDGE] = g_buf[other, c, EDGE + span - 1 : EDGE + span]

        @pl.when(i >= 1)
        def _():
            x_copy(i - 1, other).wait()

        @pl.when(i >= 3)
        def _():
            o_copy(i - 3, other).wait()

        if not last:
            x_copy(i, slot).start()

        def part(n, _):
            units = finish(other, 2 * n) + finish(other, 2 * n + 1)
            interleave([] if last else spread(slot, n), units)
            if last:
                for unit in units:
                    unit()
            elif joined:
                sharing.step(4 * triple + i * (channels // 256) + n)
            return 0

        lax.fori_loop(0, channels // 256, part, 0)

        @pl.when(i >= 1)
        def _():
            o_copy(i - 1, other).start()

    xs[1] = jnp.zeros(xs.shape[1:], f32)
    g_buf[1] = jnp.zeros(g_buf.shape[1:], f32)

    def pair(j, _):
        for slot in range(2):
            turn(2 * j + slot, slot, False)
        return 0

    lax.fori_loop(0, tiles // 2, pair, 0)
    turn(tiles, 0, True)
    settle()
    talk.start_sums(stats)
    o_copy(tiles - 2, 0).wait()
    o_copy(tiles - 1, 1).wait()
    if joined:
        def more(t, _):
            sharing.step(t)
            return 0

        lax.fori_loop(4 * triple + tiles * (channels // 256), sharing.steps, more, 0)
    d_copy = pltpu.make_async_copy(sharing.done if joined else data, w_grad, d_sem)
    d_copy.start()
    talk.finish_sums(grads1)
    d_copy.wait()


def conv_one_spread(low, x, sums1, gain1, shift1, weight, s, parts, entries, number):
    windows, length, _ = low.shape
    channels = x.shape[2]
    tile = min(512, length)
    slabs = channels // LANES
    rows, chunks = 2 * channels, 5 * slabs // 2
    parts = parts.reshape(EARLY * slabs // 2, rows, LANES)
    joined = Reduction.fits(rows)
    estimate = params(10 * low.size * channels // 3, 12 * x.size, x.size)
    da, grad, grads1 = pl.pallas_call(
        functools.partial(conv_one_spread_kernel, tile, entries, joined),
        out_shape=(
            jax.ShapeDtypeStruct((windows, 2 * length, channels), bf16),
            jax.ShapeDtypeStruct((chunks, rows, LANES), bf16),
            jax.ShapeDtypeStruct((8, channels), f32),
        ),
        in_specs=[ANY] * 2 + [VM] * 3 + [ANY] * 3,
        out_specs=(ANY, ANY, VM),
        scratch_shapes=[
            pltpu.VMEM((2, tile, 3 * channels), bf16),
            pltpu.VMEM((2, 2 * tile, channels), f32),
            pltpu.VMEM((2, slabs, 2 * tile + 2 * EDGE, LANES), f32),
            pltpu.VMEM((2, 2 * tile, channels), bf16),
            pltpu.VMEM((slabs, 8, LANES), f32),
            pltpu.VMEM(weight.shape, bf16),
            pltpu.VMEM((channels, channels), f32),
            pltpu.VMEM((AHEAD + 1, tile, channels), bf16),
            pltpu.VMEM((AHEAD + 1, tile, channels), bf16),
            pltpu.VMEM((chunks, rows, LANES), bf16),
            pltpu.VMEM((2, 8, channels), f32),
            DMA((2,)),
            DMA((2,)),
            DMA((2,)),
            DMA,
            DMA,
            DMA((AHEAD + 1, 2)),
        ]
        + Exchange.scratch(channels)
        + (Reduction.scratch(chunks, rows) if joined else []),
        name="conv_one_spread",
        **joining(estimate, number),
    )(low, x, sums1, gain1, shift1, weight, s, parts)
    if not joined:
        grad = lax.psum(grad, ("dp", "seq"))
    return da, grad, grads1


def widen_kernel(one, small, grads1, grads2, grads3, one_out, two_out, three_out, *vectors):
    for c in range(one.shape[1]):
        one_out[0, :, lanes_of(c)] = one[0, c].astype(f32)

    @pl.when(pl.program_id(0) == 0)
    def _():
        taps, rows, width = two_out.shape
        at = 0
        for k in range(taps):
            for c in range(width // LANES):
                two_out[k, :, lanes_of(c)] = small[at : at + rows].astype(f32)
                at += rows
        rows = three_out.shape[0]
        for c in range(three_out.shape[1] // LANES):
            three_out[:, lanes_of(c)] = small[at : at + rows].astype(f32)
            at += rows
        for n, grads in enumerate((grads1, grads2, grads3)):
            vectors[2 * n][...] = grads[0]
            vectors[2 * n + 1][...] = grads[1]


def widen(one, small, two_shape, three_shape, grads):
    channels = two_shape[1]
    slabs = channels // LANES
    one = one.reshape(5, slabs, channels, LANES)
    small = small.reshape(-1, LANES)
    flat = lambda k: (0, 0)
    lengths = [g.shape[1] for g in grads for _ in range(2)]
    return pl.pallas_call(
        widen_kernel,
        grid=(5,),
        out_shape=[
            jax.ShapeDtypeStruct((5, channels, channels), f32),
            jax.ShapeDtypeStruct(two_shape, f32),
            jax.ShapeDtypeStruct(three_shape, f32),
        ]
        + [jax.ShapeDtypeStruct((n,), f32) for n in lengths],
        in_specs=[pl.BlockSpec((1, slabs, channels, LANES), lambda k: (k, 0, 0, 0)), pl.BlockSpec(small.shape, flat)]
        + [pl.BlockSpec(g.shape, flat) for g in grads],
        out_specs=[
            pl.BlockSpec((1, channels, channels), lambda k: (k, 0, 0)),
            pl.BlockSpec(two_shape, lambda k: (0, 0, 0)),
            pl.BlockSpec(three_shape, flat),
        ]
        + [pl.BlockSpec((n,), lambda k: (0,)) for n in lengths],
        name="widen",
        **params(moved=6 * one.size),
    )(one, small, *grads)


def last_kernel(entries, x, da, sums, grads, gain, out):
    center, inverse = center_inverse(sums[...], entries)
    both = grads[...]
    scale = inverse * flat_row(gain)
    lean = scale * inverse * (both[0:1] / entries)
    flat = scale * (both[1:2] / entries)
    for c in range(x.shape[2] // LANES):
        cols, at = lanes(c), lanes_of(c)
        m, s, l, f = center[:, at], scale[:, at], lean[:, at], flat[:, at]
        for r in range(0, x.shape[1], 128):
            rows = slice(r, r + 128)
            out[0, rows, cols] = da[0, rows, cols].astype(f32) * (0.5 * s) - (x[0, rows, cols] - m) * l - f


def input_back(x, da, sums, grads, gain, entries):
    windows, length, channels = x.shape
    tile = min(1024, length)
    per = length // tile
    rows = pl.BlockSpec((1, tile, channels), lambda i: (i // per, i % per, 0))
    whole = lambda i: (0, 0)
    return pl.pallas_call(
        functools.partial(last_kernel, entries),
        grid=(windows * per,),
        out_shape=jax.ShapeDtypeStruct(x.shape, f32),
        in_specs=[
            rows,
            rows,
            pl.BlockSpec((8, channels), whole),
            pl.BlockSpec((8, channels), whole),
            pl.BlockSpec((channels,), lambda i: (0,)),
        ],
        out_specs=rows,
        name="input_back",
        **params(moved=10 * x.size),
    )(x, da, sums, grads, gain)


def on_device(
    inputs,
    conv_one,
    conv_two,
    conv_three,
    gain_one,
    shift_one,
    gain_two,
    shift_two,
    gain_three,
    shift_three,
    cotangent,
):
    windows, length, channels = inputs.shape
    entries = float(windows * length * lax.axis_size("dp") * lax.axis_size("seq"))
    half = entries / 2
    (pooled, s, first, sums1, sums2), c_sides, p_sides = conv_one_forward(
        inputs, cotangent, gain_one, shift_one, conv_one, entries, 0
    )
    (narrow, hidden_two, sums3), n_sides = conv_two_forward(
        pooled, *p_sides, sums2, gain_two, shift_two, conv_two, half, 1
    )
    outputs, da3, stats, three_grad = conv_three_both(
        narrow, cotangent, pooled, sums3, gain_three, shift_three, conv_three, half
    )
    grads3, a_sides = exchange(stats, [da3], 2)
    (da2, two_grad, grads2), b_sides = conv_two_back(
        da3, a_sides, narrow, n_sides, sums3, grads3, gain_three, pooled, sums2, gain_two, shift_two,
        hidden_two, conv_two, half, 3,
    )
    low, parts, small = conv_one_weigh(
        da2, b_sides, pooled, p_sides, cotangent, c_sides, sums2, grads2, gain_two, s, first,
        two_grad, three_grad, entries, 4,
    )
    da1, one_grad, grads1 = conv_one_spread(
        low, inputs, sums1, gain_one, shift_one, conv_one, s, parts, entries, 5
    )
    input_grad = input_back(inputs, da1, sums1, grads1, gain_one, entries)
    small_grads = widen(one_grad, small, conv_two.shape, conv_three.shape, (grads1, grads2, grads3))
    return (outputs, input_grad, *small_grads)


def solution(mesh):
    rows = P("dp", "seq", None)
    in_specs = (rows,) + (P(),) * 9 + (rows,)
    out_specs = (rows, rows) + (P(),) * 9
    return jax.shard_map(on_device, mesh=mesh, in_specs=in_specs, out_specs=out_specs, check_vma=False)
```

```python
import functools

import jax
import jax.numpy as jnp
from jax import lax
from jax.experimental import pallas as pl
from jax.experimental.pallas import tpu as pltpu
from jax.sharding import PartitionSpec as P

epsilon = 1e-05
bf16 = jnp.bfloat16
f32 = jnp.float32
LANES = 128
UNIT = 64
SUB = 32
EDGE = 8
MESH = pl.DeviceIdType.MESH
LINEAR = 0.7978845608028654
CUBIC = 0.7978845608028654 * 0.044715
VMEM_LIMIT = 60 << 20
EARLY = 3
AHEAD = 3
SLOTS = 3
NN = (((1,), (0,)), ((), ()))
NT = (((1,), (1,)), ((), ()))
TN = (((0,), (0,)), ((), ()))


def dot(a, b, dims=NN):
    return lax.dot_general(a, b, dims, preferred_element_type=f32)


def gelu(v):
    half = 0.5 * v
    return half + half * jnp.tanh(v * (LINEAR + CUBIC * (v * v)))


ROOT = CUBIC ** (1.0 / 3.0)
BEND = LINEAR / ROOT


def gelu_scaled(q):
    return q * (1.0 + jnp.tanh(q * (BEND + q * q)))


def slope_scaled(q):
    square = q * q
    th = jnp.tanh(q * (BEND + square))
    return (1.0 + th) * (1.0 + (1.0 - th) * (q * (BEND + 3.0 * square)))


def gelu_both(v):
    square = v * v
    up = 0.5 + 0.5 * jnp.tanh(v * (LINEAR + CUBIC * square))
    value = v * up
    slope = up + value * (1.0 - up) * (2.0 * LINEAR + (6.0 * CUBIC) * square)
    return value, slope


def gelu_slope(v):
    square = v * v
    up = 0.5 + 0.5 * jnp.tanh(v * (LINEAR + CUBIC * square))
    return up + (v * up) * (1.0 - up) * (2.0 * LINEAR + (6.0 * CUBIC) * square)


def center_inverse(sums, entries):
    center = sums[0:1] / entries
    return center, lax.rsqrt(sums[1:2] / entries - center * center + epsilon)


def flat_row(v):
    return v[...].reshape(1, v.shape[0])


def lanes(c, width=LANES):
    if isinstance(c, int):
        return pl.ds(c * width, width)
    return pl.ds(pl.multiple_of(c * width, width), width)


def folded(values):
    return jnp.sum(values.reshape(values.shape[0] // 8, 8, values.shape[1]), axis=0)


def interleave(pieces, units):
    done = 0
    for k, piece in enumerate(pieces):
        piece()
        until = (k + 1) * len(units) // len(pieces)
        for unit in units[done:until]:
            unit()
        done = until


def place_flags():
    return lax.axis_index("seq") == 0, lax.axis_index("seq") == lax.axis_size("seq") - 1


class Walk:
    def __init__(self, windows, length, tile):
        self.tile = tile
        self.per = length // tile
        self.count = windows * self.per
        self.at_start, self.at_end = place_flags()

    def where(self, i):
        return i // self.per, i % self.per

    def hide_left(self, i):
        return jnp.logical_and(i % self.per == 0, self.at_start)

    def hide_right(self, i):
        return jnp.logical_and(i % self.per == self.per - 1, self.at_end)

    def rows(self, i, scale=1):
        span = self.tile * scale
        return pl.ds(pl.multiple_of((i % self.per) * span, span), span)

    def fetch(self, i, src, left, right, dst, sem, scale=1):
        w, p = self.where(i)
        span = self.tile * scale
        low = pl.multiple_of(p * span, span)
        first, last = p == 0, p == self.per - 1
        pltpu.make_async_copy(src.at[w, pl.ds(low, span)], dst.at[pl.ds(EDGE, span)], sem).start()
        head, tail = dst.at[pl.ds(0, EDGE)], dst.at[pl.ds(EDGE + span, EDGE)]

        @pl.when(first)
        def _():
            pltpu.make_async_copy(left.at[w], head, sem).start()

        @pl.when(jnp.logical_not(first))
        def _():
            pltpu.make_async_copy(src.at[w, pl.ds(pl.multiple_of(low - EDGE, EDGE), EDGE)], head, sem).start()

        @pl.when(last)
        def _():
            pltpu.make_async_copy(right.at[w], tail, sem).start()

        @pl.when(jnp.logical_not(last))
        def _():
            pltpu.make_async_copy(src.at[w, pl.ds(pl.multiple_of(low + span, EDGE), EDGE)], tail, sem).start()


def wait_for(dst, sem):
    pltpu.make_async_copy(dst, dst, sem).wait()


ANY = pl.BlockSpec(memory_space=pl.ANY)
VM = pl.BlockSpec(memory_space=pltpu.VMEM)
DMA = pltpu.SemaphoreType.DMA


def params(flops=0, moved=0, waved=0):
    return dict(
        compiler_params=pltpu.CompilerParams(vmem_limit_bytes=VMEM_LIMIT),
        cost_estimate=pl.CostEstimate(flops=flops, bytes_accessed=moved, transcendentals=waved),
    )


def greet(seqs, dps):
    seq, dp = lax.axis_index("seq"), lax.axis_index("dp")
    barrier = pltpu.get_barrier_semaphore()

    def near(d, _):
        pl.semaphore_signal(barrier, inc=1, device_id={"seq": lax.rem(seq + d, seqs)}, device_id_type=MESH)
        return 0

    def far(d, _):
        pl.semaphore_signal(barrier, inc=1, device_id={"dp": lax.rem(dp + d, dps)}, device_id_type=MESH)
        return 0

    lax.fori_loop(1, seqs, near, 0)
    lax.fori_loop(1, dps, far, 0)
    pl.semaphore_wait(barrier, seqs - 1 + dps - 1)


class Exchange:
    SUMS = 7

    def __init__(self, refs, edge_refs=()):
        self.message, self.near, self.far, self.near_send, self.near_recv, self.far_send, self.far_recv = refs
        self.seqs, self.dps = self.near.shape[0], self.far.shape[0]
        self.seq, self.dp = lax.axis_index("seq"), lax.axis_index("dp")
        if edge_refs:
            self.lands, (self.edge_send, self.edge_recv) = edge_refs[:-2], edge_refs[-2:]

    @staticmethod
    def scratch(channels):
        seqs, dps = lax.axis_size("seq"), lax.axis_size("dp")
        rows = -(-2 * (channels // LANES) // 8) * 8
        return [
            pltpu.VMEM((rows, LANES), f32),
            pltpu.VMEM((seqs, rows, LANES), f32),
            pltpu.VMEM((dps, rows, LANES), f32),
            DMA((seqs,)),
            DMA((seqs,)),
            DMA((dps,)),
            DMA((dps,)),
        ]

    @staticmethod
    def edges(arrays):
        return [jax.ShapeDtypeStruct((a.shape[0], EDGE, a.shape[2]), a.dtype) for a in arrays for _ in range(2)]

    @staticmethod
    def edge_scratch(arrays):
        edges = Exchange.edges(arrays)
        return [pltpu.VMEM(e.shape, e.dtype) for e in edges] + [DMA((len(edges),)), DMA((len(edges),))]

    def edge_copy(self, n, src):
        length = src.shape[1]
        part = src.at[:, pl.ds(length - EDGE, EDGE)] if n % 2 == 0 else src.at[:, pl.ds(0, EDGE)]
        to = self.seq + 1 if n % 2 == 0 else self.seq - 1
        return pltpu.make_async_remote_copy(
            src_ref=part, dst_ref=self.lands[n], send_sem=self.edge_send.at[n], recv_sem=self.edge_recv.at[n],
            device_id={"seq": to}, device_id_type=MESH,
        )

    def start_edges(self, sources):
        for a, src in enumerate(sources):
            @pl.when(self.seq < self.seqs - 1)
            def _():
                self.edge_copy(2 * a, src).start()

            @pl.when(self.seq > 0)
            def _():
                self.edge_copy(2 * a + 1, src).start()

    def finish_edges(self, sources):
        for a, src in enumerate(sources):
            @pl.when(self.seq < self.seqs - 1)
            def _():
                self.edge_copy(2 * a, src).wait_send()
                self.edge_copy(2 * a + 1, src).wait_recv()

            @pl.when(self.seq > 0)
            def _():
                self.edge_copy(2 * a + 1, src).wait_send()
                self.edge_copy(2 * a, src).wait_recv()

    def near_copy(self, d):
        return pltpu.make_async_remote_copy(
            src_ref=self.message, dst_ref=self.near.at[self.seq], send_sem=self.near_send.at[d],
            recv_sem=self.near_recv.at[d], device_id={"seq": lax.rem(self.seq + d, self.seqs)}, device_id_type=MESH,
        )

    def far_copy(self, d):
        mine = self.far.at[self.dp]
        return pltpu.make_async_remote_copy(
            src_ref=mine, dst_ref=mine, send_sem=self.far_send.at[d], recv_sem=self.far_recv.at[d],
            device_id={"dp": lax.rem(self.dp + d, self.dps)}, device_id_type=MESH,
        )

    def each(self, count, run):
        def body(d, _):
            run(d)
            return 0

        lax.fori_loop(1, count, body, 0)

    def start_sums(self, stats):
        slabs = stats.shape[2] // LANES
        self.message[...] = jnp.zeros_like(self.message)
        for row in range(2):
            total = jnp.sum(stats[row], axis=0, keepdims=True)
            for c in range(slabs):
                self.message[row * slabs + c : row * slabs + c + 1] = total[:, lanes_of(c)]
        self.each(self.seqs, lambda d: self.near_copy(d).start())
        self.near[self.seq] = self.message[...]
        self.each(self.seqs, lambda d: self.near_copy(d).wait())
        self.far[self.dp] = lax.fori_loop(1, self.seqs, lambda n, t: t + self.near[n], self.near[0])
        self.each(self.dps, lambda d: self.far_copy(d).start())

    def finish_sums(self, sums):
        slabs = sums.shape[1] // LANES
        self.each(self.dps, lambda d: self.far_copy(d).wait())
        total = lax.fori_loop(1, self.dps, lambda n, t: t + self.far[n], self.far[0])
        sums[...] = jnp.zeros_like(sums)
        for row in range(2):
            for c in range(slabs):
                sums[row : row + 1, lanes_of(c)] = total[row * slabs + c : row * slabs + c + 1]


def lanes_of(c):
    return slice(c * LANES, (c + 1) * LANES)


def joining(estimate, number):
    return dict(
        estimate,
        compiler_params=pltpu.CompilerParams(
            vmem_limit_bytes=VMEM_LIMIT, collective_id=number, has_side_effects=True
        ),
    )


def conv_one_kernel(
    tile, entries, x, cotangent, gain, shift, w_hbm,
    pooled, s_out, first_out, sums1, sums2, c_left, c_right, p_left, p_right,
    xs, h_buf, lhs_a, lhs_b, outs, coef, w_ref, stats, x_sem, s_sem, f_sem, o_sem, w_sem, *talks,
):
    windows, length, channels = x.shape
    slabs = channels // LANES
    span = 2 * tile
    walk = Walk(windows, length // 2, tile)
    tiles = walk.count
    lhs = (lhs_a, lhs_b)
    n = Exchange.SUMS
    talk1 = Exchange(talks[:n], talks[2 * n : 2 * n + 6])
    talk2 = Exchange(talks[n : 2 * n], talks[2 * n + 6 :])
    left, right = talk1.lands[:2]

    def scan_copy(i, slot):
        w, _ = walk.where(i)
        return pltpu.make_async_copy(x.at[w, walk.rows(i, 2)], xs.at[slot, pl.ds(EDGE, span)], x_sem.at[slot])

    scan_copy(0, 0).start()
    scan_copy(1, 1).start()
    greet(talk1.seqs, talk1.dps)
    talk1.start_edges((x, cotangent))
    stats[...] = jnp.zeros_like(stats)

    def scan(i, _):
        slot = i % 2
        scan_copy(i, slot).wait()

        def slab(c, _):
            cols = lanes(c)
            total = jnp.zeros((8, LANES), f32)
            squares = jnp.zeros((8, LANES), f32)
            for r in range(EDGE, EDGE + span, 128):
                v = xs[slot, r : r + 128, cols]
                total += folded(v)
                squares += folded(v * v)
            stats[0, :, cols] += total
            stats[1, :, cols] += squares
            return 0

        lax.fori_loop(0, slabs, slab, 0)

        @pl.when(i + 2 < tiles)
        def _():
            scan_copy(i + 2, slot).start()

        return 0

    lax.fori_loop(0, tiles, scan, 0)
    talk1.start_sums(stats)
    w_copy = pltpu.make_async_copy(w_hbm, w_ref, w_sem)

    def load(i, slot):
        walk.fetch(i, x, left, right, xs.at[slot], x_sem.at[slot], 2)

    def s_copy(i, slot, which):
        w, _ = walk.where(i)
        return pltpu.make_async_copy(
            lhs[slot].at[:, pl.ds((2 + which) * channels, channels)], s_out.at[which, w, walk.rows(i)],
            s_sem.at[slot, which],
        )

    def first_copy(i, slot):
        w, _ = walk.where(i)
        return pltpu.make_async_copy(
            lhs[slot].at[pl.ds(0, 16), pl.ds(channels, channels)], first_out.at[w], f_sem
        )

    def o_copy(i, slot):
        w, _ = walk.where(i)
        return pltpu.make_async_copy(outs.at[slot], pooled.at[w, walk.rows(i)], o_sem.at[slot])

    def activate(i, slot, c):
        scale = coef[c, 0:1]
        offset = coef[c, 1:2]
        src = xs.at[slot]
        dst = lhs[slot]
        cols = lanes(c)

        def ends():
            head = gelu_scaled(src[0:EDGE, cols] * scale + offset)
            h_buf[c, 0:EDGE] = jnp.where(walk.hide_left(i), 0.0, head)
            tail = gelu_scaled(src[EDGE + span : 2 * EDGE + span, cols] * scale + offset)
            h_buf[c, EDGE + span : 2 * EDGE + span] = jnp.where(walk.hide_right(i), 0.0, tail)

        def rows(r):
            def run():
                for q in range(EDGE + r, EDGE + r + 2 * UNIT, 2 * SUB):
                    h_buf[c, q : q + 2 * SUB] = gelu_scaled(src[q : q + 2 * SUB, cols] * scale + offset)

            return run

        def taps(r):
            def run():
                for q in range(r, r + UNIT, SUB):
                    h = [h_buf[c, pl.ds(EDGE + 2 * q + d, SUB, stride=2)] for d in range(-2, 4)]
                    for tap in range(5):
                        at = pl.ds(pl.multiple_of(tap * channels + c * LANES, LANES), LANES)
                        dst[q : q + SUB, at] = (h[tap] + h[tap + 1]).astype(bf16)

            return run

        units = [ends, rows(0)]
        for r in range(UNIT, tile, UNIT):
            units += [rows(2 * r), taps(r - UNIT)]
        return units + [taps(tile - UNIT)]

    def matmul(slot, n):
        cols = lanes(n, 256)
        src = lhs[slot]
        held = []

        def piece(k):
            def run():
                at = slice(k * channels, (k + 1) * channels)
                part = dot(src[:, at], w_ref[at, cols])
                held[:] = [held[0] + part] if held else [part]

            return run

        def finish():
            total = (0.25 / ROOT) * held[0]
            outs[slot, :, cols] = total
            stats[0, :, cols] += folded(total)
            stats[1, :, cols] += folded(total * total)

        return [piece(k) for k in range(5)], finish

    talk1.finish_edges((x, cotangent))
    c_left[...] = talk1.lands[2][...]
    c_right[...] = talk1.lands[3][...]
    load(0, 0)
    load(1, 1)
    w_copy.start()
    talk1.finish_sums(sums1)
    center, inverse = center_inverse(sums1[...], entries)
    scale = inverse * flat_row(gain)
    offset = flat_row(shift) - center * scale
    for c in range(slabs):
        coef[c, 0:1] = ROOT * scale[:, lanes_of(c)]
        coef[c, 1:2] = ROOT * offset[:, lanes_of(c)]
    stats[...] = jnp.zeros_like(stats)
    wait_for(xs.at[0], x_sem.at[0])

    def first_slab(c, _):
        for unit in activate(0, 0, c):
            unit()
        return 0

    lax.fori_loop(0, slabs, first_slab, 0)
    for which in range(2):
        s_copy(0, 0, which).start()
    first_copy(0, 0).start()
    w_copy.wait()

    def pair(j, _):
        for slot in range(2):
            i = 2 * j + slot
            other = 1 - slot

            @pl.when(i + 1 < tiles)
            def _():
                wait_for(xs.at[other], x_sem.at[other])

            @pl.when(i + 2 < tiles)
            def _():
                load(i + 2, slot)

            @pl.when(i >= 1)
            def _():
                for which in range(2):
                    s_copy(i - 1, other, which).wait()

                @pl.when((i - 1) % walk.per == 0)
                def _():
                    first_copy(i - 1, other).wait()

            @pl.when(i >= 2)
            def _():
                o_copy(i - 2, slot).wait()

            def part(n, _):
                pieces, finish = matmul(slot, n)
                units = []
                for c in range(2):
                    units += activate(i + 1, other, 2 * n + c)
                interleave(pieces, units)
                finish()
                return 0

            lax.fori_loop(0, channels // 256, part, 0)
            o_copy(i, slot).start()

            @pl.when(i + 1 < tiles)
            def _():
                for which in range(2):
                    s_copy(i + 1, other, which).start()

                @pl.when((i + 1) % walk.per == 0)
                def _():
                    first_copy(i + 1, other).start()

        return 0

    lax.fori_loop(0, tiles // 2, pair, 0)
    for which in range(2):
        s_copy(tiles - 1, 1, which).wait()
    if walk.per == 1:
        first_copy(tiles - 1, 1).wait()
    o_copy(tiles - 2, 0).wait()
    o_copy(tiles - 1, 1).wait()
    talk2.start_edges((pooled,))
    talk2.start_sums(stats)
    talk2.finish_edges((pooled,))
    p_left[...] = talk2.lands[0][...]
    p_right[...] = talk2.lands[1][...]
    talk2.finish_sums(sums2)


def conv_one_forward(x, cotangent, gain, shift, weight, entries, number):
    windows, length, channels = x.shape
    half = length // 2
    tile = min(512, half)
    slabs = channels // LANES
    pooled = jax.ShapeDtypeStruct((windows, half, channels), f32)
    edges = Exchange.edges([cotangent, pooled])
    got = pl.pallas_call(
        functools.partial(conv_one_kernel, tile, entries),
        out_shape=[
            pooled,
            jax.ShapeDtypeStruct((2, windows, half, channels), bf16),
            jax.ShapeDtypeStruct((windows, 16, channels), bf16),
            jax.ShapeDtypeStruct((8, channels), f32),
            jax.ShapeDtypeStruct((8, channels), f32),
        ]
        + edges,
        in_specs=[ANY, ANY, VM, VM, ANY],
        out_specs=[ANY] * 3 + [VM] * 6,
        scratch_shapes=[
            pltpu.VMEM((2, 2 * tile + 2 * EDGE, channels), f32),
            pltpu.VMEM((slabs, 2 * tile + 2 * EDGE, LANES), f32),
            pltpu.VMEM((tile, 5 * channels), bf16),
            pltpu.VMEM((tile, 5 * channels), bf16),
            pltpu.VMEM((2, tile, channels), f32),
            pltpu.VMEM((slabs, 8, LANES), f32),
            pltpu.VMEM((5 * channels, channels), bf16),
            pltpu.VMEM((2, 8, channels), f32),
            DMA((2,)),
            DMA((2, 2)),
            DMA,
            DMA((2,)),
            DMA,
        ]
        + Exchange.scratch(channels) * 2
        + Exchange.edge_scratch([x, cotangent])
        + Exchange.edge_scratch([pooled]),
        name="conv_one_forward",
        **joining(params(10 * windows * half * channels * channels, 12 * x.size, x.size), number),
    )(x, cotangent, gain, shift, weight.reshape(5 * channels, channels))
    return got[:5], got[5:7], got[7:9]


def conv_two_kernel(
    tile, entries, v, left, right, sums, gain, shift, w_hbm, narrow, h_out, sums3, n_left, n_right,
    vs, h_buf, lhs_a, lhs_b, outs, w_ref, stats, v_sem, h_sem, o_sem, w_sem, *talks,
):
    windows, length, channels = v.shape
    slabs = channels // LANES
    walk = Walk(windows, length, tile)
    tiles = walk.count
    lhs = (lhs_a, lhs_b)
    center, inverse = center_inverse(sums[...], entries)
    scale = inverse * flat_row(gain)
    offset = flat_row(shift) - center * scale
    scale, offset = ROOT * scale, ROOT * offset
    stats[...] = jnp.zeros_like(stats)

    def load(i):
        walk.fetch(i, v, left, right, vs.at[i % SLOTS], v_sem.at[i % SLOTS])

    def wait_load(i):
        wait_for(vs.at[i % SLOTS], v_sem.at[i % SLOTS])

    def h_copy(i, slot):
        w, _ = walk.where(i)
        return pltpu.make_async_copy(
            lhs[slot].at[:, pl.ds(channels, channels)], h_out.at[w, walk.rows(i)], h_sem.at[slot]
        )

    def o_copy(i, slot):
        w, _ = walk.where(i)
        return pltpu.make_async_copy(outs.at[slot], narrow.at[w, walk.rows(i)], o_sem.at[slot])

    def activate(i, slot, c):
        a, b = scale[:, lanes_of(c)], offset[:, lanes_of(c)]
        src, dst, cols = vs.at[i % SLOTS], lhs[slot], lanes(c)

        def ends():
            head = gelu_scaled(src[0:EDGE, cols] * a + b)
            h_buf[c, 0:EDGE] = jnp.where(walk.hide_left(i), 0.0, head)
            tail = gelu_scaled(src[EDGE + tile : 2 * EDGE + tile, cols] * a + b)
            h_buf[c, EDGE + tile : 2 * EDGE + tile] = jnp.where(walk.hide_right(i), 0.0, tail)

        def rows(r):
            def run():
                q = EDGE + r
                h_buf[c, q : q + UNIT] = gelu_scaled(src[q : q + UNIT, cols] * a + b)

            return run

        def taps(r):
            def run():
                for tap in range(3):
                    at = EDGE + r + 5 * (tap - 1)
                    dst[r : r + UNIT, lanes(tap * slabs + c)] = h_buf[c, at : at + UNIT].astype(bf16)

            return run

        units = [ends, rows(0)]
        for r in range(UNIT, tile, UNIT):
            units += [rows(r), taps(r - UNIT)]
        return units + [taps(tile - UNIT)]

    for i in range(min(SLOTS, tiles)):
        load(i)
    talk = Exchange(talks[: Exchange.SUMS], talks[Exchange.SUMS :])
    greet(talk.seqs, talk.dps)
    wait_load(0)
    w_copy = pltpu.make_async_copy(w_hbm, w_ref, w_sem)
    w_copy.start()
    for c in range(slabs):
        for unit in activate(0, 0, c):
            unit()
    h_copy(0, 0).start()
    w_copy.wait()

    def pair(j, _):
        for slot in range(2):
            i = 2 * j + slot
            other = 1 - slot

            @pl.when(i + 1 < tiles)
            def _():
                wait_load(i + 1)

            @pl.when(jnp.logical_and(i >= 1, i + SLOTS - 1 < tiles))
            def _():
                load(i + SLOTS - 1)

            @pl.when(i >= 1)
            def _():
                h_copy(i - 1, other).wait()

            @pl.when(i >= 2)
            def _():
                o_copy(i - 2, slot).wait()

            held = []

            def piece(k):
                def run():
                    at = slice(k * channels, (k + 1) * channels)
                    part = dot(lhs[slot][:, at], w_ref[at])
                    held[:] = [held[0] + part] if held else [part]

                return run

            units = []
            for c in range(slabs):
                units += activate(i + 1, other, c)
            interleave([piece(k) for k in range(3)], units)
            total = (0.5 / ROOT) * held[0]
            outs[slot] = total
            stats[0] += folded(total)
            stats[1] += folded(total * total)
            o_copy(i, slot).start()

            @pl.when(i + 1 < tiles)
            def _():
                h_copy(i + 1, other).start()

        return 0

    lax.fori_loop(0, tiles // 2, pair, 0)
    h_copy(tiles - 1, 1).wait()
    o_copy(tiles - 2, 0).wait()
    o_copy(tiles - 1, 1).wait()
    talk.start_edges((narrow,))
    talk.start_sums(stats)
    talk.finish_edges((narrow,))
    n_left[...] = talk.lands[0][...]
    n_right[...] = talk.lands[1][...]
    talk.finish_sums(sums3)


def conv_two_forward(v, left, right, sums, gain, shift, weight, entries, number):
    windows, length, channels = v.shape
    tile = min(512, length)
    slabs = channels // LANES
    width = weight.shape[2]
    narrow = jax.ShapeDtypeStruct((windows, length, width), f32)
    got = pl.pallas_call(
        functools.partial(conv_two_kernel, tile, entries),
        out_shape=[
            narrow,
            jax.ShapeDtypeStruct((windows, length, channels), bf16),
            jax.ShapeDtypeStruct((8, width), f32),
        ]
        + Exchange.edges([narrow]),
        in_specs=[ANY, ANY, ANY, VM, VM, VM, ANY],
        out_specs=[ANY, ANY, VM, VM, VM],
        scratch_shapes=[
            pltpu.VMEM((SLOTS, tile + 2 * EDGE, channels), f32),
            pltpu.VMEM((slabs, tile + 2 * EDGE, LANES), f32),
            pltpu.VMEM((tile, 3 * channels), bf16),
            pltpu.VMEM((tile, 3 * channels), bf16),
            pltpu.VMEM((2, tile, width), f32),
            pltpu.VMEM((3 * channels, width), bf16),
            pltpu.VMEM((2, 8, width), f32),
            DMA((SLOTS,)),
            DMA((2,)),
            DMA((2,)),
            DMA,
        ]
        + Exchange.scratch(width)
        + Exchange.edge_scratch([narrow]),
        name="conv_two_forward",
        **joining(params(6 * v.size * width, 8 * v.size, v.size), number),
    )(v, left, right, sums, gain, shift, weight.reshape(3 * channels, width))
    return got[:3], got[3:]


def conv_three_kernel(
    entries, narrow, cotangent, pooled, sums, gain, shift, w_ref, outputs, da, stats, w_grad,
    branch, grad, hidden, total,
):
    tile = narrow.shape[1]
    step = pl.program_id(0)
    center, inverse = center_inverse(sums[...], entries)

    @pl.when(step == 0)
    def _():
        stats[...] = jnp.zeros_like(stats)
        total[...] = jnp.zeros_like(total)

    branch[...] = cotangent[0].astype(bf16)
    grad[...] = dot(branch[...], w_ref[...], NT)
    for c in range(narrow.shape[2] // LANES):
        cols = lanes(c)
        at = lanes_of(c)
        m, inv, g, s = center[:, at], inverse[:, at], gain[at][None], shift[at][None]
        gains = jnp.zeros((8, LANES), f32)
        shifts = jnp.zeros((8, LANES), f32)
        for r in range(0, tile, UNIT):
            normed = (narrow[0, r : r + UNIT, cols] - m) * inv
            value, slope = gelu_both(normed * g + s)
            hidden[r : r + UNIT, cols] = value.astype(bf16)
            back = slope * grad[r : r + UNIT, cols]
            da[0, r : r + UNIT, cols] = back
            gains += folded(back * normed)
            shifts += folded(back)
        stats[0, :, cols] += gains
        stats[1, :, cols] += shifts
    outputs[0] = pooled[0] + dot(hidden[...], w_ref[...])
    total[...] += dot(hidden[...], branch[...], TN)

    @pl.when(step == pl.num_programs(0) - 1)
    def _():
        for c in range(total.shape[1] // LANES):
            w_grad[c] = total[:, lanes_of(c)].astype(bf16)


def conv_three_both(narrow, cotangent, pooled, sums, gain, shift, weight, entries):
    windows, length, width = narrow.shape
    channels = weight.shape[1]
    tile = min(512, length)
    per = length // tile
    rows = lambda i: (i // per, i % per, 0)
    whole = lambda i: (0, 0)
    return pl.pallas_call(
        functools.partial(conv_three_kernel, entries),
        grid=(windows * per,),
        out_shape=(
            jax.ShapeDtypeStruct((windows, length, channels), f32),
            jax.ShapeDtypeStruct((windows, length, width), f32),
            jax.ShapeDtypeStruct((2, 8, width), f32),
            jax.ShapeDtypeStruct((channels // LANES, width, LANES), bf16),
        ),
        in_specs=[
            pl.BlockSpec((1, tile, width), rows),
            pl.BlockSpec((1, tile, channels), rows),
            pl.BlockSpec((1, tile, channels), rows),
            pl.BlockSpec((8, width), whole),
            pl.BlockSpec((width,), lambda i: (0,)),
            pl.BlockSpec((width,), lambda i: (0,)),
            pl.BlockSpec((width, channels), whole),
        ],
        out_specs=(
            pl.BlockSpec((1, tile, channels), rows),
            pl.BlockSpec((1, tile, width), rows),
            pl.BlockSpec((2, 8, width), lambda i: (0, 0, 0)),
            pl.BlockSpec((channels // LANES, width, LANES), lambda i: (0, 0, 0)),
        ),
        scratch_shapes=[
            pltpu.VMEM((tile, channels), bf16),
            pltpu.VMEM((tile, width), f32),
            pltpu.VMEM((tile, width), bf16),
            pltpu.VMEM((width, channels), f32),
        ],
        name="conv_three_both",
        **params(6 * narrow.size * channels, 12 * cotangent.size, narrow.size),
    )(narrow, cotangent, pooled, sums, gain, shift, weight)


class Reduction:
    STAGES = 8

    def __init__(self, data, done, lands, send, recv, lag):
        self.data, self.done, self.lands, self.send, self.recv = data, done, lands, send, recv
        self.chunks, self.rows = data.shape[0], data.shape[1]
        self.lag = lag
        self.steps = self.chunks + lag * self.STAGES
        self.planes = lax.axis_size("dp") // 4
        seq, dp = lax.axis_index("seq"), lax.axis_index("dp")
        self.seq, self.dp = seq, dp
        one, two = dp % 2, (dp // 2) % 2
        swap = seq == 1
        first_bit, second_bit = jnp.where(swap, two, one), jnp.where(swap, one, two)
        to_one, to_two = dp + 1 - 2 * one, dp + 2 - 4 * two
        first_peer, second_peer = jnp.where(swap, to_two, to_one), jnp.where(swap, to_one, to_two)
        self.peers = ({"seq": 1 - seq}, {"dp": first_peer}, {"dp": second_peer})
        self.plane = dp // 4
        rows = self.rows
        self.size = [rows // 2, rows // 4, rows // 8, rows // 8 // self.planes]
        self.base = [seq * self.size[0]]
        self.away = [(1 - seq) * self.size[0]]
        for bit, size in ((first_bit, self.size[1]), (second_bit, self.size[2])):
            self.away.append(self.base[-1] + (1 - bit) * size)
            self.base.append(self.base[-1] + bit * size)

    def part(self, ref, c, start, size):
        return ref.at[c, pl.ds(pl.multiple_of(start, 16), size)]

    def copy(self, c, number, src, dst, peer):
        return pltpu.make_async_remote_copy(
            src_ref=src, dst_ref=dst, send_sem=self.send.at[c, number], recv_sem=self.recv.at[c, number],
            device_id=peer, device_id_type=MESH,
        )

    def copies(self, c, stage):
        size, base = self.size, self.base
        if stage < 3:
            src = self.part(self.data, c, self.away[stage], size[stage])
            return [self.copy(c, stage, src, self.lands[stage].at[c], self.peers[stage])]
        if stage == 3 or stage == 4:
            out = []
            for d in range(1, self.planes):
                there = (self.plane + d) % self.planes
                peer = {"dp": self.dp + (there - self.plane) * 4}
                if stage == 3:
                    src = self.part(self.data, c, base[2] + there * size[3], size[3])
                    dst = self.lands[3].at[c, d - 1]
                else:
                    src = dst = self.part(self.done, c, base[2] + self.plane * size[3], size[3])
                out.append(self.copy(c, 3 + (stage - 3) * (self.planes - 1) + d - 1, src, dst, peer))
            return out
        level = 7 - stage
        mine = self.part(self.done, c, base[level], size[level])
        return [self.copy(c, 2 * (self.planes - 1) + stage - 2, mine, mine, self.peers[level])]

    def launch(self, c, stage):
        for copy in self.copies(c, stage):
            copy.start()

    def arrive(self, c, stage):
        for copy in self.copies(c, stage):
            copy.wait()
        size, base = self.size, self.base
        if stage < 3:
            unit = self.rows // 8

            def add(r, _):
                at = pl.ds(pl.multiple_of(base[stage] + r * unit, 16), unit)
                got = self.lands[stage][c, pl.ds(pl.multiple_of(r * unit, 16), unit)].astype(f32)
                self.data[c, at] = (self.data[c, at].astype(f32) + got).astype(bf16)
                return 0

            lax.fori_loop(0, size[stage] // unit, add, 0)
        elif stage == 3:
            at = pl.ds(pl.multiple_of(base[2] + self.plane * size[3], 16), size[3])
            total = self.data[c, at].astype(f32)
            for d in range(1, self.planes):
                total += self.lands[3][c, d - 1].astype(f32)
            self.done[c, at] = total.astype(bf16)

    def step(self, t):
        for stage in range(self.STAGES, -1, -1):
            c = t - self.lag * stage

            @pl.when(jnp.logical_and(c >= 0, c < self.chunks))
            def _():
                if stage > 0:
                    self.arrive(c, stage - 1)
                if stage < self.STAGES:
                    self.launch(c, stage)

    @staticmethod
    def fits(rows):
        dps = lax.axis_size("dp")
        return lax.axis_size("seq") == 2 and dps % 4 == 0 and dps > 4 and rows % (128 * (dps // 4)) == 0

    @staticmethod
    def scratch(chunks, rows):
        planes = lax.axis_size("dp") // 4
        copies = 2 * (planes - 1) + 6
        shapes = [(chunks, rows, LANES)] + [(chunks, rows >> (n + 1), LANES) for n in range(3)]
        shapes += [(chunks, planes - 1, rows // 8 // planes, LANES)]
        return [pltpu.VMEM(shape, bf16) for shape in shapes] + [DMA((chunks, copies)), DMA((chunks, copies))]

    @staticmethod
    def of(data, refs, lag):
        return Reduction(data, refs[0], refs[1:5], refs[5], refs[6], lag)


def conv_two_back_kernel(
    tile, entries, joined, da, stats3, v, v_left, v_right, sums3, gain3, pooled, p_left, p_right, sums2, gain2, shift2,
    h, w_hbm, ct, ct_left, ct_right, s, first, three, da_out, low_out, w_grad, small, grads3, grads2,
    das, vs, hs, low_buf, low_a, low_b, total, w_ref, w_flip, stats, wide, wide_buf, wide_a, wide_b, ss, firsts, coef,
    taps, packed, data, a_sem, v_sem, p_sem, h_sem, o_sem, w_sem, r_sem, s_sem, f_sem, l_sem, g_sem, d_sem, t_sem, *refs,
):
    windows, length, width = da.shape
    channels = pooled.shape[2]
    thin, slabs = width // LANES, channels // LANES
    walk = Walk(windows, length, tile)
    tiles = walk.count
    low = (low_a, low_b)
    center, inverse = center_inverse(sums2[...], entries)
    scale = inverse * flat_row(gain2)
    offset = ROOT * (flat_row(shift2) - center * scale)
    scale = ROOT * scale
    stats[...] = jnp.zeros_like(stats)
    total[...] = jnp.zeros_like(total)

    def load(i):
        slot = i % SLOTS
        walk.fetch(i, da, talk3.lands[0], talk3.lands[1], das.at[slot], a_sem.at[slot])
        walk.fetch(i, v, v_left, v_right, vs.at[slot], v_sem.at[slot])

    def wait_load(i):
        slot = i % SLOTS
        wait_for(das.at[slot], a_sem.at[slot])
        wait_for(vs.at[slot], v_sem.at[slot])

    def h_copy(i):
        w, _ = walk.where(i)
        return pltpu.make_async_copy(h.at[w, walk.rows(i)], hs.at[i % SLOTS], h_sem.at[i % SLOTS])

    def p_copy(i):
        w, _ = walk.where(i)
        return pltpu.make_async_copy(
            pooled.at[w, walk.rows(i)], wide.at[i % SLOTS, 0, pl.ds(0, tile)], p_sem.at[i % SLOTS]
        )

    def o_copy(i, slot):
        w, _ = walk.where(i)
        return pltpu.make_async_copy(wide.at[slot, 1, pl.ds(0, tile)], da_out.at[w, walk.rows(i)], o_sem.at[slot])

    def lower(i, slot, c):
        at, cols = lanes_of(c), lanes(c)
        m, s, l, f = center3[:, at], scale3[:, at], lean[:, at], flat[:, at]
        dst = low[slot]

        def value(q, size):
            at = i % SLOTS
            return das[at, q : q + size, cols] * s - (vs[at, q : q + size, cols] - m) * l - f

        def ends():
            low_buf[c, 0:EDGE] = jnp.where(walk.hide_left(i), 0.0, value(0, EDGE))
            low_buf[c, EDGE + tile : 2 * EDGE + tile] = jnp.where(walk.hide_right(i), 0.0, value(EDGE + tile, EDGE))

        def rows(r):
            def run():
                low_buf[c, EDGE + r : EDGE + r + UNIT] = value(EDGE + r, UNIT)

            return run

        def taps(r):
            def run():
                for tap in range(3):
                    q = EDGE + r - 5 * (tap - 1)
                    dst[r : r + UNIT, lanes(tap * thin + c)] = low_buf[c, q : q + UNIT].astype(bf16)

            return run

        units = [ends, rows(0)]
        for r in range(UNIT, tile, UNIT):
            units += [rows(r), taps(r - UNIT)]
        return units + [taps(tile - UNIT)]

    def finish(i, slot, c):
        at, cols = lanes_of(c), lanes(c)
        a, b = scale[:, at], offset[:, at]
        sums = [jnp.zeros((8, LANES), f32), jnp.zeros((8, LANES), f32)]

        def rows(r):
            def run():
                q = wide[i % SLOTS, 0, r : r + UNIT, cols] * a + b
                back = slope_scaled(q) * wide[slot, 2, r : r + UNIT, cols]
                wide[slot, 1, r : r + UNIT, cols] = back
                sums[0] = sums[0] + folded(back * q)
                sums[1] = sums[1] + folded(back)

            return run

        def close():
            stats[0, :, cols] += sums[0]
            stats[1, :, cols] += sums[1]

        return [rows(r) for r in range(0, tile, UNIT)] + [close]

    n = Exchange.SUMS
    talk3 = Exchange(refs[:n], refs[2 * n : 2 * n + 4])
    talk2 = Exchange(refs[n : 2 * n], refs[2 * n + 4 : 2 * n + 8])
    w_copy = pltpu.make_async_copy(w_hbm, w_ref, w_sem)
    w_copy.start()
    f_copy = pltpu.make_async_copy(first, firsts, f_sem)
    f_copy.start()
    size = three.shape[1]

    def three_copy(c):
        chunk, start = divmod(3 * thin * channels + c * size, data.shape[1])
        return pltpu.make_async_copy(three.at[c], data.at[chunk, pl.ds(start, size)], t_sem.at[c])

    for c in range(slabs):
        three_copy(c).start()
    for i in range(min(SLOTS, tiles)):
        h_copy(i).start()
    greet(talk3.seqs, talk3.dps)
    talk3.start_edges((da,))
    talk3.start_sums(stats3)
    w_copy.wait()
    for k in range(3):
        w_flip[k * width : (k + 1) * width] = w_ref[k].T
    talk3.finish_edges((da,))
    for i in range(min(SLOTS, tiles)):
        load(i)
    talk3.finish_sums(grads3)
    center3, inverse3 = center_inverse(sums3[...], entries)
    sums = grads3[...]
    scale3 = inverse3 * flat_row(gain3)
    lean = scale3 * inverse3 * (sums[0:1] / entries)
    flat = scale3 * (sums[1:2] / entries)

    def low_tile(i, slot):
        for c in range(thin):
            for unit in lower(i, slot, c):
                unit()

    def weigh_pair(j, _):
        for slot in range(2):
            i = 2 * j + slot
            other = 1 - slot

            @pl.when(i + 1 < tiles)
            def _():
                wait_load(i + 1)

            @pl.when(jnp.logical_and(i >= 1, i + SLOTS - 1 < tiles))
            def _():
                load(i + SLOTS - 1)
                h_copy(i + SLOTS - 1).start()

            h_copy(i).wait()

            def weigh(n):
                def run():
                    at = slice(n * 256, (n + 1) * 256)
                    total[at] += dot(hs[i % SLOTS, :, at], low[slot][...], TN)

                return run

            units = []
            for c in range(thin):
                units += lower(i + 1, other, c)
            interleave([weigh(n) for n in range(channels // 256)], units)
        return 0

    wait_load(0)
    low_tile(0, 0)
    lax.fori_loop(0, tiles // 2, weigh_pair, 0)
    for i in range(min(SLOTS, tiles)):
        load(i)
    for c in range(3 * thin):
        chunk, start = divmod(c * channels, data.shape[1])
        data[chunk, start : start + channels] = ((0.5 / ROOT) * total[:, lanes_of(c)]).astype(bf16)
    for c in range(slabs):
        three_copy(c).wait()
    if joined:
        sharing = Reduction.of(data, refs[2 * n + 8 :], 4)

    def back_turn(i, slot, last):
        other = 1 - slot
        if not last:
            @pl.when(i + 1 < tiles)
            def _():
                wait_load(i + 1)

            @pl.when(jnp.logical_and(i >= 1, i + SLOTS - 1 < tiles))
            def _():
                load(i + SLOTS - 1)

            @pl.when(jnp.logical_and(i >= 1, i + 1 < tiles))
            def _():
                p_copy(i + 1).start()

        @pl.when(i >= 1)
        def _():
            p_copy(i - 1).wait()

        @pl.when(i >= 3)
        def _():
            o_copy(i - 3, other).wait()

        def back(n):
            def run():
                cols = lanes(n, 256)
                wide[slot, 2, 0:tile, cols] = dot(low[slot][...], w_flip[:, cols])

            return run

        units = []
        for c in range(slabs):
            units += finish(i + SLOTS - 1, other, c)
        if last:
            for unit in units:
                unit()
        else:
            for c in range(thin):
                units += lower(i + 1, other, c)
            interleave([back(n) for n in range(channels // 256)], units)

        @pl.when(i >= 1)
        def _():
            o_copy(i - 1, other).start()

    def back_pair(j, _):
        for slot in range(2):
            back_turn(2 * j + slot, slot, False)
            if joined:
                sharing.step(2 * (2 * j + slot))
                sharing.step(2 * (2 * j + slot) + 1)
        return 0

    wide[SLOTS - 1, 0, 0:tile] = jnp.zeros((tile, channels), f32)
    wide[1, 2, 0:tile] = jnp.zeros((tile, channels), f32)
    for i in range(2):
        p_copy(i).start()
    wait_load(0)
    low_tile(0, 0)
    lax.fori_loop(0, tiles // 2, back_pair, 0)
    back_turn(tiles, 0, True)
    shifts = 0.5 * stats[1]
    stats[0] = (0.5 / ROOT * stats[0] - shifts * flat_row(shift2)) / flat_row(gain2)
    stats[1] = shifts
    o_copy(tiles - 2, 0).wait()
    o_copy(tiles - 1, 1).wait()
    talk2.start_edges((da_out,))
    talk2.start_sums(stats)
    taps[...] = jnp.zeros_like(taps)
    talk2.finish_edges((da_out,))
    lefts, rights = (talk2.lands[0], p_left, ct_left), (talk2.lands[1], p_right, ct_right)

    def wide_load(i):
        slot = i % SLOTS
        for n, src in enumerate((da_out, pooled, ct)):
            walk.fetch(i, src, lefts[n], rights[n], wide.at[slot, n], r_sem.at[slot])

    for i in range(min(SLOTS - 1, tiles)):
        wide_load(i)
    f_copy.wait()
    talk2.finish_sums(grads2)
    sums = grads2[...]
    scale2 = 0.5 * inverse * flat_row(gain2)
    lean2 = scale2 * inverse * (sums[0:1] / entries)
    flat2 = scale2 * (sums[1:2] / entries)
    for c in range(slabs):
        for row, values in enumerate((0.5 * scale2, lean2, center * lean2 - flat2)):
            coef[c, row : row + 1] = values[:, lanes_of(c)]
    wides = (wide_a, wide_b)

    def s_copy(i, slot):
        w, _ = walk.where(i)
        return pltpu.make_async_copy(s.at[:, w, walk.rows(i)], ss.at[slot], s_sem.at[slot])

    def l_copy(i, slot):
        w, _ = walk.where(i)
        return pltpu.make_async_copy(wides[slot], low_out.at[w, walk.rows(i)], l_sem.at[slot])

    def shift_slab(i, slot, c):
        cols = lanes(c)
        sc, l, f = coef[c, 0:1], coef[c, 1:2], coef[c, 2:3]
        dst = wides[slot]

        def value(q, size):
            a, p, g = (wide[i % SLOTS, n, q : q + size, cols] for n in range(3))
            return 0.5 * g + a * sc - p * l + f

        def ends():
            wide_buf[c, 0:EDGE] = jnp.where(walk.hide_left(i), 0.0, value(0, EDGE))
            wide_buf[c, EDGE + tile : 2 * EDGE + tile] = jnp.where(walk.hide_right(i), 0.0, value(EDGE + tile, EDGE))

        def rows(r):
            def run():
                wide_buf[c, EDGE + r : EDGE + r + UNIT] = value(EDGE + r, UNIT)

            return run

        def shifts(r):
            def run():
                for tap in range(3):
                    q = EDGE + r + 1 - tap
                    at = pl.ds(pl.multiple_of(tap * channels + c * LANES, LANES), LANES)
                    dst[r : r + UNIT, at] = wide_buf[c, q : q + UNIT].astype(bf16)

            return run

        units = [ends, rows(0)]
        for r in range(UNIT, tile, UNIT):
            units += [rows(r), shifts(r - UNIT)]
        return units + [shifts(tile - UNIT)]

    s_copy(0, 0).start()
    wait_for(wide.at[0], r_sem.at[0])

    def first_slab(c, _):
        for unit in shift_slab(0, 0, c):
            unit()
        return 0

    lax.fori_loop(0, slabs, first_slab, 0)
    l_copy(0, 0).start()

    def wide_pair(j, _):
        for slot in range(2):
            i = 2 * j + slot
            other = 1 - slot
            w, p = walk.where(i)

            @pl.when(jnp.logical_and(p == 0, walk.at_start))
            def _():
                row = lax.broadcasted_iota(jnp.int32, (16, channels), 0)
                here = jnp.where(row == 0, firsts[w].astype(f32), 0.0).astype(bf16)
                taps[1] += dot(here, wides[slot][0:16, channels : 2 * channels], TN)

            @pl.when(i + 1 < tiles)
            def _():
                wait_for(wide.at[(i + 1) % SLOTS], r_sem.at[(i + 1) % SLOTS])
                s_copy(i + 1, other).start()

            @pl.when(i + SLOTS - 1 < tiles)
            def _():
                wide_load(i + SLOTS - 1)

            @pl.when(i >= 1)
            def _():
                l_copy(i - 1, other).wait()

            s_copy(i, slot).wait()

            def part(n, _):
                cols = lanes(n, 256)

                def weigh(k):
                    def run():
                        at = pl.ds(pl.multiple_of((k // 2) * channels + n * 256, 256), 256)
                        taps[k, :, cols] += dot(ss[slot, k % 2], wides[slot][:, at], TN)

                    return run

                units = shift_slab(i + 1, other, 2 * n) + shift_slab(i + 1, other, 2 * n + 1)
                interleave([weigh(k) for k in range(EARLY)], units)
                if joined:
                    sharing.step(2 * tiles + i * (channels // 256) + n)
                return 0

            lax.fori_loop(0, channels // 256, part, 0)

            @pl.when(i + 1 < tiles)
            def _():
                l_copy(i + 1, other).start()

        return 0

    lax.fori_loop(0, tiles // 2, wide_pair, 0)
    l_copy(tiles - 1, 1).wait()
    for k in range(EARLY):
        for c in range(slabs):
            packed[k, c] = ((0.5 / ROOT) * taps[k, :, lanes_of(c)]).astype(bf16)
    g_copy = pltpu.make_async_copy(packed, w_grad, g_sem)
    g_copy.start()
    if joined:
        def more(t, _):
            sharing.step(t)
            return 0

        lax.fori_loop(2 * tiles + tiles * (channels // 256), sharing.steps, more, 0)
    d_copy = pltpu.make_async_copy(sharing.done if joined else data, small, d_sem)
    d_copy.start()
    d_copy.wait()
    g_copy.wait()


def conv_two_back(
    da, stats3, v, v_sides, sums3, gain3, pooled, p_sides, sums2, gain2, shift2, h, weight, ct, ct_sides, s, first, three,
    entries, number,
):
    windows, length, width = da.shape
    channels = pooled.shape[2]
    tile = min(512, length)
    thin, slabs = width // LANES, channels // LANES
    back = jax.ShapeDtypeStruct((windows, length, channels), f32)
    packed = (EARLY, slabs, channels, LANES)
    rows = 2 * channels
    chunks = (3 * channels * width + width * channels) // (rows * LANES)
    joined = Reduction.fits(rows)
    got = pl.pallas_call(
        functools.partial(conv_two_back_kernel, tile, entries, joined),
        out_shape=[
            back,
            jax.ShapeDtypeStruct((windows, length, 3 * channels), bf16),
            jax.ShapeDtypeStruct(packed, bf16),
            jax.ShapeDtypeStruct((chunks, rows, LANES), bf16),
            jax.ShapeDtypeStruct((8, width), f32),
            jax.ShapeDtypeStruct((8, channels), f32),
        ],
        in_specs=[ANY, VM] + [ANY] * 3 + [VM] * 2 + [ANY] * 3 + [VM] * 3 + [ANY] * 8,
        out_specs=[ANY] * 4 + [VM] * 2,
        scratch_shapes=[
            pltpu.VMEM((SLOTS, tile + 2 * EDGE, width), f32),
            pltpu.VMEM((SLOTS, tile + 2 * EDGE, width), f32),
            pltpu.VMEM((SLOTS, tile, channels), bf16),
            pltpu.VMEM((thin, tile + 2 * EDGE, LANES), f32),
            pltpu.VMEM((tile, 3 * width), bf16),
            pltpu.VMEM((tile, 3 * width), bf16),
            pltpu.VMEM((channels, 3 * width), f32),
            pltpu.VMEM(weight.shape, bf16),
            pltpu.VMEM((3 * width, channels), bf16),
            pltpu.VMEM((2, 8, channels), f32),
            pltpu.VMEM((SLOTS, 3, tile + 2 * EDGE, channels), f32),
            pltpu.VMEM((slabs, tile + 2 * EDGE, LANES), f32),
            pltpu.VMEM((tile, 3 * channels), bf16),
            pltpu.VMEM((tile, 3 * channels), bf16),
            pltpu.VMEM((2, 2, tile, channels), bf16),
            pltpu.VMEM(first.shape, bf16),
            pltpu.VMEM((slabs, 8, LANES), f32),
            pltpu.VMEM((EARLY, channels, channels), f32),
            pltpu.VMEM(packed, bf16),
            pltpu.VMEM((chunks, rows, LANES), bf16),
        ]
        + [DMA((SLOTS,))] * 4
        + [DMA((2,))]
        + [DMA, DMA((SLOTS,)), DMA((2,)), DMA, DMA((2,)), DMA, DMA, DMA((slabs,))]
        + Exchange.scratch(width)
        + Exchange.scratch(channels)
        + Exchange.edge_scratch([da])
        + Exchange.edge_scratch([back])
        + (Reduction.scratch(chunks, rows) if joined else []),
        name="conv_two_back",
        **joining(params(20 * pooled.size * channels, 40 * pooled.size, pooled.size), number),
    )(
        da, stats3, v, *v_sides, sums3, gain3, pooled, *p_sides, sums2, gain2, shift2, h, weight, ct, *ct_sides, s, first,
        three,
    )
    low, parts, small = got[1:4]
    if not joined:
        small = lax.psum(small, ("dp", "seq"))
    return low, parts, small, got[4], got[5]


def conv_one_spread_kernel(
    tile, entries, joined, low, x, sums1, gain1, shift1, w_hbm, s, parts, da_out, q_out, w_grad, grads1,
    lows, xs, g_buf, outs, q_buf, coef, w_ref, total, ss, ls, data, stats, l_sem, x_sem, o_sem, q_sem, w_sem, d_sem, t_sem, *refs,
):
    windows, length, _ = low.shape
    channels = x.shape[2]
    slabs = channels // LANES
    span = 2 * tile
    walk = Walk(windows, length, tile)
    tiles = walk.count
    center, inverse = center_inverse(sums1[...], entries)
    scale = inverse * flat_row(gain1)
    offset = flat_row(shift1) - center * scale
    for c in range(slabs):
        for row, values in enumerate((ROOT * scale, ROOT * offset)):
            coef[c, row : row + 1] = values[:, lanes_of(c)]
    stats[...] = jnp.zeros_like(stats)

    def l_copy(i, slot):
        w, _ = walk.where(i)
        return pltpu.make_async_copy(low.at[w, walk.rows(i)], lows.at[slot], l_sem.at[slot])

    def x_copy(i, slot):
        w, _ = walk.where(i)
        return pltpu.make_async_copy(x.at[w, walk.rows(i, 2)], xs.at[slot], x_sem.at[slot])

    def o_copies(i, slot):
        w, _ = walk.where(i)
        return (
            pltpu.make_async_copy(outs.at[slot], da_out.at[w, walk.rows(i, 2)], o_sem.at[slot]),
            pltpu.make_async_copy(q_buf.at[slot], q_out.at[w, walk.rows(i, 2)], q_sem.at[slot]),
        )

    def t_copies(g, slot):
        k = EARLY + g // tiles
        w, _ = walk.where(g % tiles)
        rows = walk.rows(g % tiles)
        at = pl.ds(pl.multiple_of((k // 2) * channels, channels), channels)
        return (
            pltpu.make_async_copy(s.at[k % 2, w, rows], ss.at[slot], t_sem.at[slot, 0]),
            pltpu.make_async_copy(low.at[w, rows, at], ls.at[slot], t_sem.at[slot, 1]),
        )

    d_copy = pltpu.make_async_copy(parts, data.at[pl.ds(0, EARLY * slabs // 2)], d_sem)
    d_copy.start()
    for g in range(AHEAD):
        for copy in t_copies(g, g):
            copy.start()
    talk, reduction = Exchange(refs[: Exchange.SUMS]), refs[Exchange.SUMS :]
    greet(talk.seqs, talk.dps)
    d_copy.wait()
    l_copy(0, 0).start()
    w_copy = pltpu.make_async_copy(w_hbm, w_ref, w_sem)
    w_copy.start()
    if joined:
        sharing = Reduction.of(data, reduction, 3)
        sharing.step(0)

    late = (5 - EARLY) * tiles
    triple = slabs // 2

    def due(g):
        whole, part = g // tiles, g % tiles
        first = jnp.where(whole == 0, 1, (EARLY + whole - 1) * triple)
        count = jnp.where(whole == 0, EARLY * triple - 1, triple)
        return first + count * part // tiles, first + count * (part + 1) // tiles

    def weigh(g, _):
        slot = g % (AHEAD + 1)
        for copy in t_copies(g, slot):
            copy.wait()

        @pl.when(g + AHEAD < late)
        def _():
            for copy in t_copies(g + AHEAD, (g + AHEAD) % (AHEAD + 1)):
                copy.start()

        @pl.when(g % tiles == 0)
        def _():
            total[...] = dot(ss[slot], ls[slot], TN)

        @pl.when(g % tiles > 0)
        def _():
            total[...] += dot(ss[slot], ls[slot], TN)

        @pl.when(g % tiles == tiles - 1)
        def _():
            for c in range(slabs):
                at = slice((c % 2) * channels, (c % 2 + 1) * channels)
                data[(EARLY + g // tiles) * triple + c // 2, at] = ((0.5 / ROOT) * total[:, lanes_of(c)]).astype(bf16)

        if joined:
            def take(t, _):
                sharing.step(t)
                return 0

            lax.fori_loop(*due(g), take, 0)

        return 0

    lax.fori_loop(0, late, weigh, 0)
    w_copy.wait()

    def finish(slot, c):
        cols = lanes(c)
        a, b = coef[c, 0:1], coef[c, 1:2]
        held = [jnp.zeros((8, LANES), f32), jnp.zeros((8, LANES), f32)]

        def rows(r):
            def run():
                q = xs[slot, r : r + UNIT, cols] * a + b
                incoming = g_buf[slot, c, EDGE + r : EDGE + r + UNIT] + g_buf[slot, c, EDGE + r - 1 : EDGE + r - 1 + UNIT]
                back = slope_scaled(q) * incoming
                outs[slot, r : r + UNIT, cols] = back.astype(bf16)
                q_buf[slot, r : r + UNIT, cols] = q.astype(bf16)
                held[0] = held[0] + folded(back * q)
                held[1] = held[1] + folded(back)

            return run

        def close():
            stats[0, :, cols] += held[0]
            stats[1, :, cols] += held[1]

        return [rows(r) for r in range(0, span, UNIT)] + [close]

    def settle():
        shifts = 0.5 * stats[1]
        stats[0] = (0.5 / ROOT * stats[0] - shifts * flat_row(shift1)) / flat_row(gain1)
        stats[1] = shifts

    def spread(slot, n):
        at = lanes(n, 256)

        def even():
            part = dot(lows[slot, :, 0:channels], w_ref[0, at], NT)
            part += dot(lows[slot, :, channels : 2 * channels], w_ref[2, at], NT)
            part += dot(lows[slot, :, 2 * channels : 3 * channels], w_ref[4, at], NT)
            for c in range(2):
                g_buf[slot, 2 * n + c, pl.ds(EDGE, tile, stride=2)] = part[:, lanes_of(c)]

        def odd():
            part = dot(lows[slot, :, 0:channels], w_ref[1, at], NT)
            part += dot(lows[slot, :, channels : 2 * channels], w_ref[3, at], NT)
            for c in range(2):
                g_buf[slot, 2 * n + c, pl.ds(EDGE + 1, tile, stride=2)] = part[:, lanes_of(c)]

        return [even, odd]

    def turn(i, slot, last):
        other = 1 - slot
        w, p = walk.where(i)
        if not last:
            l_copy(i, slot).wait()

            @pl.when(i + 1 < tiles)
            def _():
                l_copy(i + 1, other).start()

            @pl.when(p == 0)
            def _():
                edge = lows[slot, 0:16]
                part = dot(edge[:, channels : 2 * channels], w_ref[1], NT) + dot(edge[:, 2 * channels :], w_ref[3], NT)
                for c in range(slabs):
                    g_buf[slot, c, EDGE - 1 : EDGE] = part[0:1, lanes_of(c)]

            @pl.when(p > 0)
            def _():
                for c in range(slabs):
                    g_buf[slot, c, EDGE - 1 : EDGE] = g_buf[other, c, EDGE + span - 1 : EDGE + span]

        @pl.when(i >= 1)
        def _():
            x_copy(i - 1, other).wait()

        @pl.when(i >= 3)
        def _():
            for copy in o_copies(i - 3, other):
                copy.wait()

        if not last:
            x_copy(i, slot).start()

        def part(n, _):
            units = finish(other, 2 * n) + finish(other, 2 * n + 1)
            interleave([] if last else spread(slot, n), units)
            if last:
                for unit in units:
                    unit()
            elif joined:
                sharing.step(4 * triple + i * (channels // 256) + n)
            return 0

        lax.fori_loop(0, channels // 256, part, 0)

        @pl.when(i >= 1)
        def _():
            for copy in o_copies(i - 1, other):
                copy.start()

    xs[1] = jnp.zeros(xs.shape[1:], f32)
    g_buf[1] = jnp.zeros(g_buf.shape[1:], f32)

    def pair(j, _):
        for slot in range(2):
            turn(2 * j + slot, slot, False)
        return 0

    lax.fori_loop(0, tiles // 2, pair, 0)
    turn(tiles, 0, True)
    settle()
    talk.start_sums(stats)
    for copy in o_copies(tiles - 2, 0) + o_copies(tiles - 1, 1):
        copy.wait()
    if joined:
        def more(t, _):
            sharing.step(t)
            return 0

        lax.fori_loop(4 * triple + tiles * (channels // 256), sharing.steps, more, 0)
    d_copy = pltpu.make_async_copy(sharing.done if joined else data, w_grad, d_sem)
    d_copy.start()
    talk.finish_sums(grads1)
    d_copy.wait()


def conv_one_spread(low, x, sums1, gain1, shift1, weight, s, parts, entries, number):
    windows, length, _ = low.shape
    channels = x.shape[2]
    tile = min(512, length)
    slabs = channels // LANES
    rows, chunks = 2 * channels, 5 * slabs // 2
    parts = parts.reshape(EARLY * slabs // 2, rows, LANES)
    joined = Reduction.fits(rows)
    estimate = params(10 * low.size * channels // 3, 12 * x.size, x.size)
    da, q, grad, grads1 = pl.pallas_call(
        functools.partial(conv_one_spread_kernel, tile, entries, joined),
        out_shape=(
            jax.ShapeDtypeStruct((windows, 2 * length, channels), bf16),
            jax.ShapeDtypeStruct((windows, 2 * length, channels), bf16),
            jax.ShapeDtypeStruct((chunks, rows, LANES), bf16),
            jax.ShapeDtypeStruct((8, channels), f32),
        ),
        in_specs=[ANY] * 2 + [VM] * 3 + [ANY] * 3,
        out_specs=(ANY, ANY, ANY, VM),
        scratch_shapes=[
            pltpu.VMEM((2, tile, 3 * channels), bf16),
            pltpu.VMEM((2, 2 * tile, channels), f32),
            pltpu.VMEM((2, slabs, 2 * tile + 2 * EDGE, LANES), f32),
            pltpu.VMEM((2, 2 * tile, channels), bf16),
            pltpu.VMEM((2, 2 * tile, channels), bf16),
            pltpu.VMEM((slabs, 8, LANES), f32),
            pltpu.VMEM(weight.shape, bf16),
            pltpu.VMEM((channels, channels), f32),
            pltpu.VMEM((AHEAD + 1, tile, channels), bf16),
            pltpu.VMEM((AHEAD + 1, tile, channels), bf16),
            pltpu.VMEM((chunks, rows, LANES), bf16),
            pltpu.VMEM((2, 8, channels), f32),
            DMA((2,)),
            DMA((2,)),
            DMA((2,)),
            DMA((2,)),
            DMA,
            DMA,
            DMA((AHEAD + 1, 2)),
        ]
        + Exchange.scratch(channels)
        + (Reduction.scratch(chunks, rows) if joined else []),
        name="conv_one_spread",
        **joining(estimate, number),
    )(low, x, sums1, gain1, shift1, weight, s, parts)
    if not joined:
        grad = lax.psum(grad, ("dp", "seq"))
    return da, q, grad, grads1


def last_kernel(
    entries, taps, da, q, sums, grads1, gain, shift, one, small, grads2, grads3, out, one_out, two_out, three_out, *vectors
):
    center, inverse = center_inverse(sums[...], entries)
    both = grads1[...]
    scale = inverse * flat_row(gain)
    lean = inverse * (both[0:1] / entries)
    flat = flat_row(shift) * lean - scale * (both[1:2] / entries)
    for c in range(da.shape[2] // LANES):
        cols, at = lanes(c), lanes_of(c)
        s, l, f = 0.5 * scale[:, at], (1.0 / ROOT) * lean[:, at], flat[:, at]
        for r in range(0, da.shape[1], 128):
            rows = slice(r, r + 128)
            out[0, rows, cols] = da[0, rows, cols].astype(f32) * s - q[0, rows, cols].astype(f32) * l + f

    @pl.when(pl.program_id(0) < taps)
    def _():
        for c in range(one.shape[1]):
            one_out[0, :, lanes_of(c)] = one[0, c].astype(f32)

    @pl.when(pl.program_id(0) == 0)
    def _():
        kinds, rows, width = two_out.shape
        at = 0
        for k in range(kinds):
            for c in range(width // LANES):
                two_out[k, :, lanes_of(c)] = small[at : at + rows].astype(f32)
                at += rows
        rows = three_out.shape[0]
        for c in range(three_out.shape[1] // LANES):
            three_out[:, lanes_of(c)] = small[at : at + rows].astype(f32)
            at += rows
        for n, grads in enumerate((grads1, grads2, grads3)):
            vectors[2 * n][...] = grads[0]
            vectors[2 * n + 1][...] = grads[1]


def last(da, q, sums, gain, shift, one, small, two_shape, three_shape, grads, entries):
    windows, length, channels = da.shape
    slabs = channels // LANES
    tile = min(1024, windows * length // 8)
    per = length // tile
    taps = 5
    one = one.reshape(taps, slabs, channels, LANES)
    small = small.reshape(-1, LANES)
    rows = pl.BlockSpec((1, tile, channels), lambda i: (i // per, i % per, 0))
    flat = lambda i: (0, 0)
    vector = lambda v: pl.BlockSpec((v.shape[0],), lambda i: (0,))
    lengths = [g.shape[1] for g in grads for _ in range(2)]
    tap = lambda i: jnp.minimum(i, taps - 1)
    grads1, grads2, grads3 = grads
    return pl.pallas_call(
        functools.partial(last_kernel, entries, taps),
        grid=(windows * per,),
        out_shape=[
            jax.ShapeDtypeStruct(da.shape, f32),
            jax.ShapeDtypeStruct((taps, channels, channels), f32),
            jax.ShapeDtypeStruct(two_shape, f32),
            jax.ShapeDtypeStruct(three_shape, f32),
        ]
        + [jax.ShapeDtypeStruct((n,), f32) for n in lengths],
        in_specs=[rows, rows, pl.BlockSpec(sums.shape, flat), pl.BlockSpec(grads1.shape, flat), vector(gain), vector(shift)]
        + [pl.BlockSpec((1, slabs, channels, LANES), lambda i: (tap(i), 0, 0, 0)), pl.BlockSpec(small.shape, flat)]
        + [pl.BlockSpec(g.shape, flat) for g in grads[1:]],
        out_specs=[
            rows,
            pl.BlockSpec((1, channels, channels), lambda i: (tap(i), 0, 0)),
            pl.BlockSpec(two_shape, lambda i: (0, 0, 0)),
            pl.BlockSpec(three_shape, flat),
        ]
        + [pl.BlockSpec((n,), lambda i: (0,)) for n in lengths],
        name="last",
        **params(moved=8 * da.size + 6 * one.size),
    )(da, q, sums, grads1, gain, shift, one, small, grads2, grads3)


def on_device(
    inputs,
    conv_one,
    conv_two,
    conv_three,
    gain_one,
    shift_one,
    gain_two,
    shift_two,
    gain_three,
    shift_three,
    cotangent,
):
    windows, length, channels = inputs.shape
    entries = float(windows * length * lax.axis_size("dp") * lax.axis_size("seq"))
    half = entries / 2
    (pooled, s, first, sums1, sums2), c_sides, p_sides = conv_one_forward(
        inputs, cotangent, gain_one, shift_one, conv_one, entries, 0
    )
    (narrow, hidden_two, sums3), n_sides = conv_two_forward(
        pooled, *p_sides, sums2, gain_two, shift_two, conv_two, half, 1
    )
    outputs, da3, stats, three_grad = conv_three_both(
        narrow, cotangent, pooled, sums3, gain_three, shift_three, conv_three, half
    )
    low, parts, small, grads3, grads2 = conv_two_back(
        da3, stats, narrow, n_sides, sums3, gain_three, pooled, p_sides, sums2, gain_two, shift_two, hidden_two, conv_two,
        cotangent, c_sides, s, first, three_grad, half, 2,
    )
    da1, q1, one_grad, grads1 = conv_one_spread(
        low, inputs, sums1, gain_one, shift_one, conv_one, s, parts, entries, 3
    )
    input_grad, *small_grads = last(
        da1, q1, sums1, gain_one, shift_one, one_grad, small, conv_two.shape, conv_three.shape,
        (grads1, grads2, grads3), entries,
    )
    return (outputs, input_grad, *small_grads)


def solution(mesh):
    rows = P("dp", "seq", None)
    in_specs = (rows,) + (P(),) * 9 + (rows,)
    out_specs = (rows, rows) + (P(),) * 9
    return jax.shard_map(on_device, mesh=mesh, in_specs=in_specs, out_specs=out_specs, check_vma=False)
```

```python
import functools

import jax
import jax.numpy as jnp
from jax import lax
from jax.experimental import pallas as pl
from jax.experimental.pallas import tpu as pltpu
from jax.sharding import PartitionSpec as P

epsilon = 1e-05
bf16 = jnp.bfloat16
f32 = jnp.float32
LANES = 128
UNIT = 64
SUB = 32
EDGE = 8
MESH = pl.DeviceIdType.MESH
LINEAR = 0.7978845608028654
CUBIC = 0.7978845608028654 * 0.044715
VMEM_LIMIT = 60 << 20
EARLY = 3
AHEAD = 2
TALL = 1024
SLOTS = 3
NN = (((1,), (0,)), ((), ()))
NT = (((1,), (1,)), ((), ()))
TN = (((0,), (0,)), ((), ()))


def dot(a, b, dims=NN):
    return lax.dot_general(a, b, dims, preferred_element_type=f32)


ROOT = CUBIC ** (1.0 / 3.0)
BEND = LINEAR / ROOT


def gelu_scaled(q):
    return q * (1.0 + jnp.tanh(q * (BEND + q * q)))


def slope_scaled(q):
    square = q * q
    th = jnp.tanh(q * (BEND + square))
    return (1.0 + th) * (1.0 + (1.0 - th) * (q * (BEND + 3.0 * square)))


def center_inverse(sums, entries):
    center = sums[0:1] / entries
    return center, lax.rsqrt(sums[1:2] / entries - center * center + epsilon)


def flat_row(v):
    return v[...].reshape(1, v.shape[0])


def lanes(c, width=LANES):
    if isinstance(c, int):
        return pl.ds(c * width, width)
    return pl.ds(pl.multiple_of(c * width, width), width)


def folded(values):
    return jnp.sum(values.reshape(values.shape[0] // 8, 8, values.shape[1]), axis=0)


def interleave(pieces, units):
    done = 0
    for k, piece in enumerate(pieces):
        piece()
        until = (k + 1) * len(units) // len(pieces)
        for unit in units[done:until]:
            unit()
        done = until


def place_flags():
    return lax.axis_index("seq") == 0, lax.axis_index("seq") == lax.axis_size("seq") - 1


class Walk:
    def __init__(self, windows, length, tile):
        self.tile = tile
        self.per = length // tile
        self.count = windows * self.per
        self.at_start, self.at_end = place_flags()

    def where(self, i):
        return i // self.per, i % self.per

    def hide_left(self, i):
        return jnp.logical_and(i % self.per == 0, self.at_start)

    def hide_right(self, i):
        return jnp.logical_and(i % self.per == self.per - 1, self.at_end)

    def rows(self, i, scale=1):
        span = self.tile * scale
        return pl.ds(pl.multiple_of((i % self.per) * span, span), span)

    def fetch(self, i, src, left, right, dst, sem, scale=1):
        w, p = self.where(i)
        span = self.tile * scale
        low = pl.multiple_of(p * span, span)
        first, last = p == 0, p == self.per - 1
        pltpu.make_async_copy(src.at[w, pl.ds(low, span)], dst.at[pl.ds(EDGE, span)], sem).start()
        head, tail = dst.at[pl.ds(0, EDGE)], dst.at[pl.ds(EDGE + span, EDGE)]

        @pl.when(first)
        def _():
            pltpu.make_async_copy(left.at[w], head, sem).start()

        @pl.when(jnp.logical_not(first))
        def _():
            pltpu.make_async_copy(src.at[w, pl.ds(pl.multiple_of(low - EDGE, EDGE), EDGE)], head, sem).start()

        @pl.when(last)
        def _():
            pltpu.make_async_copy(right.at[w], tail, sem).start()

        @pl.when(jnp.logical_not(last))
        def _():
            pltpu.make_async_copy(src.at[w, pl.ds(pl.multiple_of(low + span, EDGE), EDGE)], tail, sem).start()


def wait_for(dst, sem):
    pltpu.make_async_copy(dst, dst, sem).wait()


ANY = pl.BlockSpec(memory_space=pl.ANY)
VM = pl.BlockSpec(memory_space=pltpu.VMEM)
DMA = pltpu.SemaphoreType.DMA


def params(flops=0, moved=0, waved=0):
    return dict(
        compiler_params=pltpu.CompilerParams(vmem_limit_bytes=VMEM_LIMIT),
        cost_estimate=pl.CostEstimate(flops=flops, bytes_accessed=moved, transcendentals=waved),
    )


def greet(seqs, dps):
    seq, dp = lax.axis_index("seq"), lax.axis_index("dp")
    barrier = pltpu.get_barrier_semaphore()

    def near(d, _):
        pl.semaphore_signal(barrier, inc=1, device_id={"seq": lax.rem(seq + d, seqs)}, device_id_type=MESH)
        return 0

    def far(d, _):
        pl.semaphore_signal(barrier, inc=1, device_id={"dp": lax.rem(dp + d, dps)}, device_id_type=MESH)
        return 0

    lax.fori_loop(1, seqs, near, 0)
    lax.fori_loop(1, dps, far, 0)
    pl.semaphore_wait(barrier, seqs - 1 + dps - 1)


class Exchange:
    SUMS = 7

    def __init__(self, refs, edge_refs=()):
        self.message, self.near, self.far, self.near_send, self.near_recv, self.far_send, self.far_recv = refs
        self.seqs, self.dps = self.near.shape[0], self.far.shape[0]
        self.seq, self.dp = lax.axis_index("seq"), lax.axis_index("dp")
        if edge_refs:
            self.lands, (self.edge_send, self.edge_recv) = edge_refs[:-2], edge_refs[-2:]

    @staticmethod
    def scratch(channels):
        seqs, dps = lax.axis_size("seq"), lax.axis_size("dp")
        rows = -(-2 * (channels // LANES) // 8) * 8
        return [
            pltpu.VMEM((rows, LANES), f32),
            pltpu.VMEM((seqs, rows, LANES), f32),
            pltpu.VMEM((dps, rows, LANES), f32),
            DMA((seqs,)),
            DMA((seqs,)),
            DMA((dps,)),
            DMA((dps,)),
        ]

    @staticmethod
    def edges(arrays):
        return [jax.ShapeDtypeStruct((a.shape[0], EDGE, a.shape[2]), a.dtype) for a in arrays for _ in range(2)]

    @staticmethod
    def edge_scratch(arrays):
        edges = Exchange.edges(arrays)
        return [pltpu.VMEM(e.shape, e.dtype) for e in edges] + [DMA((len(edges),)), DMA((len(edges),))]

    def edge_copy(self, n, src):
        length = src.shape[1]
        part = src.at[:, pl.ds(length - EDGE, EDGE)] if n % 2 == 0 else src.at[:, pl.ds(0, EDGE)]
        to = self.seq + 1 if n % 2 == 0 else self.seq - 1
        return pltpu.make_async_remote_copy(
            src_ref=part, dst_ref=self.lands[n], send_sem=self.edge_send.at[n], recv_sem=self.edge_recv.at[n],
            device_id={"seq": to}, device_id_type=MESH,
        )

    def start_edges(self, sources):
        for a, src in enumerate(sources):
            @pl.when(self.seq < self.seqs - 1)
            def _():
                self.edge_copy(2 * a, src).start()

            @pl.when(self.seq > 0)
            def _():
                self.edge_copy(2 * a + 1, src).start()

    def finish_edges(self, sources):
        for a, src in enumerate(sources):
            @pl.when(self.seq < self.seqs - 1)
            def _():
                self.edge_copy(2 * a, src).wait_send()
                self.edge_copy(2 * a + 1, src).wait_recv()

            @pl.when(self.seq > 0)
            def _():
                self.edge_copy(2 * a + 1, src).wait_send()
                self.edge_copy(2 * a, src).wait_recv()

    def near_copy(self, d):
        return pltpu.make_async_remote_copy(
            src_ref=self.message, dst_ref=self.near.at[self.seq], send_sem=self.near_send.at[d],
            recv_sem=self.near_recv.at[d], device_id={"seq": lax.rem(self.seq + d, self.seqs)}, device_id_type=MESH,
        )

    def far_copy(self, d):
        mine = self.far.at[self.dp]
        return pltpu.make_async_remote_copy(
            src_ref=mine, dst_ref=mine, send_sem=self.far_send.at[d], recv_sem=self.far_recv.at[d],
            device_id={"dp": lax.rem(self.dp + d, self.dps)}, device_id_type=MESH,
        )

    def each(self, count, run):
        def body(d, _):
            run(d)
            return 0

        lax.fori_loop(1, count, body, 0)

    def start_sums(self, stats):
        slabs = stats.shape[2] // LANES
        self.message[...] = jnp.zeros_like(self.message)
        for row in range(2):
            total = jnp.sum(stats[row], axis=0, keepdims=True)
            for c in range(slabs):
                self.message[row * slabs + c : row * slabs + c + 1] = total[:, lanes_of(c)]
        self.each(self.seqs, lambda d: self.near_copy(d).start())
        self.near[self.seq] = self.message[...]
        self.each(self.seqs, lambda d: self.near_copy(d).wait())
        self.far[self.dp] = lax.fori_loop(1, self.seqs, lambda n, t: t + self.near[n], self.near[0])
        self.each(self.dps, lambda d: self.far_copy(d).start())

    def finish_sums(self, sums):
        slabs = sums.shape[1] // LANES
        self.each(self.dps, lambda d: self.far_copy(d).wait())
        total = lax.fori_loop(1, self.dps, lambda n, t: t + self.far[n], self.far[0])
        sums[...] = jnp.zeros_like(sums)
        for row in range(2):
            for c in range(slabs):
                sums[row : row + 1, lanes_of(c)] = total[row * slabs + c : row * slabs + c + 1]


def lanes_of(c):
    return slice(c * LANES, (c + 1) * LANES)


def joining(estimate, number):
    return dict(
        estimate,
        compiler_params=pltpu.CompilerParams(
            vmem_limit_bytes=VMEM_LIMIT, collective_id=number, has_side_effects=True
        ),
    )


def conv_two_phase(
    tile, entries, v, left, right, sums, gain, shift, w_copy, w_ref, talk, narrow, h_out, sums3, n_left, n_right,
    vs, h_buf, lhs_a, lhs_b, outs, stats, v_sem, h_sem, o_sem,
):
    windows, length, channels = v.shape
    slabs = channels // LANES
    walk = Walk(windows, length, tile)
    tiles = walk.count
    lhs = (lhs_a, lhs_b)
    stats[...] = jnp.zeros_like(stats)

    def load(i):
        walk.fetch(i, v, left, right, vs.at[i % SLOTS], v_sem.at[i % SLOTS])

    def wait_load(i):
        wait_for(vs.at[i % SLOTS], v_sem.at[i % SLOTS])

    def h_copy(i, slot):
        w, _ = walk.where(i)
        return pltpu.make_async_copy(
            lhs[slot].at[:, pl.ds(channels, channels)], h_out.at[w, walk.rows(i)], h_sem.at[slot]
        )

    def o_copy(i, slot):
        w, _ = walk.where(i)
        return pltpu.make_async_copy(outs.at[slot], narrow.at[w, walk.rows(i)], o_sem.at[slot])

    def activate(i, slot, c):
        a, b = scale[:, lanes_of(c)], offset[:, lanes_of(c)]
        src, dst, cols = vs.at[i % SLOTS], lhs[slot], lanes(c)

        def ends():
            head = gelu_scaled(src[0:EDGE, cols] * a + b)
            h_buf[c, 0:EDGE] = jnp.where(walk.hide_left(i), 0.0, head)
            tail = gelu_scaled(src[EDGE + tile : 2 * EDGE + tile, cols] * a + b)
            h_buf[c, EDGE + tile : 2 * EDGE + tile] = jnp.where(walk.hide_right(i), 0.0, tail)

        def rows(r):
            def run():
                q = EDGE + r
                h_buf[c, q : q + UNIT] = gelu_scaled(src[q : q + UNIT, cols] * a + b)

            return run

        def taps(r):
            def run():
                for tap in range(3):
                    at = EDGE + r + 5 * (tap - 1)
                    dst[r : r + UNIT, lanes(tap * slabs + c)] = h_buf[c, at : at + UNIT].astype(bf16)

            return run

        units = [ends, rows(0)]
        for r in range(UNIT, tile, UNIT):
            units += [rows(r), taps(r - UNIT)]
        return units + [taps(tile - UNIT)]

    for i in range(min(SLOTS, tiles)):
        load(i)
    center, inverse = center_inverse(sums(), entries)
    scale = inverse * flat_row(gain)
    offset = ROOT * (flat_row(shift) - center * scale)
    scale = ROOT * scale
    wait_load(0)
    for c in range(slabs):
        for unit in activate(0, 0, c):
            unit()
    h_copy(0, 0).start()
    w_copy.wait()

    def pair(j, _):
        for slot in range(2):
            i = 2 * j + slot
            other = 1 - slot

            @pl.when(i + 1 < tiles)
            def _():
                wait_load(i + 1)

            @pl.when(jnp.logical_and(i >= 1, i + SLOTS - 1 < tiles))
            def _():
                load(i + SLOTS - 1)

            @pl.when(i >= 1)
            def _():
                h_copy(i - 1, other).wait()

            @pl.when(i >= 2)
            def _():
                o_copy(i - 2, slot).wait()

            held = []

            def piece(k):
                def run():
                    at = slice(k * channels, (k + 1) * channels)
                    part = dot(lhs[slot][:, at], w_ref[at])
                    held[:] = [held[0] + part] if held else [part]

                return run

            units = []
            for c in range(slabs):
                units += activate(i + 1, other, c)
            interleave([piece(k) for k in range(3)], units)
            total = (0.5 / ROOT) * held[0]
            outs[slot] = total
            stats[0] += folded(total)
            stats[1] += folded(total * total)
            o_copy(i, slot).start()

            @pl.when(i + 1 < tiles)
            def _():
                h_copy(i + 1, other).start()

        return 0

    lax.fori_loop(0, tiles // 2, pair, 0)
    h_copy(tiles - 1, 1).wait()
    o_copy(tiles - 2, 0).wait()
    o_copy(tiles - 1, 1).wait()
    talk.start_edges((narrow,))
    talk.start_sums(stats)
    talk.finish_edges((narrow,))
    n_left[...] = talk.lands[0][...]
    n_right[...] = talk.lands[1][...]
    talk.finish_sums(sums3)


def conv_one_kernel(
    tile, entries, x, cotangent, gain, shift, w_hbm, gain2, shift2, w2_hbm,
    pooled, pooled_low, s_out, first_out, narrow, h_out, sums1, sums2, sums3, c_left, c_right, p_left, p_right, n_left, n_right,
    xs, h_buf, lhs_a, lhs_b, outs, low_outs, coef, w_ref, stats, vs, v_buf, v_lhs_a, v_lhs_b, v_outs, w2_ref, stats3,
    x_sem, scan_sem, s_sem, f_sem, o_sem, q_sem, w_sem, v_sem, h_sem, n_sem, w2_sem, *talks,
):
    windows, length, channels = x.shape
    slabs = channels // LANES
    span = 2 * tile
    walk = Walk(windows, length // 2, tile)
    tiles = walk.count
    lhs = (lhs_a, lhs_b)
    n = Exchange.SUMS
    talk1 = Exchange(talks[:n], talks[3 * n : 3 * n + 6])
    talk2 = Exchange(talks[n : 2 * n], talks[3 * n + 6 : 3 * n + 10])
    talk3 = Exchange(talks[2 * n : 3 * n], talks[3 * n + 10 :])
    left, right = talk1.lands[:2]

    pieces = 4
    part = 2 * span // pieces

    def scan_copy(i):
        slot, w = i % pieces, i // (length // part)
        at = pl.ds(pl.multiple_of(i % (length // part) * part, 8), part)
        room = xs.at[slot // 2, pl.ds(pl.multiple_of(EDGE + slot % 2 * part, 8), part)]
        return pltpu.make_async_copy(x.at[w, at], room, scan_sem.at[slot])

    for i in range(pieces - 1):
        scan_copy(i).start()
    greet(talk1.seqs, talk1.dps)
    talk1.start_edges((x, cotangent))
    stats[...] = jnp.zeros_like(stats)

    def scan(i, _):
        slot = i % pieces
        scan_copy(i).wait()

        @pl.when(i + pieces - 1 < windows * length // part)
        def _():
            scan_copy(i + pieces - 1).start()

        def slab(c, _):
            cols = lanes(c)
            total = jnp.zeros((8, LANES), f32)
            squares = jnp.zeros((8, LANES), f32)
            for r in range(0, part, 128):
                at = pl.ds(pl.multiple_of(EDGE + slot % 2 * part + r, 8), 128)
                v = xs[slot // 2, at, cols]
                total += folded(v)
                squares += folded(v * v)
            stats[0, :, cols] += total
            stats[1, :, cols] += squares
            return 0

        lax.fori_loop(0, slabs, slab, 0)
        return 0

    lax.fori_loop(0, windows * length // part, scan, 0)
    talk1.start_sums(stats)
    w_copy = pltpu.make_async_copy(w_hbm, w_ref, w_sem)
    w2_copy = pltpu.make_async_copy(w2_hbm, w2_ref, w2_sem)

    def load(i, slot):
        walk.fetch(i, x, left, right, xs.at[slot], x_sem.at[slot], 2)

    def s_copy(i, slot, which):
        w, _ = walk.where(i)
        return pltpu.make_async_copy(
            lhs[slot].at[:, pl.ds((2 + which) * channels, channels)], s_out.at[which, w, walk.rows(i)],
            s_sem.at[slot, which],
        )

    def first_copy(i, slot):
        w, _ = walk.where(i)
        return pltpu.make_async_copy(
            lhs[slot].at[pl.ds(0, 16), pl.ds(channels, channels)], first_out.at[w], f_sem
        )

    def o_copies(i, slot):
        w, _ = walk.where(i)
        return (
            pltpu.make_async_copy(outs.at[slot], pooled.at[w, walk.rows(i)], o_sem.at[slot]),
            pltpu.make_async_copy(low_outs.at[slot], pooled_low.at[w, walk.rows(i)], q_sem.at[slot]),
        )

    def activate(i, slot, c):
        scale = coef[c, 0:1]
        offset = coef[c, 1:2]
        src = xs.at[slot]
        dst = lhs[slot]
        cols = lanes(c)

        def ends():
            head = gelu_scaled(src[0:EDGE, cols] * scale + offset)
            h_buf[c, 0:EDGE] = jnp.where(walk.hide_left(i), 0.0, head)
            tail = gelu_scaled(src[EDGE + span : 2 * EDGE + span, cols] * scale + offset)
            h_buf[c, EDGE + span : 2 * EDGE + span] = jnp.where(walk.hide_right(i), 0.0, tail)

        def rows(r):
            def run():
                for q in range(EDGE + r, EDGE + r + 2 * UNIT, 2 * SUB):
                    h_buf[c, q : q + 2 * SUB] = gelu_scaled(src[q : q + 2 * SUB, cols] * scale + offset)

            return run

        def taps(r):
            def run():
                for q in range(r, r + UNIT, SUB):
                    h = [h_buf[c, pl.ds(EDGE + 2 * q + d, SUB, stride=2)] for d in range(-2, 4)]
                    for tap in range(5):
                        at = pl.ds(pl.multiple_of(tap * channels + c * LANES, LANES), LANES)
                        dst[q : q + SUB, at] = (h[tap] + h[tap + 1]).astype(bf16)

            return run

        units = [ends, rows(0)]
        for r in range(UNIT, tile, UNIT):
            units += [rows(2 * r), taps(r - UNIT)]
        return units + [taps(tile - UNIT)]

    def matmul(slot, n):
        cols = lanes(n, 256)
        src = lhs[slot]
        held = []

        def piece(k):
            def run():
                at = slice(k * channels, (k + 1) * channels)
                part = dot(src[:, at], w_ref[at, cols])
                held[:] = [held[0] + part] if held else [part]

            return run

        def finish():
            total = (0.25 / ROOT) * held[0]
            outs[slot, :, cols] = total
            low_outs[slot, :, cols] = total.astype(bf16)
            stats[0, :, cols] += folded(total)
            stats[1, :, cols] += folded(total * total)

        return [piece(k) for k in range(5)], finish

    talk1.finish_edges((x, cotangent))
    c_left[...] = talk1.lands[2][...]
    c_right[...] = talk1.lands[3][...]
    load(0, 0)
    load(1, 1)
    w_copy.start()
    talk1.finish_sums(sums1)
    center, inverse = center_inverse(sums1[...], entries)
    scale = inverse * flat_row(gain)
    offset = flat_row(shift) - center * scale
    for c in range(slabs):
        coef[c, 0:1] = ROOT * scale[:, lanes_of(c)]
        coef[c, 1:2] = ROOT * offset[:, lanes_of(c)]
    stats[...] = jnp.zeros_like(stats)
    wait_for(xs.at[0], x_sem.at[0])

    def first_slab(c, _):
        for unit in activate(0, 0, c):
            unit()
        return 0

    lax.fori_loop(0, slabs, first_slab, 0)
    for which in range(2):
        s_copy(0, 0, which).start()
    first_copy(0, 0).start()
    w_copy.wait()

    def pair(j, _):
        for slot in range(2):
            i = 2 * j + slot
            other = 1 - slot

            @pl.when(i + 1 < tiles)
            def _():
                wait_for(xs.at[other], x_sem.at[other])

            @pl.when(i + 2 < tiles)
            def _():
                load(i + 2, slot)

            @pl.when(i >= 1)
            def _():
                for which in range(2):
                    s_copy(i - 1, other, which).wait()

                @pl.when((i - 1) % walk.per == 0)
                def _():
                    first_copy(i - 1, other).wait()

            @pl.when(i >= 2)
            def _():
                for copy in o_copies(i - 2, slot):
                    copy.wait()

            def part(n, _):
                pieces, finish = matmul(slot, n)
                units = []
                for c in range(2):
                    units += activate(i + 1, other, 2 * n + c)
                interleave(pieces, units)
                finish()
                return 0

            lax.fori_loop(0, channels // 256, part, 0)
            for copy in o_copies(i, slot):
                copy.start()

            @pl.when(i + 1 < tiles)
            def _():
                for which in range(2):
                    s_copy(i + 1, other, which).start()

                @pl.when((i + 1) % walk.per == 0)
                def _():
                    first_copy(i + 1, other).start()

        return 0

    lax.fori_loop(0, tiles // 2, pair, 0)
    for which in range(2):
        s_copy(tiles - 1, 1, which).wait()
    if walk.per == 1:
        first_copy(tiles - 1, 1).wait()
    for copy in o_copies(tiles - 2, 0) + o_copies(tiles - 1, 1):
        copy.wait()
    talk2.start_edges((pooled,))
    talk2.start_sums(stats)
    w2_copy.start()
    talk2.finish_edges((pooled,))
    p_left[...] = talk2.lands[0][...]
    p_right[...] = talk2.lands[1][...]

    def all_sums():
        talk2.finish_sums(sums2)
        return sums2[...]

    conv_two_phase(
        tile, entries / 2, pooled, talk2.lands[0], talk2.lands[1], all_sums, gain2, shift2, w2_copy, w2_ref, talk3,
        narrow, h_out, sums3, n_left, n_right, vs, v_buf, v_lhs_a, v_lhs_b, v_outs, stats3, v_sem, h_sem, n_sem,
    )


def conv_forward(x, cotangent, gain, shift, weight, gain2, shift2, weight2, entries, number):
    windows, length, channels = x.shape
    half = length // 2
    tile = min(512, half)
    slabs = channels // LANES
    width = weight2.shape[2]
    pooled = jax.ShapeDtypeStruct((windows, half, channels), f32)
    narrow = jax.ShapeDtypeStruct((windows, half, width), f32)
    edges = Exchange.edges([cotangent, pooled, narrow])
    got = pl.pallas_call(
        functools.partial(conv_one_kernel, tile, entries),
        out_shape=[
            pooled,
            jax.ShapeDtypeStruct(pooled.shape, bf16),
            jax.ShapeDtypeStruct((2, windows, half, channels), bf16),
            jax.ShapeDtypeStruct((windows, 16, channels), bf16),
            narrow,
            jax.ShapeDtypeStruct((windows, half, channels), bf16),
            jax.ShapeDtypeStruct((8, channels), f32),
            jax.ShapeDtypeStruct((8, channels), f32),
            jax.ShapeDtypeStruct((8, width), f32),
        ]
        + edges,
        in_specs=[ANY, ANY, VM, VM, ANY, VM, VM, ANY],
        out_specs=[ANY] * 6 + [VM] * 9,
        scratch_shapes=[
            pltpu.VMEM((2, 2 * tile + 2 * EDGE, channels), f32),
            pltpu.VMEM((slabs, 2 * tile + 2 * EDGE, LANES), f32),
            pltpu.VMEM((tile, 5 * channels), bf16),
            pltpu.VMEM((tile, 5 * channels), bf16),
            pltpu.VMEM((2, tile, channels), f32),
            pltpu.VMEM((2, tile, channels), bf16),
            pltpu.VMEM((slabs, 8, LANES), f32),
            pltpu.VMEM((5 * channels, channels), bf16),
            pltpu.VMEM((2, 8, channels), f32),
            pltpu.VMEM((SLOTS, tile + 2 * EDGE, channels), f32),
            pltpu.VMEM((slabs, tile + 2 * EDGE, LANES), f32),
            pltpu.VMEM((tile, 3 * channels), bf16),
            pltpu.VMEM((tile, 3 * channels), bf16),
            pltpu.VMEM((2, tile, width), f32),
            pltpu.VMEM((3 * channels, width), bf16),
            pltpu.VMEM((2, 8, width), f32),
            DMA((2,)),
            DMA((4,)),
            DMA((2, 2)),
            DMA,
            DMA((2,)),
            DMA((2,)),
            DMA,
            DMA((SLOTS,)),
            DMA((2,)),
            DMA((2,)),
            DMA,
        ]
        + Exchange.scratch(channels) * 2
        + Exchange.scratch(width)
        + Exchange.edge_scratch([x, cotangent])
        + Exchange.edge_scratch([pooled])
        + Exchange.edge_scratch([narrow]),
        name="conv_forward",
        **joining(params(13 * windows * half * channels * channels, 20 * x.size, 2 * x.size), number),
    )(
        x, cotangent, gain, shift, weight.reshape(5 * channels, channels), gain2, shift2,
        weight2.reshape(3 * channels, width),
    )
    return got[:6], got[6:9], got[9:11], got[11:13], got[13:15]


def conv_three_kernel(
    entries, narrow, cotangent, pooled, sums, gain, shift, w_ref, outputs, da, stats, w_grad,
    branch_a, branch_b, grad_a, grad_b, hidden, total, coef,
):
    tile, width = narrow.shape[1:]
    channels = cotangent.shape[2]
    step = pl.program_id(0)

    @pl.when(step == 0)
    def _():
        center, inverse = center_inverse(sums[...], entries)
        scale = inverse * flat_row(gain)
        offset = flat_row(shift) - center * scale
        coef[0:1] = ROOT * scale
        coef[1:2] = ROOT * offset
        stats[...] = jnp.zeros_like(stats)

    def turn(branch, grad, branch_old, grad_old):
        held = [[jnp.zeros((8, LANES), f32), jnp.zeros((8, LANES), f32)] for _ in range(width // LANES)]

        def back(n):
            def run():
                rows = slice(n * tile // 4, (n + 1) * tile // 4)
                branch[rows] = cotangent[0, rows].astype(bf16)
                if n % 2 == 1:
                    both = slice((n - 1) * tile // 4, (n + 1) * tile // 4)
                    grad[both] = dot(branch[both], w_ref[...], NT)

            return run

        def rows(r, c):
            def run():
                cols = lanes_of(c)
                q = narrow[0, r : r + UNIT, cols] * coef[0:1, cols] + coef[1:2, cols]
                square = q * q
                th = jnp.tanh(q * (BEND + square))
                up = 1.0 + th
                hidden[r : r + UNIT, cols] = (q * up).astype(bf16)
                back = up * (1.0 + (1.0 - th) * (q * (BEND + 3.0 * square))) * grad_old[r : r + UNIT, cols]
                da[0, r : r + UNIT, cols] = back
                held[c][0] = held[c][0] + folded(back * q)
                held[c][1] = held[c][1] + folded(back)

            return run

        def forward(n):
            def run():
                at = slice(n * tile // 2, (n + 1) * tile // 2)
                outputs[0, at] = pooled[0, at].astype(f32) + (0.5 / ROOT) * dot(hidden[at], w_ref[...])

            return run

        def weigh(n):
            def run():
                at = slice(n * tile // 2, (n + 1) * tile // 2)
                got = dot(hidden[at], branch_old[at], TN)
                total[...] = jnp.where(step <= 1, got, total[...] + got) if n == 0 else total[...] + got

            return run

        units = [rows(r, c) for r in range(0, tile, UNIT) for c in range(width // LANES)]
        half = len(units) // 2
        interleave([back(n) for n in range(4)], units[:half])
        interleave([forward(0), weigh(0)], units[half:])
        forward(1)()
        weigh(1)()
        for c in range(width // LANES):
            for n in range(2):
                stats[n, :, lanes_of(c)] += held[c][n]

    @pl.when(step % 2 == 0)
    def _():
        turn(branch_a, grad_a, branch_b, grad_b)

    @pl.when(step % 2 == 1)
    def _():
        turn(branch_b, grad_b, branch_a, grad_a)

    @pl.when(step == 0)
    def _():
        stats[...] = jnp.zeros_like(stats)

    @pl.when(step == pl.num_programs(0) - 1)
    def _():
        shifts = 0.5 * stats[1]
        stats[0] = (0.5 / ROOT * stats[0] - shifts * flat_row(shift)) / flat_row(gain)
        stats[1] = shifts
        for c in range(channels // LANES):
            w_grad[c] = ((0.5 / ROOT) * total[:, lanes_of(c)]).astype(bf16)


def conv_three_both(narrow, cotangent, pooled, sums, gain, shift, weight, entries):
    windows, length, width = narrow.shape
    channels = weight.shape[1]
    tile = min(512, length)
    per = length // tile
    tiles = windows * per
    ahead = lambda i: (jnp.minimum(i, tiles - 1) // per, jnp.minimum(i, tiles - 1) % per, 0)
    rows = lambda i: (jnp.maximum(i - 1, 0) // per, jnp.maximum(i - 1, 0) % per, 0)
    whole = lambda i: (0, 0)
    return pl.pallas_call(
        functools.partial(conv_three_kernel, entries),
        grid=(tiles + 1,),
        out_shape=(
            jax.ShapeDtypeStruct((windows, length, channels), f32),
            jax.ShapeDtypeStruct((windows, length, width), f32),
            jax.ShapeDtypeStruct((2, 8, width), f32),
            jax.ShapeDtypeStruct((channels // LANES, width, LANES), bf16),
        ),
        in_specs=[
            pl.BlockSpec((1, tile, width), rows),
            pl.BlockSpec((1, tile, channels), ahead),
            pl.BlockSpec((1, tile, channels), rows),
            pl.BlockSpec((8, width), whole),
            pl.BlockSpec((width,), lambda i: (0,)),
            pl.BlockSpec((width,), lambda i: (0,)),
            pl.BlockSpec((width, channels), whole),
        ],
        out_specs=(
            pl.BlockSpec((1, tile, channels), rows),
            pl.BlockSpec((1, tile, width), rows),
            pl.BlockSpec((2, 8, width), lambda i: (0, 0, 0)),
            pl.BlockSpec((channels // LANES, width, LANES), lambda i: (0, 0, 0)),
        ),
        scratch_shapes=[pltpu.VMEM((tile, channels), bf16)] * 2
        + [pltpu.VMEM((tile, width), f32)] * 2
        + [pltpu.VMEM((tile, width), bf16), pltpu.VMEM((width, channels), f32), pltpu.VMEM((8, width), f32)],
        name="conv_three_both",
        **params(6 * narrow.size * channels, 12 * cotangent.size, narrow.size),
    )(narrow, cotangent, pooled, sums, gain, shift, weight)


class Reduction:
    STAGES = 8

    def __init__(self, data, done, lands, send, recv, lag):
        self.data, self.done, self.lands, self.send, self.recv = data, done, lands, send, recv
        self.chunks, self.rows = data.shape[0], data.shape[1]
        self.lag = lag
        self.steps = self.chunks + lag * self.STAGES
        self.planes = lax.axis_size("dp") // 4
        seq, dp = lax.axis_index("seq"), lax.axis_index("dp")
        self.seq, self.dp = seq, dp
        one, two = dp % 2, (dp // 2) % 2
        swap = seq == 1
        first_bit, second_bit = jnp.where(swap, two, one), jnp.where(swap, one, two)
        to_one, to_two = dp + 1 - 2 * one, dp + 2 - 4 * two
        first_peer, second_peer = jnp.where(swap, to_two, to_one), jnp.where(swap, to_one, to_two)
        self.peers = ({"seq": 1 - seq}, {"dp": first_peer}, {"dp": second_peer})
        self.plane = dp // 4
        rows = self.rows
        self.size = [rows // 2, rows // 4, rows // 8, rows // 8 // self.planes]
        self.base = [seq * self.size[0]]
        self.away = [(1 - seq) * self.size[0]]
        for bit, size in ((first_bit, self.size[1]), (second_bit, self.size[2])):
            self.away.append(self.base[-1] + (1 - bit) * size)
            self.base.append(self.base[-1] + bit * size)

    def part(self, ref, c, start, size):
        return ref.at[c, pl.ds(pl.multiple_of(start, 16), size)]

    def copy(self, c, number, src, dst, peer):
        return pltpu.make_async_remote_copy(
            src_ref=src, dst_ref=dst, send_sem=self.send.at[c, number], recv_sem=self.recv.at[c, number],
            device_id=peer, device_id_type=MESH,
        )

    def copies(self, c, stage):
        size, base = self.size, self.base
        if stage < 3:
            src = self.part(self.data, c, self.away[stage], size[stage])
            return [self.copy(c, stage, src, self.lands[stage].at[c], self.peers[stage])]
        if stage == 3 or stage == 4:
            out = []
            for d in range(1, self.planes):
                there = (self.plane + d) % self.planes
                peer = {"dp": self.dp + (there - self.plane) * 4}
                if stage == 3:
                    src = self.part(self.data, c, base[2] + there * size[3], size[3])
                    dst = self.lands[3].at[c, d - 1]
                else:
                    src = dst = self.part(self.done, c, base[2] + self.plane * size[3], size[3])
                out.append(self.copy(c, 3 + (stage - 3) * (self.planes - 1) + d - 1, src, dst, peer))
            return out
        level = 7 - stage
        mine = self.part(self.done, c, base[level], size[level])
        return [self.copy(c, 2 * (self.planes - 1) + stage - 2, mine, mine, self.peers[level])]

    def launch(self, c, stage):
        for copy in self.copies(c, stage):
            copy.start()

    def arrive(self, c, stage):
        for copy in self.copies(c, stage):
            copy.wait()
        size, base = self.size, self.base
        if stage < 3:
            unit = self.rows // 8

            def add(r, _):
                at = pl.ds(pl.multiple_of(base[stage] + r * unit, 16), unit)
                got = self.lands[stage][c, pl.ds(pl.multiple_of(r * unit, 16), unit)].astype(f32)
                self.data[c, at] = (self.data[c, at].astype(f32) + got).astype(bf16)
                return 0

            lax.fori_loop(0, size[stage] // unit, add, 0)
        elif stage == 3:
            at = pl.ds(pl.multiple_of(base[2] + self.plane * size[3], 16), size[3])
            total = self.data[c, at].astype(f32)
            for d in range(1, self.planes):
                total += self.lands[3][c, d - 1].astype(f32)
            self.done[c, at] = total.astype(bf16)

    def step(self, t):
        for stage in range(self.STAGES, -1, -1):
            c = t - self.lag * stage

            @pl.when(jnp.logical_and(c >= 0, c < self.chunks))
            def _():
                if stage > 0:
                    self.arrive(c, stage - 1)
                if stage < self.STAGES:
                    self.launch(c, stage)

    @staticmethod
    def fits(rows):
        dps = lax.axis_size("dp")
        return lax.axis_size("seq") == 2 and dps % 4 == 0 and dps > 4 and rows % (128 * (dps // 4)) == 0

    @staticmethod
    def scratch(chunks, rows):
        planes = lax.axis_size("dp") // 4
        copies = 2 * (planes - 1) + 6
        shapes = [(chunks, rows, LANES)] + [(chunks, rows >> (n + 1), LANES) for n in range(3)]
        shapes += [(chunks, planes - 1, rows // 8 // planes, LANES)]
        return [pltpu.VMEM(shape, bf16) for shape in shapes] + [DMA((chunks, copies)), DMA((chunks, copies))]

    @staticmethod
    def of(data, refs, lag):
        return Reduction(data, refs[0], refs[1:5], refs[5], refs[6], lag)


def conv_two_back_kernel(
    tile, entries, joined, da, stats3, v, v_left, v_right, sums3, gain3, pooled, p_left, p_right, sums2, gain2, shift2,
    h, w_hbm, ct, ct_left, ct_right, s, first, three, da_out, low_out, w_grad, small, grads3, grads2,
    das, vs, hs, low_buf, low_a, low_b, total, w_ref, w_flip, stats, wide, wide_buf, wide_a, wide_b, ss, firsts, coef,
    taps, packed, data, a_sem, v_sem, p_sem, h_sem, o_sem, w_sem, r_sem, s_sem, f_sem, l_sem, g_sem, d_sem, t_sem, *refs,
):
    windows, length, width = da.shape
    channels = pooled.shape[2]
    thin, slabs = width // LANES, channels // LANES
    walk = Walk(windows, length, tile)
    tiles = walk.count
    low = (low_a, low_b)
    center, inverse = center_inverse(sums2[...], entries)
    scale = inverse * flat_row(gain2)
    offset = ROOT * (flat_row(shift2) - center * scale)
    scale = ROOT * scale
    stats[...] = jnp.zeros_like(stats)
    total[...] = jnp.zeros_like(total)

    def load(i):
        slot = i % SLOTS
        walk.fetch(i, da, talk3.lands[0], talk3.lands[1], das.at[slot], a_sem.at[slot])
        walk.fetch(i, v, v_left, v_right, vs.at[slot], v_sem.at[slot])

    def wait_load(i):
        slot = i % SLOTS
        wait_for(das.at[slot], a_sem.at[slot])
        wait_for(vs.at[slot], v_sem.at[slot])

    def h_copy(i):
        w, _ = walk.where(i)
        return pltpu.make_async_copy(h.at[w, walk.rows(i)], hs.at[i % SLOTS], h_sem.at[i % SLOTS])

    def p_copy(i):
        w, _ = walk.where(i)
        return pltpu.make_async_copy(
            pooled.at[w, walk.rows(i)], wide.at[i % SLOTS, 0, pl.ds(0, tile)], p_sem.at[i % SLOTS]
        )

    def o_copy(i, slot):
        w, _ = walk.where(i)
        return pltpu.make_async_copy(wide.at[slot, 1, pl.ds(0, tile)], da_out.at[w, walk.rows(i)], o_sem.at[slot])

    def lower(i, slot, c):
        at, cols = lanes_of(c), lanes(c)
        m, s, l, f = center3[:, at], scale3[:, at], lean[:, at], flat[:, at]
        dst = low[slot]

        def value(q, size):
            at = i % SLOTS
            return das[at, q : q + size, cols] * (0.5 * s) - (vs[at, q : q + size, cols] - m) * l - f

        def ends():
            low_buf[c, 0:EDGE] = jnp.where(walk.hide_left(i), 0.0, value(0, EDGE))
            low_buf[c, EDGE + tile : 2 * EDGE + tile] = jnp.where(walk.hide_right(i), 0.0, value(EDGE + tile, EDGE))

        def rows(r):
            def run():
                low_buf[c, EDGE + r : EDGE + r + UNIT] = value(EDGE + r, UNIT)

            return run

        def taps(r):
            def run():
                for tap in range(3):
                    q = EDGE + r - 5 * (tap - 1)
                    dst[r : r + UNIT, lanes(tap * thin + c)] = low_buf[c, q : q + UNIT].astype(bf16)

            return run

        units = [ends, rows(0)]
        for r in range(UNIT, tile, UNIT):
            units += [rows(r), taps(r - UNIT)]
        return units + [taps(tile - UNIT)]

    def finish(i, slot, c):
        at, cols = lanes_of(c), lanes(c)
        a, b = scale[:, at], offset[:, at]
        sums = [jnp.zeros((8, LANES), f32), jnp.zeros((8, LANES), f32)]

        def rows(r):
            def run():
                q = wide[i % SLOTS, 0, r : r + UNIT, cols] * a + b
                back = slope_scaled(q) * wide[slot, 2, r : r + UNIT, cols]
                wide[slot, 1, r : r + UNIT, cols] = back
                sums[0] = sums[0] + folded(back * q)
                sums[1] = sums[1] + folded(back)

            return run

        def close():
            stats[0, :, cols] += sums[0]
            stats[1, :, cols] += sums[1]

        return [rows(r) for r in range(0, tile, UNIT)] + [close]

    n = Exchange.SUMS
    talk3 = Exchange(refs[:n], refs[2 * n : 2 * n + 4])
    talk2 = Exchange(refs[n : 2 * n], refs[2 * n + 4 : 2 * n + 8])
    w_copy = pltpu.make_async_copy(w_hbm, w_ref, w_sem)
    w_copy.start()
    f_copy = pltpu.make_async_copy(first, firsts, f_sem)
    f_copy.start()
    size = three.shape[1]

    def three_copy(c):
        chunk, start = divmod(3 * thin * channels + c * size, data.shape[1])
        return pltpu.make_async_copy(three.at[c], data.at[chunk, pl.ds(start, size)], t_sem.at[c])

    for c in range(slabs):
        three_copy(c).start()
    for i in range(min(SLOTS, tiles)):
        h_copy(i).start()
    greet(talk3.seqs, talk3.dps)
    talk3.start_edges((da,))
    talk3.start_sums(stats3)
    w_copy.wait()
    for k in range(3):
        w_flip[k * width : (k + 1) * width] = w_ref[k].T
    talk3.finish_edges((da,))
    for i in range(min(SLOTS, tiles)):
        load(i)
    talk3.finish_sums(grads3)
    center3, inverse3 = center_inverse(sums3[...], entries)
    sums = grads3[...]
    scale3 = inverse3 * flat_row(gain3)
    lean = scale3 * inverse3 * (sums[0:1] / entries)
    flat = scale3 * (sums[1:2] / entries)

    def low_tile(i, slot):
        for c in range(thin):
            for unit in lower(i, slot, c):
                unit()

    def weigh_pair(j, _):
        for slot in range(2):
            i = 2 * j + slot
            other = 1 - slot

            @pl.when(i + 1 < tiles)
            def _():
                wait_load(i + 1)

            @pl.when(jnp.logical_and(i >= 1, i + SLOTS - 1 < tiles))
            def _():
                load(i + SLOTS - 1)
                h_copy(i + SLOTS - 1).start()

            h_copy(i).wait()

            def weigh(n):
                def run():
                    at = slice(n * 256, (n + 1) * 256)
                    total[at] += dot(hs[i % SLOTS, :, at], low[slot][...], TN)

                return run

            units = []
            for c in range(thin):
                units += lower(i + 1, other, c)
            interleave([weigh(n) for n in range(channels // 256)], units)
        return 0

    wait_load(0)
    low_tile(0, 0)
    lax.fori_loop(0, tiles // 2, weigh_pair, 0)
    for i in range(min(SLOTS, tiles)):
        load(i)
    for c in range(3 * thin):
        chunk, start = divmod(c * channels, data.shape[1])
        data[chunk, start : start + channels] = ((0.5 / ROOT) * total[:, lanes_of(c)]).astype(bf16)
    for c in range(slabs):
        three_copy(c).wait()
    if joined:
        sharing = Reduction.of(data, refs[2 * n + 8 :], 4)

    def back_turn(i, slot, last):
        other = 1 - slot
        if not last:
            @pl.when(i + 1 < tiles)
            def _():
                wait_load(i + 1)

            @pl.when(jnp.logical_and(i >= 1, i + SLOTS - 1 < tiles))
            def _():
                load(i + SLOTS - 1)

            @pl.when(jnp.logical_and(i >= 1, i + 1 < tiles))
            def _():
                p_copy(i + 1).start()

        @pl.when(i >= 1)
        def _():
            p_copy(i - 1).wait()

        @pl.when(i >= 3)
        def _():
            o_copy(i - 3, other).wait()

        def back(n):
            def run():
                cols = lanes(n, 256)
                wide[slot, 2, 0:tile, cols] = dot(low[slot][...], w_flip[:, cols])

            return run

        units = []
        for c in range(slabs):
            units += finish(i + SLOTS - 1, other, c)
        if last:
            for unit in units:
                unit()
        else:
            for c in range(thin):
                units += lower(i + 1, other, c)
            interleave([back(n) for n in range(channels // 256)], units)

        @pl.when(i >= 1)
        def _():
            o_copy(i - 1, other).start()

        @pl.when(i == 0)
        def _():
            stats[...] = jnp.zeros_like(stats)

    def back_pair(j, _):
        for slot in range(2):
            back_turn(2 * j + slot, slot, False)
            if joined:
                sharing.step(2 * (2 * j + slot))
                sharing.step(2 * (2 * j + slot) + 1)
        return 0

    for i in range(2):
        p_copy(i).start()
    wait_load(0)
    low_tile(0, 0)
    lax.fori_loop(0, tiles // 2, back_pair, 0)
    back_turn(tiles, 0, True)
    shifts = 0.5 * stats[1]
    stats[0] = (0.5 / ROOT * stats[0] - shifts * flat_row(shift2)) / flat_row(gain2)
    stats[1] = shifts
    o_copy(tiles - 2, 0).wait()
    o_copy(tiles - 1, 1).wait()
    talk2.start_edges((da_out,))
    talk2.start_sums(stats)
    taps[...] = jnp.zeros_like(taps)
    talk2.finish_edges((da_out,))
    lefts, rights = (talk2.lands[0], p_left, ct_left), (talk2.lands[1], p_right, ct_right)

    def wide_load(i):
        slot = i % SLOTS
        for n, src in enumerate((da_out, pooled, ct)):
            walk.fetch(i, src, lefts[n], rights[n], wide.at[slot, n], r_sem.at[slot])

    for i in range(min(SLOTS - 1, tiles)):
        wide_load(i)
    f_copy.wait()
    talk2.finish_sums(grads2)
    sums = grads2[...]
    scale2 = 0.5 * inverse * flat_row(gain2)
    lean2 = scale2 * inverse * (sums[0:1] / entries)
    flat2 = scale2 * (sums[1:2] / entries)
    for c in range(slabs):
        for row, values in enumerate((0.5 * scale2, lean2, center * lean2 - flat2)):
            coef[c, row : row + 1] = values[:, lanes_of(c)]
    wides = (wide_a, wide_b)

    def s_copy(i, slot):
        w, _ = walk.where(i)
        return pltpu.make_async_copy(s.at[:, w, walk.rows(i)], ss.at[slot], s_sem.at[slot])

    def l_copy(i, slot):
        w, _ = walk.where(i)
        return pltpu.make_async_copy(wides[slot], low_out.at[w, walk.rows(i)], l_sem.at[slot])

    def shift_slab(i, slot, c):
        cols = lanes(c)
        sc, l, f = coef[c, 0:1], coef[c, 1:2], coef[c, 2:3]
        dst = wides[slot]

        def value(q, size):
            a, p, g = (wide[i % SLOTS, n, q : q + size, cols] for n in range(3))
            return 0.5 * g + a * sc - p * l + f

        def ends():
            wide_buf[c, 0:EDGE] = jnp.where(walk.hide_left(i), 0.0, value(0, EDGE))
            wide_buf[c, EDGE + tile : 2 * EDGE + tile] = jnp.where(walk.hide_right(i), 0.0, value(EDGE + tile, EDGE))

        def rows(r):
            def run():
                wide_buf[c, EDGE + r : EDGE + r + UNIT] = value(EDGE + r, UNIT)

            return run

        def shifts(r):
            def run():
                for tap in range(3):
                    q = EDGE + r + 1 - tap
                    at = pl.ds(pl.multiple_of(tap * channels + c * LANES, LANES), LANES)
                    dst[r : r + UNIT, at] = wide_buf[c, q : q + UNIT].astype(bf16)

            return run

        units = [ends, rows(0)]
        for r in range(UNIT, tile, UNIT):
            units += [rows(r), shifts(r - UNIT)]
        return units + [shifts(tile - UNIT)]

    s_copy(0, 0).start()
    wait_for(wide.at[0], r_sem.at[0])

    def first_slab(c, _):
        for unit in shift_slab(0, 0, c):
            unit()
        return 0

    lax.fori_loop(0, slabs, first_slab, 0)
    l_copy(0, 0).start()

    def wide_pair(j, _):
        for slot in range(2):
            i = 2 * j + slot
            other = 1 - slot
            w, p = walk.where(i)

            @pl.when(jnp.logical_and(p == 0, walk.at_start))
            def _():
                row = lax.broadcasted_iota(jnp.int32, (16, channels), 0)
                here = jnp.where(row == 0, firsts[w].astype(f32), 0.0).astype(bf16)
                taps[1] += dot(here, wides[slot][0:16, channels : 2 * channels], TN)

            @pl.when(i + 1 < tiles)
            def _():
                wait_for(wide.at[(i + 1) % SLOTS], r_sem.at[(i + 1) % SLOTS])
                s_copy(i + 1, other).start()

            @pl.when(i + SLOTS - 1 < tiles)
            def _():
                wide_load(i + SLOTS - 1)

            @pl.when(i >= 1)
            def _():
                l_copy(i - 1, other).wait()

            s_copy(i, slot).wait()

            def part(n, _):
                cols = lanes(n, 256)

                def weigh(k):
                    def run():
                        at = pl.ds(pl.multiple_of((k // 2) * channels + n * 256, 256), 256)
                        taps[k, :, cols] += dot(ss[slot, k % 2], wides[slot][:, at], TN)

                    return run

                units = shift_slab(i + 1, other, 2 * n) + shift_slab(i + 1, other, 2 * n + 1)
                interleave([weigh(k) for k in range(EARLY)], units)
                if joined:
                    sharing.step(2 * tiles + i * (channels // 256) + n)
                return 0

            lax.fori_loop(0, channels // 256, part, 0)

            @pl.when(i + 1 < tiles)
            def _():
                l_copy(i + 1, other).start()

        return 0

    lax.fori_loop(0, tiles // 2, wide_pair, 0)
    l_copy(tiles - 1, 1).wait()
    for k in range(EARLY):
        for c in range(slabs):
            packed[k, c] = ((0.5 / ROOT) * taps[k, :, lanes_of(c)]).astype(bf16)
    g_copy = pltpu.make_async_copy(packed, w_grad, g_sem)
    g_copy.start()
    if joined:
        def more(t, _):
            sharing.step(t)
            return 0

        lax.fori_loop(2 * tiles + tiles * (channels // 256), sharing.steps, more, 0)
    d_copy = pltpu.make_async_copy(sharing.done if joined else data, small, d_sem)
    d_copy.start()
    d_copy.wait()
    g_copy.wait()


def conv_two_back(
    da, stats3, v, v_sides, sums3, gain3, pooled, p_sides, sums2, gain2, shift2, h, weight, ct, ct_sides, s, first, three,
    entries, number,
):
    windows, length, width = da.shape
    channels = pooled.shape[2]
    tile = min(512, length)
    thin, slabs = width // LANES, channels // LANES
    back = jax.ShapeDtypeStruct((windows, length, channels), f32)
    packed = (EARLY, slabs, channels, LANES)
    rows = 2 * channels
    chunks = (3 * channels * width + width * channels) // (rows * LANES)
    joined = Reduction.fits(rows)
    got = pl.pallas_call(
        functools.partial(conv_two_back_kernel, tile, entries, joined),
        out_shape=[
            back,
            jax.ShapeDtypeStruct((windows, length, 3 * channels), bf16),
            jax.ShapeDtypeStruct(packed, bf16),
            jax.ShapeDtypeStruct((chunks, rows, LANES), bf16),
            jax.ShapeDtypeStruct((8, width), f32),
            jax.ShapeDtypeStruct((8, channels), f32),
        ],
        in_specs=[ANY, VM] + [ANY] * 3 + [VM] * 2 + [ANY] * 3 + [VM] * 3 + [ANY] * 8,
        out_specs=[ANY] * 4 + [VM] * 2,
        scratch_shapes=[
            pltpu.VMEM((SLOTS, tile + 2 * EDGE, width), f32),
            pltpu.VMEM((SLOTS, tile + 2 * EDGE, width), f32),
            pltpu.VMEM((SLOTS, tile, channels), bf16),
            pltpu.VMEM((thin, tile + 2 * EDGE, LANES), f32),
            pltpu.VMEM((tile, 3 * width), bf16),
            pltpu.VMEM((tile, 3 * width), bf16),
            pltpu.VMEM((channels, 3 * width), f32),
            pltpu.VMEM(weight.shape, bf16),
            pltpu.VMEM((3 * width, channels), bf16),
            pltpu.VMEM((2, 8, channels), f32),
            pltpu.VMEM((SLOTS, 3, tile + 2 * EDGE, channels), f32),
            pltpu.VMEM((slabs, tile + 2 * EDGE, LANES), f32),
            pltpu.VMEM((tile, 3 * channels), bf16),
            pltpu.VMEM((tile, 3 * channels), bf16),
            pltpu.VMEM((2, 2, tile, channels), bf16),
            pltpu.VMEM(first.shape, bf16),
            pltpu.VMEM((slabs, 8, LANES), f32),
            pltpu.VMEM((EARLY, channels, channels), f32),
            pltpu.VMEM(packed, bf16),
            pltpu.VMEM((chunks, rows, LANES), bf16),
        ]
        + [DMA((SLOTS,))] * 4
        + [DMA((2,))]
        + [DMA, DMA((SLOTS,)), DMA((2,)), DMA, DMA((2,)), DMA, DMA, DMA((slabs,))]
        + Exchange.scratch(width)
        + Exchange.scratch(channels)
        + Exchange.edge_scratch([da])
        + Exchange.edge_scratch([back])
        + (Reduction.scratch(chunks, rows) if joined else []),
        name="conv_two_back",
        **joining(params(20 * pooled.size * channels, 40 * pooled.size, pooled.size), number),
    )(
        da, stats3, v, *v_sides, sums3, gain3, pooled, *p_sides, sums2, gain2, shift2, h, weight, ct, *ct_sides, s, first,
        three,
    )
    low, parts, small = got[1:4]
    if not joined:
        small = lax.psum(small, ("dp", "seq"))
    return low, parts, small, got[4], got[5]


def conv_one_spread_kernel(
    tile, entries, joined, low, x, sums1, gain1, shift1, w_hbm, s, parts, da_out, q_out, w_grad, grads1,
    lows, xs, g_buf, outs, q_buf, coef, w_ref, total, ss, ls, data, stats, l_sem, x_sem, o_sem, q_sem, w_sem, d_sem, t_sem, *refs,
):
    windows, length, _ = low.shape
    channels = x.shape[2]
    slabs = channels // LANES
    span = 2 * tile
    walk = Walk(windows, length, tile)
    tiles = walk.count
    tall = Walk(windows, length, min(TALL, length))
    center, inverse = center_inverse(sums1[...], entries)
    scale = inverse * flat_row(gain1)
    offset = flat_row(shift1) - center * scale
    for c in range(slabs):
        for row, values in enumerate((ROOT * scale, ROOT * offset)):
            coef[c, row : row + 1] = values[:, lanes_of(c)]
    stats[...] = jnp.zeros_like(stats)

    def l_copy(i, slot):
        w, _ = walk.where(i)
        return pltpu.make_async_copy(low.at[w, walk.rows(i)], lows.at[slot], l_sem.at[slot])

    def x_copy(i, slot):
        w, _ = walk.where(i)
        return pltpu.make_async_copy(x.at[w, walk.rows(i, 2)], xs.at[slot], x_sem.at[slot])

    def o_copies(i, slot):
        w, _ = walk.where(i)
        return (
            pltpu.make_async_copy(outs.at[slot], da_out.at[w, walk.rows(i, 2)], o_sem.at[slot]),
            pltpu.make_async_copy(q_buf.at[slot], q_out.at[w, walk.rows(i, 2)], q_sem.at[slot]),
        )

    def t_copies(g, slot):
        k = EARLY + g // tall.count
        w, _ = tall.where(g % tall.count)
        rows = tall.rows(g % tall.count)
        at = pl.ds(pl.multiple_of((k // 2) * channels, channels), channels)
        return (
            pltpu.make_async_copy(s.at[k % 2, w, rows], ss.at[slot], t_sem.at[slot, 0]),
            pltpu.make_async_copy(low.at[w, rows, at], ls.at[slot], t_sem.at[slot, 1]),
        )

    d_copy = pltpu.make_async_copy(parts, data.at[pl.ds(0, EARLY * slabs // 2)], d_sem)
    d_copy.start()
    for g in range(AHEAD):
        for copy in t_copies(g, g):
            copy.start()
    talk, reduction = Exchange(refs[: Exchange.SUMS]), refs[Exchange.SUMS :]
    greet(talk.seqs, talk.dps)
    d_copy.wait()
    l_copy(0, 0).start()
    w_copy = pltpu.make_async_copy(w_hbm, w_ref, w_sem)
    w_copy.start()
    if joined:
        sharing = Reduction.of(data, reduction, 3)
        sharing.step(0)

    late = (5 - EARLY) * tall.count
    triple = slabs // 2

    def due(g):
        whole, part = g // tall.count, g % tall.count
        first = jnp.where(whole == 0, 1, (EARLY + whole - 1) * triple)
        count = jnp.where(whole == 0, EARLY * triple - 1, triple)
        return first + count * part // tall.count, first + count * (part + 1) // tall.count

    def weigh(g, _):
        slot = g % (AHEAD + 1)
        for copy in t_copies(g, slot):
            copy.wait()

        @pl.when(g + AHEAD < late)
        def _():
            for copy in t_copies(g + AHEAD, (g + AHEAD) % (AHEAD + 1)):
                copy.start()

        @pl.when(g % tall.count == 0)
        def _():
            total[...] = dot(ss[slot], ls[slot], TN)

        @pl.when(g % tall.count > 0)
        def _():
            total[...] += dot(ss[slot], ls[slot], TN)

        @pl.when(g % tall.count == tall.count - 1)
        def _():
            for c in range(slabs):
                at = slice((c % 2) * channels, (c % 2 + 1) * channels)
                data[(EARLY + g // tall.count) * triple + c // 2, at] = ((0.5 / ROOT) * total[:, lanes_of(c)]).astype(bf16)

        if joined:
            def take(t, _):
                sharing.step(t)
                return 0

            lax.fori_loop(*due(g), take, 0)

        return 0

    lax.fori_loop(0, late, weigh, 0)
    w_copy.wait()

    def finish(slot, c):
        cols = lanes(c)
        a, b = coef[c, 0:1], coef[c, 1:2]
        held = [jnp.zeros((8, LANES), f32), jnp.zeros((8, LANES), f32)]

        def rows(r):
            def run():
                q = xs[slot, r : r + UNIT, cols] * a + b
                incoming = g_buf[slot, c, EDGE + r : EDGE + r + UNIT] + g_buf[slot, c, EDGE + r - 1 : EDGE + r - 1 + UNIT]
                back = slope_scaled(q) * incoming
                outs[slot, r : r + UNIT, cols] = back.astype(bf16)
                q_buf[slot, r : r + UNIT, cols] = q.astype(bf16)
                held[0] = held[0] + folded(back * q)
                held[1] = held[1] + folded(back)

            return run

        def close():
            stats[0, :, cols] += held[0]
            stats[1, :, cols] += held[1]

        return [rows(r) for r in range(0, span, UNIT)] + [close]

    def settle():
        shifts = 0.5 * stats[1]
        stats[0] = (0.5 / ROOT * stats[0] - shifts * flat_row(shift1)) / flat_row(gain1)
        stats[1] = shifts

    def spread(slot, n):
        at = lanes(n, 256)

        def even():
            part = dot(lows[slot, :, 0:channels], w_ref[0, at], NT)
            part += dot(lows[slot, :, channels : 2 * channels], w_ref[2, at], NT)
            part += dot(lows[slot, :, 2 * channels : 3 * channels], w_ref[4, at], NT)
            for c in range(2):
                g_buf[slot, 2 * n + c, pl.ds(EDGE, tile, stride=2)] = part[:, lanes_of(c)]

        def odd():
            part = dot(lows[slot, :, 0:channels], w_ref[1, at], NT)
            part += dot(lows[slot, :, channels : 2 * channels], w_ref[3, at], NT)
            for c in range(2):
                g_buf[slot, 2 * n + c, pl.ds(EDGE + 1, tile, stride=2)] = part[:, lanes_of(c)]

        return [even, odd]

    def turn(i, slot, last):
        other = 1 - slot
        w, p = walk.where(i)
        if not last:
            l_copy(i, slot).wait()

            @pl.when(i + 1 < tiles)
            def _():
                l_copy(i + 1, other).start()

            @pl.when(p == 0)
            def _():
                edge = lows[slot, 0:16]
                part = dot(edge[:, channels : 2 * channels], w_ref[1], NT) + dot(edge[:, 2 * channels :], w_ref[3], NT)
                for c in range(slabs):
                    g_buf[slot, c, EDGE - 1 : EDGE] = part[0:1, lanes_of(c)]

            @pl.when(p > 0)
            def _():
                for c in range(slabs):
                    g_buf[slot, c, EDGE - 1 : EDGE] = g_buf[other, c, EDGE + span - 1 : EDGE + span]

        @pl.when(i >= 1)
        def _():
            x_copy(i - 1, other).wait()

        @pl.when(i >= 3)
        def _():
            for copy in o_copies(i - 3, other):
                copy.wait()

        if not last:
            x_copy(i, slot).start()

        def part(n, _):
            units = finish(other, 2 * n) + finish(other, 2 * n + 1)
            interleave([] if last else spread(slot, n), units)
            if last:
                for unit in units:
                    unit()
            elif joined:
                sharing.step(4 * triple + i * (channels // 256) + n)
            return 0

        lax.fori_loop(0, channels // 256, part, 0)

        @pl.when(i >= 1)
        def _():
            for copy in o_copies(i - 1, other):
                copy.start()

        @pl.when(i == 0)
        def _():
            stats[...] = jnp.zeros_like(stats)


    def pair(j, _):
        for slot in range(2):
            turn(2 * j + slot, slot, False)
        return 0

    lax.fori_loop(0, tiles // 2, pair, 0)
    turn(tiles, 0, True)
    settle()
    talk.start_sums(stats)
    for copy in o_copies(tiles - 2, 0) + o_copies(tiles - 1, 1):
        copy.wait()
    if joined:
        def more(t, _):
            sharing.step(t)
            return 0

        lax.fori_loop(4 * triple + tiles * (channels // 256), sharing.steps, more, 0)
    d_copy = pltpu.make_async_copy(sharing.done if joined else data, w_grad, d_sem)
    d_copy.start()
    talk.finish_sums(grads1)
    d_copy.wait()


def conv_one_spread(low, x, sums1, gain1, shift1, weight, s, parts, entries, number):
    windows, length, _ = low.shape
    channels = x.shape[2]
    tile = min(512, length)
    slabs = channels // LANES
    rows, chunks = 2 * channels, 5 * slabs // 2
    parts = parts.reshape(EARLY * slabs // 2, rows, LANES)
    joined = Reduction.fits(rows)
    estimate = params(10 * low.size * channels // 3, 12 * x.size, x.size)
    da, q, grad, grads1 = pl.pallas_call(
        functools.partial(conv_one_spread_kernel, tile, entries, joined),
        out_shape=(
            jax.ShapeDtypeStruct((windows, 2 * length, channels), bf16),
            jax.ShapeDtypeStruct((windows, 2 * length, channels), bf16),
            jax.ShapeDtypeStruct((chunks, rows, LANES), bf16),
            jax.ShapeDtypeStruct((8, channels), f32),
        ),
        in_specs=[ANY] * 2 + [VM] * 3 + [ANY] * 3,
        out_specs=(ANY, ANY, ANY, VM),
        scratch_shapes=[
            pltpu.VMEM((2, tile, 3 * channels), bf16),
            pltpu.VMEM((2, 2 * tile, channels), f32),
            pltpu.VMEM((2, slabs, 2 * tile + 2 * EDGE, LANES), f32),
            pltpu.VMEM((2, 2 * tile, channels), bf16),
            pltpu.VMEM((2, 2 * tile, channels), bf16),
            pltpu.VMEM((slabs, 8, LANES), f32),
            pltpu.VMEM(weight.shape, bf16),
            pltpu.VMEM((channels, channels), f32),
            pltpu.VMEM((AHEAD + 1, min(TALL, length), channels), bf16),
            pltpu.VMEM((AHEAD + 1, min(TALL, length), channels), bf16),
            pltpu.VMEM((chunks, rows, LANES), bf16),
            pltpu.VMEM((2, 8, channels), f32),
            DMA((2,)),
            DMA((2,)),
            DMA((2,)),
            DMA((2,)),
            DMA,
            DMA,
            DMA((AHEAD + 1, 2)),
        ]
        + Exchange.scratch(channels)
        + (Reduction.scratch(chunks, rows) if joined else []),
        name="conv_one_spread",
        **joining(estimate, number),
    )(low, x, sums1, gain1, shift1, weight, s, parts)
    if not joined:
        grad = lax.psum(grad, ("dp", "seq"))
    return da, q, grad, grads1


def last_kernel(
    entries, taps, da, q, sums, grads1, gain, shift, one, small, grads2, grads3, out, one_out, two_out, three_out, *vectors
):
    center, inverse = center_inverse(sums[...], entries)
    both = grads1[...]
    scale = inverse * flat_row(gain)
    lean = inverse * (both[0:1] / entries)
    flat = flat_row(shift) * lean - scale * (both[1:2] / entries)
    for c in range(da.shape[2] // LANES):
        cols, at = lanes(c), lanes_of(c)
        s, l, f = 0.5 * scale[:, at], (1.0 / ROOT) * lean[:, at], flat[:, at]
        for r in range(0, da.shape[1], 128):
            rows = slice(r, r + 128)
            out[0, rows, cols] = da[0, rows, cols].astype(f32) * s - q[0, rows, cols].astype(f32) * l + f

    @pl.when(pl.program_id(0) < taps)
    def _():
        for c in range(one.shape[1]):
            one_out[0, :, lanes_of(c)] = one[0, c].astype(f32)

    @pl.when(pl.program_id(0) == 0)
    def _():
        kinds, rows, width = two_out.shape
        at = 0
        for k in range(kinds):
            for c in range(width // LANES):
                two_out[k, :, lanes_of(c)] = small[at : at + rows].astype(f32)
                at += rows
        rows = three_out.shape[0]
        for c in range(three_out.shape[1] // LANES):
            three_out[:, lanes_of(c)] = small[at : at + rows].astype(f32)
            at += rows
        for n, grads in enumerate((grads1, grads2, grads3)):
            vectors[2 * n][...] = grads[0]
            vectors[2 * n + 1][...] = grads[1]


def last(da, q, sums, gain, shift, one, small, two_shape, three_shape, grads, entries):
    windows, length, channels = da.shape
    slabs = channels // LANES
    tile = min(1024, windows * length // 8)
    per = length // tile
    taps = 5
    one = one.reshape(taps, slabs, channels, LANES)
    small = small.reshape(-1, LANES)
    rows = pl.BlockSpec((1, tile, channels), lambda i: (i // per, i % per, 0))
    flat = lambda i: (0, 0)
    vector = lambda v: pl.BlockSpec((v.shape[0],), lambda i: (0,))
    lengths = [g.shape[1] for g in grads for _ in range(2)]
    tap = lambda i: jnp.minimum(i, taps - 1)
    grads1, grads2, grads3 = grads
    return pl.pallas_call(
        functools.partial(last_kernel, entries, taps),
        grid=(windows * per,),
        out_shape=[
            jax.ShapeDtypeStruct(da.shape, f32),
            jax.ShapeDtypeStruct((taps, channels, channels), f32),
            jax.ShapeDtypeStruct(two_shape, f32),
            jax.ShapeDtypeStruct(three_shape, f32),
        ]
        + [jax.ShapeDtypeStruct((n,), f32) for n in lengths],
        in_specs=[rows, rows, pl.BlockSpec(sums.shape, flat), pl.BlockSpec(grads1.shape, flat), vector(gain), vector(shift)]
        + [pl.BlockSpec((1, slabs, channels, LANES), lambda i: (tap(i), 0, 0, 0)), pl.BlockSpec(small.shape, flat)]
        + [pl.BlockSpec(g.shape, flat) for g in grads[1:]],
        out_specs=[
            rows,
            pl.BlockSpec((1, channels, channels), lambda i: (tap(i), 0, 0)),
            pl.BlockSpec(two_shape, lambda i: (0, 0, 0)),
            pl.BlockSpec(three_shape, flat),
        ]
        + [pl.BlockSpec((n,), lambda i: (0,)) for n in lengths],
        name="last",
        **params(moved=8 * da.size + 6 * one.size),
    )(da, q, sums, grads1, gain, shift, one, small, grads2, grads3)


def on_device(
    inputs,
    conv_one,
    conv_two,
    conv_three,
    gain_one,
    shift_one,
    gain_two,
    shift_two,
    gain_three,
    shift_three,
    cotangent,
):
    windows, length, channels = inputs.shape
    entries = float(windows * length * lax.axis_size("dp") * lax.axis_size("seq"))
    half = entries / 2
    (pooled, pooled_low, s, first, narrow, hidden_two), (sums1, sums2, sums3), c_sides, p_sides, n_sides = conv_forward(
        inputs, cotangent, gain_one, shift_one, conv_one, gain_two, shift_two, conv_two, entries, 0
    )
    outputs, da3, stats, three_grad = conv_three_both(
        narrow, cotangent, pooled_low, sums3, gain_three, shift_three, conv_three, half
    )
    low, parts, small, grads3, grads2 = conv_two_back(
        da3, stats, narrow, n_sides, sums3, gain_three, pooled, p_sides, sums2, gain_two, shift_two, hidden_two, conv_two,
        cotangent, c_sides, s, first, three_grad, half, 2,
    )
    da1, q1, one_grad, grads1 = conv_one_spread(
        low, inputs, sums1, gain_one, shift_one, conv_one, s, parts, entries, 3
    )
    input_grad, *small_grads = last(
        da1, q1, sums1, gain_one, shift_one, one_grad, small, conv_two.shape, conv_three.shape,
        (grads1, grads2, grads3), entries,
    )
    return (outputs, input_grad, *small_grads)


def solution(mesh):
    rows = P("dp", "seq", None)
    in_specs = (rows,) + (P(),) * 9 + (rows,)
    out_specs = (rows, rows) + (P(),) * 9
    return jax.shard_map(on_device, mesh=mesh, in_specs=in_specs, out_specs=out_specs, check_vma=False)
```

```python
import functools

import jax
import jax.numpy as jnp
from jax import lax
from jax.experimental import pallas as pl
from jax.experimental.pallas import tpu as pltpu
from jax.sharding import PartitionSpec as P

epsilon = 1e-05
bf16 = jnp.bfloat16
f32 = jnp.float32
LANES = 128
UNIT = 64
SUB = 32
EDGE = 8
MESH = pl.DeviceIdType.MESH
LINEAR = 0.7978845608028654
CUBIC = 0.7978845608028654 * 0.044715
VMEM_LIMIT = 62 << 20
EARLY = 3
AHEAD = 2
TALL = 1024
SLOTS = 3
NN = (((1,), (0,)), ((), ()))
NT = (((1,), (1,)), ((), ()))
TN = (((0,), (0,)), ((), ()))


def dot(a, b, dims=NN):
    return lax.dot_general(a, b, dims, preferred_element_type=f32)


ROOT = CUBIC ** (1.0 / 3.0)
BEND = LINEAR / ROOT


def gelu_scaled(q):
    return q * (1.0 + jnp.tanh(q * (BEND + q * q)))


def slope_scaled(q):
    square = q * q
    th = jnp.tanh(q * (BEND + square))
    return (1.0 + th) * (1.0 + (1.0 - th) * (q * (BEND + 3.0 * square)))


def center_inverse(sums, entries):
    center = sums[0:1] / entries
    return center, lax.rsqrt(sums[1:2] / entries - center * center + epsilon)


def flat_row(v):
    return v[...].reshape(1, v.shape[0])


def lanes(c, width=LANES):
    if isinstance(c, int):
        return pl.ds(c * width, width)
    return pl.ds(pl.multiple_of(c * width, width), width)


def folded(values):
    return jnp.sum(values.reshape(values.shape[0] // 8, 8, values.shape[1]), axis=0)


def interleave(pieces, units):
    done = 0
    for k, piece in enumerate(pieces):
        piece()
        until = (k + 1) * len(units) // len(pieces)
        for unit in units[done:until]:
            unit()
        done = until


def place_flags():
    return lax.axis_index("seq") == 0, lax.axis_index("seq") == lax.axis_size("seq") - 1


class Walk:
    def __init__(self, windows, length, tile):
        self.tile = tile
        self.per = length // tile
        self.count = windows * self.per
        self.at_start, self.at_end = place_flags()

    def where(self, i):
        return i // self.per, i % self.per

    def hide_left(self, i):
        return jnp.logical_and(i % self.per == 0, self.at_start)

    def hide_right(self, i):
        return jnp.logical_and(i % self.per == self.per - 1, self.at_end)

    def rows(self, i, scale=1):
        span = self.tile * scale
        return pl.ds(pl.multiple_of((i % self.per) * span, span), span)

    def fetch(self, i, src, left, right, dst, sem, scale=1):
        w, p = self.where(i)
        span = self.tile * scale
        low = pl.multiple_of(p * span, span)
        first, last = p == 0, p == self.per - 1
        pltpu.make_async_copy(src.at[w, pl.ds(low, span)], dst.at[pl.ds(EDGE, span)], sem).start()
        head, tail = dst.at[pl.ds(0, EDGE)], dst.at[pl.ds(EDGE + span, EDGE)]

        @pl.when(first)
        def _():
            pltpu.make_async_copy(left.at[w], head, sem).start()

        @pl.when(jnp.logical_not(first))
        def _():
            pltpu.make_async_copy(src.at[w, pl.ds(pl.multiple_of(low - EDGE, EDGE), EDGE)], head, sem).start()

        @pl.when(last)
        def _():
            pltpu.make_async_copy(right.at[w], tail, sem).start()

        @pl.when(jnp.logical_not(last))
        def _():
            pltpu.make_async_copy(src.at[w, pl.ds(pl.multiple_of(low + span, EDGE), EDGE)], tail, sem).start()


def wait_for(dst, sem):
    pltpu.make_async_copy(dst, dst, sem).wait()


ANY = pl.BlockSpec(memory_space=pl.ANY)
VM = pl.BlockSpec(memory_space=pltpu.VMEM)
DMA = pltpu.SemaphoreType.DMA


def params(flops=0, moved=0, waved=0):
    return dict(
        compiler_params=pltpu.CompilerParams(vmem_limit_bytes=VMEM_LIMIT),
        cost_estimate=pl.CostEstimate(flops=flops, bytes_accessed=moved, transcendentals=waved),
    )


def greet(seqs, dps):
    seq, dp = lax.axis_index("seq"), lax.axis_index("dp")
    barrier = pltpu.get_barrier_semaphore()

    def near(d, _):
        pl.semaphore_signal(barrier, inc=1, device_id={"seq": lax.rem(seq + d, seqs)}, device_id_type=MESH)
        return 0

    def far(d, _):
        pl.semaphore_signal(barrier, inc=1, device_id={"dp": lax.rem(dp + d, dps)}, device_id_type=MESH)
        return 0

    lax.fori_loop(1, seqs, near, 0)
    lax.fori_loop(1, dps, far, 0)


def meet(seqs, dps):
    pl.semaphore_wait(pltpu.get_barrier_semaphore(), seqs - 1 + dps - 1)


class Exchange:
    SUMS = 7

    def __init__(self, refs, edge_refs=()):
        self.message, self.near, self.far, self.near_send, self.near_recv, self.far_send, self.far_recv = refs
        self.seqs, self.dps = self.near.shape[0], self.far.shape[0]
        self.seq, self.dp = lax.axis_index("seq"), lax.axis_index("dp")
        if edge_refs:
            self.lands, (self.edge_send, self.edge_recv) = edge_refs[:-2], edge_refs[-2:]

    @staticmethod
    def scratch(channels):
        seqs, dps = lax.axis_size("seq"), lax.axis_size("dp")
        rows = -(-2 * (channels // LANES) // 8) * 8
        return [
            pltpu.VMEM((rows, LANES), f32),
            pltpu.VMEM((seqs, rows, LANES), f32),
            pltpu.VMEM((dps, rows, LANES), f32),
            DMA((seqs,)),
            DMA((seqs,)),
            DMA((dps,)),
            DMA((dps,)),
        ]

    @staticmethod
    def edges(arrays):
        return [jax.ShapeDtypeStruct((a.shape[0], EDGE, a.shape[2]), a.dtype) for a in arrays for _ in range(2)]

    @staticmethod
    def edge_scratch(arrays):
        edges = Exchange.edges(arrays)
        return [pltpu.VMEM(e.shape, e.dtype) for e in edges] + [DMA((len(edges),)), DMA((len(edges),))]

    def edge_copy(self, n, src):
        length = src.shape[1]
        part = src.at[:, pl.ds(length - EDGE, EDGE)] if n % 2 == 0 else src.at[:, pl.ds(0, EDGE)]
        to = self.seq + 1 if n % 2 == 0 else self.seq - 1
        return pltpu.make_async_remote_copy(
            src_ref=part, dst_ref=self.lands[n], send_sem=self.edge_send.at[n], recv_sem=self.edge_recv.at[n],
            device_id={"seq": to}, device_id_type=MESH,
        )

    def start_edges(self, sources):
        for a, src in enumerate(sources):
            @pl.when(self.seq < self.seqs - 1)
            def _():
                self.edge_copy(2 * a, src).start()

            @pl.when(self.seq > 0)
            def _():
                self.edge_copy(2 * a + 1, src).start()

    def finish_edges(self, sources):
        for a, src in enumerate(sources):
            @pl.when(self.seq < self.seqs - 1)
            def _():
                self.edge_copy(2 * a, src).wait_send()
                self.edge_copy(2 * a + 1, src).wait_recv()

            @pl.when(self.seq > 0)
            def _():
                self.edge_copy(2 * a + 1, src).wait_send()
                self.edge_copy(2 * a, src).wait_recv()

    def near_copy(self, d):
        return pltpu.make_async_remote_copy(
            src_ref=self.message, dst_ref=self.near.at[self.seq], send_sem=self.near_send.at[d],
            recv_sem=self.near_recv.at[d], device_id={"seq": lax.rem(self.seq + d, self.seqs)}, device_id_type=MESH,
        )

    def far_copy(self, d):
        mine = self.far.at[self.dp]
        return pltpu.make_async_remote_copy(
            src_ref=mine, dst_ref=mine, send_sem=self.far_send.at[d], recv_sem=self.far_recv.at[d],
            device_id={"dp": lax.rem(self.dp + d, self.dps)}, device_id_type=MESH,
        )

    def each(self, count, run):
        def body(d, _):
            run(d)
            return 0

        lax.fori_loop(1, count, body, 0)

    def start_sums(self, stats):
        slabs = stats.shape[2] // LANES
        self.message[...] = jnp.zeros_like(self.message)
        for row in range(2):
            total = jnp.sum(stats[row], axis=0, keepdims=True)
            for c in range(slabs):
                self.message[row * slabs + c : row * slabs + c + 1] = total[:, lanes_of(c)]
        self.each(self.seqs, lambda d: self.near_copy(d).start())
        self.near[self.seq] = self.message[...]
        self.each(self.seqs, lambda d: self.near_copy(d).wait())
        self.far[self.dp] = lax.fori_loop(1, self.seqs, lambda n, t: t + self.near[n], self.near[0])
        self.each(self.dps, lambda d: self.far_copy(d).start())

    def finish_sums(self, sums):
        slabs = sums.shape[1] // LANES
        self.each(self.dps, lambda d: self.far_copy(d).wait())
        total = lax.fori_loop(1, self.dps, lambda n, t: t + self.far[n], self.far[0])
        sums[...] = jnp.zeros_like(sums)
        for row in range(2):
            for c in range(slabs):
                sums[row : row + 1, lanes_of(c)] = total[row * slabs + c : row * slabs + c + 1]


def lanes_of(c):
    return slice(c * LANES, (c + 1) * LANES)


def joining(estimate, number):
    return dict(
        estimate,
        compiler_params=pltpu.CompilerParams(
            vmem_limit_bytes=VMEM_LIMIT, collective_id=number, has_side_effects=True
        ),
    )


def conv_two_phase(
    tile, entries, v, left, right, sums, gain, shift, w_copy, w_ref, talk, narrow, h_out, sums3, n_left, n_right,
    vs, h_buf, lhs_a, lhs_b, outs, stats, v_sem, h_sem, o_sem,
):
    windows, length, channels = v.shape
    slabs = channels // LANES
    walk = Walk(windows, length, tile)
    tiles = walk.count
    lhs = (lhs_a, lhs_b)
    stats[...] = jnp.zeros_like(stats)

    def load(i):
        walk.fetch(i, v, left, right, vs.at[i % SLOTS], v_sem.at[i % SLOTS])

    def wait_load(i):
        wait_for(vs.at[i % SLOTS], v_sem.at[i % SLOTS])

    def h_copy(i, slot):
        w, _ = walk.where(i)
        return pltpu.make_async_copy(
            lhs[slot].at[:, pl.ds(channels, channels)], h_out.at[w, walk.rows(i)], h_sem.at[slot]
        )

    def o_copy(i, slot):
        w, _ = walk.where(i)
        return pltpu.make_async_copy(outs.at[slot], narrow.at[w, walk.rows(i)], o_sem.at[slot])

    def activate(i, slot, c):
        a, b = scale[:, lanes_of(c)], offset[:, lanes_of(c)]
        src, dst, cols = vs.at[i % SLOTS], lhs[slot], lanes(c)

        def ends():
            head = gelu_scaled(src[0:EDGE, cols] * a + b)
            h_buf[c, 0:EDGE] = jnp.where(walk.hide_left(i), 0.0, head)
            tail = gelu_scaled(src[EDGE + tile : 2 * EDGE + tile, cols] * a + b)
            h_buf[c, EDGE + tile : 2 * EDGE + tile] = jnp.where(walk.hide_right(i), 0.0, tail)

        def rows(r):
            def run():
                q = EDGE + r
                h_buf[c, q : q + UNIT] = gelu_scaled(src[q : q + UNIT, cols] * a + b)

            return run

        def taps(r):
            def run():
                for tap in range(3):
                    at = EDGE + r + 5 * (tap - 1)
                    dst[r : r + UNIT, lanes(tap * slabs + c)] = h_buf[c, at : at + UNIT].astype(bf16)

            return run

        units = [ends, rows(0)]
        for r in range(UNIT, tile, UNIT):
            units += [rows(r), taps(r - UNIT)]
        return units + [taps(tile - UNIT)]

    for i in range(min(SLOTS, tiles)):
        load(i)
    center, inverse = center_inverse(sums(), entries)
    scale = inverse * flat_row(gain)
    offset = ROOT * (flat_row(shift) - center * scale)
    scale = ROOT * scale
    wait_load(0)
    for c in range(slabs):
        for unit in activate(0, 0, c):
            unit()
    h_copy(0, 0).start()
    w_copy.wait()

    def pair(j, _):
        for slot in range(2):
            i = 2 * j + slot
            other = 1 - slot

            @pl.when(i + 1 < tiles)
            def _():
                wait_load(i + 1)

            @pl.when(jnp.logical_and(i >= 1, i + SLOTS - 1 < tiles))
            def _():
                load(i + SLOTS - 1)

            @pl.when(i >= 1)
            def _():
                h_copy(i - 1, other).wait()

            @pl.when(i >= 2)
            def _():
                o_copy(i - 2, slot).wait()

            held = []

            def piece(k):
                def run():
                    at = slice(k * channels, (k + 1) * channels)
                    part = dot(lhs[slot][:, at], w_ref[at])
                    held[:] = [held[0] + part] if held else [part]

                return run

            units = []
            for c in range(slabs):
                units += activate(i + 1, other, c)
            interleave([piece(k) for k in range(3)], units)
            total = (0.5 / ROOT) * held[0]
            outs[slot] = total
            stats[0] += folded(total)
            stats[1] += folded(total * total)
            o_copy(i, slot).start()

            @pl.when(i + 1 < tiles)
            def _():
                h_copy(i + 1, other).start()

        return 0

    lax.fori_loop(0, tiles // 2, pair, 0)
    h_copy(tiles - 1, 1).wait()
    o_copy(tiles - 2, 0).wait()
    o_copy(tiles - 1, 1).wait()
    talk.start_edges((narrow,))
    talk.start_sums(stats)
    talk.finish_edges((narrow,))
    n_left[...] = talk.lands[0][...]
    n_right[...] = talk.lands[1][...]
    talk.finish_sums(sums3)


def conv_one_kernel(
    tile, entries, x, cotangent, gain, shift, w_hbm, gain2, shift2, w2_hbm,
    pooled, pooled_low, s_out, first_out, narrow, h_out, sums1, sums2, sums3, c_left, c_right, p_left, p_right, n_left, n_right,
    xs, h_buf, lhs_a, lhs_b, outs, low_outs, coef, w_ref, stats, vs, v_buf, v_lhs_a, v_lhs_b, v_outs, w2_ref, stats3,
    x_sem, scan_sem, s_sem, f_sem, o_sem, q_sem, w_sem, v_sem, h_sem, n_sem, w2_sem, *talks,
):
    windows, length, channels = x.shape
    slabs = channels // LANES
    span = 2 * tile
    walk = Walk(windows, length // 2, tile)
    tiles = walk.count
    lhs = (lhs_a, lhs_b)
    n = Exchange.SUMS
    talk1 = Exchange(talks[:n], talks[3 * n : 3 * n + 6])
    talk2 = Exchange(talks[n : 2 * n], talks[3 * n + 6 : 3 * n + 10])
    talk3 = Exchange(talks[2 * n : 3 * n], talks[3 * n + 10 :])
    left, right = talk1.lands[:2]

    pieces = 4
    part = 2 * span // pieces

    def scan_copy(i):
        slot, w = i % pieces, i // (length // part)
        at = pl.ds(pl.multiple_of(i % (length // part) * part, 8), part)
        room = xs.at[slot // 2, pl.ds(pl.multiple_of(EDGE + slot % 2 * part, 8), part)]
        return pltpu.make_async_copy(x.at[w, at], room, scan_sem.at[slot])

    for i in range(pieces - 1):
        scan_copy(i).start()
    greet(talk1.seqs, talk1.dps)
    stats[...] = jnp.zeros_like(stats)

    def scan(i, _):
        slot = i % pieces
        scan_copy(i).wait()

        @pl.when(i + pieces - 1 < windows * length // part)
        def _():
            scan_copy(i + pieces - 1).start()

        def slab(c, _):
            cols = lanes(c)
            total = jnp.zeros((8, LANES), f32)
            squares = jnp.zeros((8, LANES), f32)
            for r in range(0, part, 128):
                at = pl.ds(pl.multiple_of(EDGE + slot % 2 * part + r, 8), 128)
                v = xs[slot // 2, at, cols]
                total += folded(v)
                squares += folded(v * v)
            stats[0, :, cols] += total
            stats[1, :, cols] += squares
            return 0

        lax.fori_loop(0, slabs, slab, 0)
        return 0

    lax.fori_loop(0, windows * length // part, scan, 0)
    meet(talk1.seqs, talk1.dps)
    talk1.start_edges((x, cotangent))
    talk1.start_sums(stats)
    w_copy = pltpu.make_async_copy(w_hbm, w_ref, w_sem)
    w2_copy = pltpu.make_async_copy(w2_hbm, w2_ref, w2_sem)

    def load(i, slot):
        walk.fetch(i, x, left, right, xs.at[slot], x_sem.at[slot], 2)

    def s_copy(i, slot, which):
        w, _ = walk.where(i)
        return pltpu.make_async_copy(
            lhs[slot].at[:, pl.ds((2 + which) * channels, channels)], s_out.at[which, w, walk.rows(i)],
            s_sem.at[slot, which],
        )

    def first_copy(i, slot):
        w, _ = walk.where(i)
        return pltpu.make_async_copy(
            lhs[slot].at[pl.ds(0, 16), pl.ds(channels, channels)], first_out.at[w], f_sem
        )

    def o_copies(i, slot):
        w, _ = walk.where(i)
        return (
            pltpu.make_async_copy(outs.at[slot], pooled.at[w, walk.rows(i)], o_sem.at[slot]),
            pltpu.make_async_copy(low_outs.at[slot], pooled_low.at[w, walk.rows(i)], q_sem.at[slot]),
        )

    def activate(i, slot, c):
        scale = coef[c, 0:1]
        offset = coef[c, 1:2]
        src = xs.at[slot]
        dst = lhs[slot]
        cols = lanes(c)

        def ends():
            head = gelu_scaled(src[0:EDGE, cols] * scale + offset)
            h_buf[c, 0:EDGE] = jnp.where(walk.hide_left(i), 0.0, head)
            tail = gelu_scaled(src[EDGE + span : 2 * EDGE + span, cols] * scale + offset)
            h_buf[c, EDGE + span : 2 * EDGE + span] = jnp.where(walk.hide_right(i), 0.0, tail)

        def rows(r):
            def run():
                for q in range(EDGE + r, EDGE + r + 2 * UNIT, 2 * SUB):
                    h_buf[c, q : q + 2 * SUB] = gelu_scaled(src[q : q + 2 * SUB, cols] * scale + offset)

            return run

        def taps(r):
            def run():
                for q in range(r, r + UNIT, SUB):
                    h = [h_buf[c, pl.ds(EDGE + 2 * q + d, SUB, stride=2)] for d in range(-2, 4)]
                    for tap in range(5):
                        at = pl.ds(pl.multiple_of(tap * channels + c * LANES, LANES), LANES)
                        dst[q : q + SUB, at] = (h[tap] + h[tap + 1]).astype(bf16)

            return run

        units = [ends, rows(0)]
        for r in range(UNIT, tile, UNIT):
            units += [rows(2 * r), taps(r - UNIT)]
        return units + [taps(tile - UNIT)]

    def matmul(slot, n):
        cols = lanes(n, 256)
        src = lhs[slot]
        held = []

        def piece(k):
            def run():
                at = slice(k * channels, (k + 1) * channels)
                part = dot(src[:, at], w_ref[at, cols])
                held[:] = [held[0] + part] if held else [part]

            return run

        def finish():
            total = (0.25 / ROOT) * held[0]
            outs[slot, :, cols] = total
            low_outs[slot, :, cols] = total.astype(bf16)
            stats[0, :, cols] += folded(total)
            stats[1, :, cols] += folded(total * total)

        return [piece(k) for k in range(5)], finish

    talk1.finish_edges((x, cotangent))
    c_left[...] = talk1.lands[2][...]
    c_right[...] = talk1.lands[3][...]
    load(0, 0)
    load(1, 1)
    w_copy.start()
    talk1.finish_sums(sums1)
    center, inverse = center_inverse(sums1[...], entries)
    scale = inverse * flat_row(gain)
    offset = flat_row(shift) - center * scale
    for c in range(slabs):
        coef[c, 0:1] = ROOT * scale[:, lanes_of(c)]
        coef[c, 1:2] = ROOT * offset[:, lanes_of(c)]
    stats[...] = jnp.zeros_like(stats)
    wait_for(xs.at[0], x_sem.at[0])

    def first_slab(c, _):
        for unit in activate(0, 0, c):
            unit()
        return 0

    lax.fori_loop(0, slabs, first_slab, 0)
    for which in range(2):
        s_copy(0, 0, which).start()
    first_copy(0, 0).start()
    w_copy.wait()

    def pair(j, _):
        for slot in range(2):
            i = 2 * j + slot
            other = 1 - slot

            @pl.when(i + 1 < tiles)
            def _():
                wait_for(xs.at[other], x_sem.at[other])

            @pl.when(i + 2 < tiles)
            def _():
                load(i + 2, slot)

            @pl.when(i >= 1)
            def _():
                for which in range(2):
                    s_copy(i - 1, other, which).wait()

                @pl.when((i - 1) % walk.per == 0)
                def _():
                    first_copy(i - 1, other).wait()

            @pl.when(i >= 2)
            def _():
                for copy in o_copies(i - 2, slot):
                    copy.wait()

            def part(n, _):
                pieces, finish = matmul(slot, n)
                units = []
                for c in range(2):
                    units += activate(i + 1, other, 2 * n + c)
                interleave(pieces, units)
                finish()
                return 0

            lax.fori_loop(0, channels // 256, part, 0)
            for copy in o_copies(i, slot):
                copy.start()

            @pl.when(i + 1 < tiles)
            def _():
                for which in range(2):
                    s_copy(i + 1, other, which).start()

                @pl.when((i + 1) % walk.per == 0)
                def _():
                    first_copy(i + 1, other).start()

        return 0

    lax.fori_loop(0, tiles // 2, pair, 0)
    for which in range(2):
        s_copy(tiles - 1, 1, which).wait()
    if walk.per == 1:
        first_copy(tiles - 1, 1).wait()
    for copy in o_copies(tiles - 2, 0) + o_copies(tiles - 1, 1):
        copy.wait()
    talk2.start_edges((pooled,))
    talk2.start_sums(stats)
    w2_copy.start()
    talk2.finish_edges((pooled,))
    p_left[...] = talk2.lands[0][...]
    p_right[...] = talk2.lands[1][...]

    def all_sums():
        talk2.finish_sums(sums2)
        return sums2[...]

    conv_two_phase(
        tile, entries / 2, pooled, talk2.lands[0], talk2.lands[1], all_sums, gain2, shift2, w2_copy, w2_ref, talk3,
        narrow, h_out, sums3, n_left, n_right, vs, v_buf, v_lhs_a, v_lhs_b, v_outs, stats3, v_sem, h_sem, n_sem,
    )


def conv_forward(x, cotangent, gain, shift, weight, gain2, shift2, weight2, entries, number):
    windows, length, channels = x.shape
    half = length // 2
    tile = min(512, half)
    slabs = channels // LANES
    width = weight2.shape[2]
    pooled = jax.ShapeDtypeStruct((windows, half, channels), f32)
    narrow = jax.ShapeDtypeStruct((windows, half, width), f32)
    edges = Exchange.edges([cotangent, pooled, narrow])
    got = pl.pallas_call(
        functools.partial(conv_one_kernel, tile, entries),
        out_shape=[
            pooled,
            jax.ShapeDtypeStruct(pooled.shape, bf16),
            jax.ShapeDtypeStruct((2, windows, half, channels), bf16),
            jax.ShapeDtypeStruct((windows, 16, channels), bf16),
            narrow,
            jax.ShapeDtypeStruct((windows, half, channels), bf16),
            jax.ShapeDtypeStruct((8, channels), f32),
            jax.ShapeDtypeStruct((8, channels), f32),
            jax.ShapeDtypeStruct((8, width), f32),
        ]
        + edges,
        in_specs=[ANY, ANY, VM, VM, ANY, VM, VM, ANY],
        out_specs=[ANY] * 6 + [VM] * 9,
        scratch_shapes=[
            pltpu.VMEM((2, 2 * tile + 2 * EDGE, channels), f32),
            pltpu.VMEM((slabs, 2 * tile + 2 * EDGE, LANES), f32),
            pltpu.VMEM((tile, 5 * channels), bf16),
            pltpu.VMEM((tile, 5 * channels), bf16),
            pltpu.VMEM((2, tile, channels), f32),
            pltpu.VMEM((2, tile, channels), bf16),
            pltpu.VMEM((slabs, 8, LANES), f32),
            pltpu.VMEM((5 * channels, channels), bf16),
            pltpu.VMEM((2, 8, channels), f32),
            pltpu.VMEM((SLOTS, tile + 2 * EDGE, channels), f32),
            pltpu.VMEM((slabs, tile + 2 * EDGE, LANES), f32),
            pltpu.VMEM((tile, 3 * channels), bf16),
            pltpu.VMEM((tile, 3 * channels), bf16),
            pltpu.VMEM((2, tile, width), f32),
            pltpu.VMEM((3 * channels, width), bf16),
            pltpu.VMEM((2, 8, width), f32),
            DMA((2,)),
            DMA((4,)),
            DMA((2, 2)),
            DMA,
            DMA((2,)),
            DMA((2,)),
            DMA,
            DMA((SLOTS,)),
            DMA((2,)),
            DMA((2,)),
            DMA,
        ]
        + Exchange.scratch(channels) * 2
        + Exchange.scratch(width)
        + Exchange.edge_scratch([x, cotangent])
        + Exchange.edge_scratch([pooled])
        + Exchange.edge_scratch([narrow]),
        name="conv_forward",
        **joining(params(13 * windows * half * channels * channels, 20 * x.size, 2 * x.size), number),
    )(
        x, cotangent, gain, shift, weight.reshape(5 * channels, channels), gain2, shift2,
        weight2.reshape(3 * channels, width),
    )
    return got[:6], got[6:9], got[9:11], got[11:13], got[13:15]


def conv_three_kernel(
    entries, narrow, cotangent, pooled, sums, gain, shift, w_ref, outputs, da, stats, w_grad,
    branch_a, branch_b, grad_a, grad_b, hidden, total, coef,
):
    tile, width = narrow.shape[1:]
    channels = cotangent.shape[2]
    step = pl.program_id(0)

    @pl.when(step == 0)
    def _():
        center, inverse = center_inverse(sums[...], entries)
        scale = inverse * flat_row(gain)
        offset = flat_row(shift) - center * scale
        coef[0:1] = ROOT * scale
        coef[1:2] = ROOT * offset
        stats[...] = jnp.zeros_like(stats)

    def turn(branch, grad, branch_old, grad_old):
        held = [[jnp.zeros((8, LANES), f32), jnp.zeros((8, LANES), f32)] for _ in range(width // LANES)]

        def back(n):
            def run():
                rows = slice(n * tile // 4, (n + 1) * tile // 4)
                branch[rows] = cotangent[0, rows].astype(bf16)
                if n % 2 == 1:
                    both = slice((n - 1) * tile // 4, (n + 1) * tile // 4)
                    grad[both] = dot(branch[both], w_ref[...], NT)

            return run

        def rows(r, c):
            def run():
                cols = lanes_of(c)
                q = narrow[0, r : r + UNIT, cols] * coef[0:1, cols] + coef[1:2, cols]
                square = q * q
                th = jnp.tanh(q * (BEND + square))
                up = 1.0 + th
                hidden[r : r + UNIT, cols] = (q * up).astype(bf16)
                back = up * (1.0 + (1.0 - th) * (q * (BEND + 3.0 * square))) * grad_old[r : r + UNIT, cols]
                da[0, r : r + UNIT, cols] = back
                held[c][0] = held[c][0] + folded(back * q)
                held[c][1] = held[c][1] + folded(back)

            return run

        def forward(n):
            def run():
                at = slice(n * tile // 2, (n + 1) * tile // 2)
                outputs[0, at] = pooled[0, at].astype(f32) + (0.5 / ROOT) * dot(hidden[at], w_ref[...])

            return run

        def weigh(n):
            def run():
                at = slice(n * tile // 2, (n + 1) * tile // 2)
                got = dot(hidden[at], branch_old[at], TN)
                total[...] = jnp.where(step <= 1, got, total[...] + got) if n == 0 else total[...] + got

            return run

        units = [rows(r, c) for r in range(0, tile, UNIT) for c in range(width // LANES)]
        half = len(units) // 2
        interleave([back(n) for n in range(4)], units[:half])
        interleave([forward(0), weigh(0)], units[half:])
        forward(1)()
        weigh(1)()
        for c in range(width // LANES):
            for n in range(2):
                stats[n, :, lanes_of(c)] += held[c][n]

    @pl.when(step % 2 == 0)
    def _():
        turn(branch_a, grad_a, branch_b, grad_b)

    @pl.when(step % 2 == 1)
    def _():
        turn(branch_b, grad_b, branch_a, grad_a)

    @pl.when(step == 0)
    def _():
        stats[...] = jnp.zeros_like(stats)

    @pl.when(step == pl.num_programs(0) - 1)
    def _():
        shifts = 0.5 * stats[1]
        stats[0] = (0.5 / ROOT * stats[0] - shifts * flat_row(shift)) / flat_row(gain)
        stats[1] = shifts
        for c in range(channels // LANES):
            w_grad[c] = ((0.5 / ROOT) * total[:, lanes_of(c)]).astype(bf16)


def conv_three_both(narrow, cotangent, pooled, sums, gain, shift, weight, entries):
    windows, length, width = narrow.shape
    channels = weight.shape[1]
    tile = min(512, length)
    per = length // tile
    tiles = windows * per
    ahead = lambda i: (jnp.minimum(i, tiles - 1) // per, jnp.minimum(i, tiles - 1) % per, 0)
    rows = lambda i: (jnp.maximum(i - 1, 0) // per, jnp.maximum(i - 1, 0) % per, 0)
    whole = lambda i: (0, 0)
    return pl.pallas_call(
        functools.partial(conv_three_kernel, entries),
        grid=(tiles + 1,),
        out_shape=(
            jax.ShapeDtypeStruct((windows, length, channels), f32),
            jax.ShapeDtypeStruct((windows, length, width), f32),
            jax.ShapeDtypeStruct((2, 8, width), f32),
            jax.ShapeDtypeStruct((channels // LANES, width, LANES), bf16),
        ),
        in_specs=[
            pl.BlockSpec((1, tile, width), rows),
            pl.BlockSpec((1, tile, channels), ahead),
            pl.BlockSpec((1, tile, channels), rows),
            pl.BlockSpec((8, width), whole),
            pl.BlockSpec((width,), lambda i: (0,)),
            pl.BlockSpec((width,), lambda i: (0,)),
            pl.BlockSpec((width, channels), whole),
        ],
        out_specs=(
            pl.BlockSpec((1, tile, channels), rows),
            pl.BlockSpec((1, tile, width), rows),
            pl.BlockSpec((2, 8, width), lambda i: (0, 0, 0)),
            pl.BlockSpec((channels // LANES, width, LANES), lambda i: (0, 0, 0)),
        ),
        scratch_shapes=[pltpu.VMEM((tile, channels), bf16)] * 2
        + [pltpu.VMEM((tile, width), f32)] * 2
        + [pltpu.VMEM((tile, width), bf16), pltpu.VMEM((width, channels), f32), pltpu.VMEM((8, width), f32)],
        name="conv_three_both",
        **params(6 * narrow.size * channels, 12 * cotangent.size, narrow.size),
    )(narrow, cotangent, pooled, sums, gain, shift, weight)


class Reduction:
    STAGES = 8

    def __init__(self, data, done, lands, send, recv, leave, lag, out):
        self.data, self.done, self.lands, self.send, self.recv = data, done, lands, send, recv
        self.chunks, self.rows = data.shape[0], data.shape[1]
        self.lag, self.leave, self.out = lag, leave, out
        self.steps = self.chunks + lag * self.STAGES
        self.planes = lax.axis_size("dp") // 4
        seq, dp = lax.axis_index("seq"), lax.axis_index("dp")
        self.seq, self.dp = seq, dp
        one, two = dp % 2, (dp // 2) % 2
        swap = seq == 1
        first_bit, second_bit = jnp.where(swap, two, one), jnp.where(swap, one, two)
        to_one, to_two = dp + 1 - 2 * one, dp + 2 - 4 * two
        first_peer, second_peer = jnp.where(swap, to_two, to_one), jnp.where(swap, to_one, to_two)
        self.peers = ({"seq": 1 - seq}, {"dp": first_peer}, {"dp": second_peer})
        self.plane = dp // 4
        rows = self.rows
        self.size = [rows // 2, rows // 4, rows // 8, rows // 8 // self.planes]
        self.base = [seq * self.size[0]]
        self.away = [(1 - seq) * self.size[0]]
        for bit, size in ((first_bit, self.size[1]), (second_bit, self.size[2])):
            self.away.append(self.base[-1] + (1 - bit) * size)
            self.base.append(self.base[-1] + bit * size)

    def part(self, ref, c, start, size):
        return ref.at[c, pl.ds(pl.multiple_of(start, 16), size)]

    def copy(self, c, number, src, dst, peer):
        return pltpu.make_async_remote_copy(
            src_ref=src, dst_ref=dst, send_sem=self.send.at[c, number], recv_sem=self.recv.at[c, number],
            device_id=peer, device_id_type=MESH,
        )

    def copies(self, c, stage):
        size, base = self.size, self.base
        if stage < 3:
            src = self.part(self.data, c, self.away[stage], size[stage])
            return [self.copy(c, stage, src, self.lands[stage].at[c], self.peers[stage])]
        if stage == 3 or stage == 4:
            out = []
            for d in range(1, self.planes):
                there = (self.plane + d) % self.planes
                peer = {"dp": self.dp + (there - self.plane) * 4}
                if stage == 3:
                    src = self.part(self.data, c, base[2] + there * size[3], size[3])
                    dst = self.lands[3].at[c, d - 1]
                else:
                    src = dst = self.part(self.done, c, base[2] + self.plane * size[3], size[3])
                out.append(self.copy(c, 3 + (stage - 3) * (self.planes - 1) + d - 1, src, dst, peer))
            return out
        level = 7 - stage
        mine = self.part(self.done, c, base[level], size[level])
        return [self.copy(c, 2 * (self.planes - 1) + stage - 2, mine, mine, self.peers[level])]

    def launch(self, c, stage):
        for copy in self.copies(c, stage):
            copy.start()

    def arrive(self, c, stage):
        for copy in self.copies(c, stage):
            copy.wait()
        size, base = self.size, self.base
        if stage < 3:
            unit = self.rows // 8

            def add(r, _):
                at = pl.ds(pl.multiple_of(base[stage] + r * unit, 16), unit)
                got = self.lands[stage][c, pl.ds(pl.multiple_of(r * unit, 16), unit)].astype(f32)
                self.data[c, at] = (self.data[c, at].astype(f32) + got).astype(bf16)
                return 0

            lax.fori_loop(0, size[stage] // unit, add, 0)
        elif stage == 3:
            at = pl.ds(pl.multiple_of(base[2] + self.plane * size[3], 16), size[3])
            total = self.data[c, at].astype(f32)
            for d in range(1, self.planes):
                total += self.lands[3][c, d - 1].astype(f32)
            self.done[c, at] = total.astype(bf16)

    def step(self, t):
        for stage in range(self.STAGES, -1, -1):
            c = t - self.lag * stage

            @pl.when(jnp.logical_and(c >= 0, c < self.chunks))
            def _():
                if stage > 0:
                    self.arrive(c, stage - 1)
                if stage < self.STAGES:
                    self.launch(c, stage)
                else:
                    self.out_copy(c).start()

    def out_copy(self, c):
        return pltpu.make_async_copy(self.done.at[c], self.out.at[c], self.leave.at[c])

    def drain(self):
        def one(c, _):
            self.out_copy(c).wait()
            return 0

        lax.fori_loop(0, self.chunks, one, 0)

    @staticmethod
    def fits(rows):
        dps = lax.axis_size("dp")
        return lax.axis_size("seq") == 2 and dps % 4 == 0 and dps > 4 and rows % (128 * (dps // 4)) == 0

    @staticmethod
    def scratch(chunks, rows):
        planes = lax.axis_size("dp") // 4
        copies = 2 * (planes - 1) + 6
        shapes = [(chunks, rows, LANES)] + [(chunks, rows >> (n + 1), LANES) for n in range(3)]
        shapes += [(chunks, planes - 1, rows // 8 // planes, LANES)]
        return [pltpu.VMEM(shape, bf16) for shape in shapes] + [
            DMA((chunks, copies)),
            DMA((chunks, copies)),
            DMA((chunks,)),
        ]

    @staticmethod
    def of(data, refs, lag, out):
        return Reduction(data, refs[0], refs[1:5], refs[5], refs[6], refs[7], lag, out)


def conv_two_back_kernel(
    tile, entries, joined, da, stats3, v, v_left, v_right, sums3, gain3, pooled, p_left, p_right, sums2, gain2, shift2,
    h, w_hbm, ct, ct_left, ct_right, s, first, three, da_out, low_out, w_grad, small, grads3, grads2,
    das, vs, hs, low_buf, low_a, low_b, total, w_ref, w_flip, stats, wide, wide_buf, wide_a, wide_b, ss, firsts, coef,
    taps, packed, data, a_sem, v_sem, p_sem, h_sem, o_sem, w_sem, r_sem, s_sem, f_sem, l_sem, g_sem, d_sem, t_sem, *refs,
):
    windows, length, width = da.shape
    channels = pooled.shape[2]
    thin, slabs = width // LANES, channels // LANES
    walk = Walk(windows, length, tile)
    tiles = walk.count
    low = (low_a, low_b)
    center, inverse = center_inverse(sums2[...], entries)
    scale = inverse * flat_row(gain2)
    offset = ROOT * (flat_row(shift2) - center * scale)
    scale = ROOT * scale
    stats[...] = jnp.zeros_like(stats)
    total[...] = jnp.zeros_like(total)

    def load(i):
        slot = i % SLOTS
        walk.fetch(i, da, talk3.lands[0], talk3.lands[1], das.at[slot], a_sem.at[slot])
        walk.fetch(i, v, v_left, v_right, vs.at[slot], v_sem.at[slot])

    def wait_load(i):
        slot = i % SLOTS
        wait_for(das.at[slot], a_sem.at[slot])
        wait_for(vs.at[slot], v_sem.at[slot])

    def h_copy(i):
        w, _ = walk.where(i)
        return pltpu.make_async_copy(h.at[w, walk.rows(i)], hs.at[i % SLOTS], h_sem.at[i % SLOTS])

    def p_copy(i):
        w, _ = walk.where(i)
        return pltpu.make_async_copy(
            pooled.at[w, walk.rows(i)], wide.at[i % SLOTS, 0, pl.ds(0, tile)], p_sem.at[i % SLOTS]
        )

    def o_copy(i, slot):
        w, _ = walk.where(i)
        return pltpu.make_async_copy(wide.at[slot, 1, pl.ds(0, tile)], da_out.at[w, walk.rows(i)], o_sem.at[slot])

    def lower(i, slot, c):
        at, cols = lanes_of(c), lanes(c)
        m, s, l, f = center3[:, at], scale3[:, at], lean[:, at], flat[:, at]
        dst = low[slot]

        def value(q, size):
            at = i % SLOTS
            return das[at, q : q + size, cols] * (0.5 * s) - (vs[at, q : q + size, cols] - m) * l - f

        def ends():
            low_buf[c, 0:EDGE] = jnp.where(walk.hide_left(i), 0.0, value(0, EDGE))
            low_buf[c, EDGE + tile : 2 * EDGE + tile] = jnp.where(walk.hide_right(i), 0.0, value(EDGE + tile, EDGE))

        def rows(r):
            def run():
                low_buf[c, EDGE + r : EDGE + r + UNIT] = value(EDGE + r, UNIT)

            return run

        def taps(r):
            def run():
                for tap in range(3):
                    q = EDGE + r - 5 * (tap - 1)
                    dst[r : r + UNIT, lanes(tap * thin + c)] = low_buf[c, q : q + UNIT].astype(bf16)

            return run

        units = [ends, rows(0)]
        for r in range(UNIT, tile, UNIT):
            units += [rows(r), taps(r - UNIT)]
        return units + [taps(tile - UNIT)]

    def finish(i, slot, c):
        at, cols = lanes_of(c), lanes(c)
        a, b = scale[:, at], offset[:, at]
        sums = [jnp.zeros((8, LANES), f32), jnp.zeros((8, LANES), f32)]

        def rows(r):
            def run():
                q = wide[i % SLOTS, 0, r : r + UNIT, cols] * a + b
                back = slope_scaled(q) * wide[slot, 2, r : r + UNIT, cols]
                wide[slot, 1, r : r + UNIT, cols] = back
                sums[0] = sums[0] + folded(back * q)
                sums[1] = sums[1] + folded(back)

            return run

        def close():
            stats[0, :, cols] += sums[0]
            stats[1, :, cols] += sums[1]

        return [rows(r) for r in range(0, tile, UNIT)] + [close]

    n = Exchange.SUMS
    talk3 = Exchange(refs[:n], refs[2 * n : 2 * n + 4])
    talk2 = Exchange(refs[n : 2 * n], refs[2 * n + 4 : 2 * n + 8])
    greet(talk3.seqs, talk3.dps)
    w_copy = pltpu.make_async_copy(w_hbm, w_ref, w_sem)
    w_copy.start()
    f_copy = pltpu.make_async_copy(first, firsts, f_sem)
    f_copy.start()
    size = three.shape[1]

    def three_copy(c):
        chunk, start = divmod(3 * thin * channels + c * size, data.shape[1])
        return pltpu.make_async_copy(three.at[c], data.at[chunk, pl.ds(start, size)], t_sem.at[c])

    for c in range(slabs):
        three_copy(c).start()
    for i in range(min(SLOTS, tiles)):
        h_copy(i).start()
    meet(talk3.seqs, talk3.dps)
    talk3.start_edges((da,))
    talk3.start_sums(stats3)
    w_copy.wait()
    for k in range(3):
        w_flip[k * width : (k + 1) * width] = w_ref[k].T
    talk3.finish_edges((da,))
    for i in range(min(SLOTS, tiles)):
        load(i)
    talk3.finish_sums(grads3)
    center3, inverse3 = center_inverse(sums3[...], entries)
    sums = grads3[...]
    scale3 = inverse3 * flat_row(gain3)
    lean = scale3 * inverse3 * (sums[0:1] / entries)
    flat = scale3 * (sums[1:2] / entries)

    def low_tile(i, slot):
        for c in range(thin):
            for unit in lower(i, slot, c):
                unit()

    def weigh_pair(j, _):
        for slot in range(2):
            i = 2 * j + slot
            other = 1 - slot

            @pl.when(i + 1 < tiles)
            def _():
                wait_load(i + 1)

            @pl.when(jnp.logical_and(i >= 1, i + SLOTS - 1 < tiles))
            def _():
                load(i + SLOTS - 1)
                h_copy(i + SLOTS - 1).start()

            h_copy(i).wait()

            def weigh(n):
                def run():
                    at = slice(n * 256, (n + 1) * 256)
                    total[at] += dot(hs[i % SLOTS, :, at], low[slot][...], TN)

                return run

            units = []
            for c in range(thin):
                units += lower(i + 1, other, c)
            interleave([weigh(n) for n in range(channels // 256)], units)
        return 0

    wait_load(0)
    low_tile(0, 0)
    lax.fori_loop(0, tiles // 2, weigh_pair, 0)
    for i in range(min(SLOTS, tiles)):
        load(i)
    for c in range(3 * thin):
        chunk, start = divmod(c * channels, data.shape[1])
        data[chunk, start : start + channels] = ((0.5 / ROOT) * total[:, lanes_of(c)]).astype(bf16)
    for c in range(slabs):
        three_copy(c).wait()
    if joined:
        sharing = Reduction.of(data, refs[2 * n + 8 :], 4, small)

    def back_turn(i, slot, last):
        other = 1 - slot
        if not last:
            @pl.when(i + 1 < tiles)
            def _():
                wait_load(i + 1)

            @pl.when(jnp.logical_and(i >= 1, i + SLOTS - 1 < tiles))
            def _():
                load(i + SLOTS - 1)

            @pl.when(jnp.logical_and(i >= 1, i + 1 < tiles))
            def _():
                p_copy(i + 1).start()

        @pl.when(i >= 1)
        def _():
            p_copy(i - 1).wait()

        @pl.when(i >= 3)
        def _():
            o_copy(i - 3, other).wait()

        def back(n):
            def run():
                cols = lanes(n, 256)
                wide[slot, 2, 0:tile, cols] = dot(low[slot][...], w_flip[:, cols])

            return run

        units = []
        for c in range(slabs):
            units += finish(i + SLOTS - 1, other, c)
        if last:
            for unit in units:
                unit()
        else:
            for c in range(thin):
                units += lower(i + 1, other, c)
            interleave([back(n) for n in range(channels // 256)], units)

        @pl.when(i >= 1)
        def _():
            o_copy(i - 1, other).start()

        @pl.when(i == 0)
        def _():
            stats[...] = jnp.zeros_like(stats)

    def back_pair(j, _):
        for slot in range(2):
            back_turn(2 * j + slot, slot, False)
            if joined:
                sharing.step(2 * (2 * j + slot))
                sharing.step(2 * (2 * j + slot) + 1)
        return 0

    for i in range(2):
        p_copy(i).start()
    wait_load(0)
    low_tile(0, 0)
    lax.fori_loop(0, tiles // 2, back_pair, 0)
    back_turn(tiles, 0, True)
    shifts = 0.5 * stats[1]
    stats[0] = (0.5 / ROOT * stats[0] - shifts * flat_row(shift2)) / flat_row(gain2)
    stats[1] = shifts
    o_copy(tiles - 2, 0).wait()
    o_copy(tiles - 1, 1).wait()
    talk2.start_edges((da_out,))
    talk2.start_sums(stats)
    taps[...] = jnp.zeros_like(taps)
    talk2.finish_edges((da_out,))
    lefts, rights = (talk2.lands[0], p_left, ct_left), (talk2.lands[1], p_right, ct_right)

    def wide_load(i):
        slot = i % SLOTS
        for n, src in enumerate((da_out, pooled, ct)):
            walk.fetch(i, src, lefts[n], rights[n], wide.at[slot, n], r_sem.at[slot])

    for i in range(min(SLOTS - 1, tiles)):
        wide_load(i)
    f_copy.wait()
    talk2.finish_sums(grads2)
    sums = grads2[...]
    scale2 = 0.5 * inverse * flat_row(gain2)
    lean2 = scale2 * inverse * (sums[0:1] / entries)
    flat2 = scale2 * (sums[1:2] / entries)
    for c in range(slabs):
        for row, values in enumerate((0.5 * scale2, lean2, center * lean2 - flat2)):
            coef[c, row : row + 1] = values[:, lanes_of(c)]
    wides = (wide_a, wide_b)

    def s_copy(i, slot):
        w, _ = walk.where(i)
        return pltpu.make_async_copy(s.at[:, w, walk.rows(i)], ss.at[slot], s_sem.at[slot])

    def l_copy(i, slot):
        w, _ = walk.where(i)
        return pltpu.make_async_copy(wides[slot], low_out.at[w, walk.rows(i)], l_sem.at[slot])

    def shift_slab(i, slot, c):
        cols = lanes(c)
        sc, l, f = coef[c, 0:1], coef[c, 1:2], coef[c, 2:3]
        dst = wides[slot]

        def value(q, size):
            a, p, g = (wide[i % SLOTS, n, q : q + size, cols] for n in range(3))
            return 0.5 * g + a * sc - p * l + f

        def ends():
            wide_buf[c, 0:EDGE] = jnp.where(walk.hide_left(i), 0.0, value(0, EDGE))
            wide_buf[c, EDGE + tile : 2 * EDGE + tile] = jnp.where(walk.hide_right(i), 0.0, value(EDGE + tile, EDGE))

        def rows(r):
            def run():
                wide_buf[c, EDGE + r : EDGE + r + UNIT] = value(EDGE + r, UNIT)

            return run

        def shifts(r):
            def run():
                for tap in range(3):
                    q = EDGE + r + 1 - tap
                    at = pl.ds(pl.multiple_of(tap * channels + c * LANES, LANES), LANES)
                    dst[r : r + UNIT, at] = wide_buf[c, q : q + UNIT].astype(bf16)

            return run

        units = [ends, rows(0)]
        for r in range(UNIT, tile, UNIT):
            units += [rows(r), shifts(r - UNIT)]
        return units + [shifts(tile - UNIT)]

    s_copy(0, 0).start()
    wait_for(wide.at[0], r_sem.at[0])

    def first_slab(c, _):
        for unit in shift_slab(0, 0, c):
            unit()
        return 0

    lax.fori_loop(0, slabs, first_slab, 0)
    l_copy(0, 0).start()

    def wide_pair(j, _):
        for slot in range(2):
            i = 2 * j + slot
            other = 1 - slot
            w, p = walk.where(i)

            @pl.when(jnp.logical_and(p == 0, walk.at_start))
            def _():
                row = lax.broadcasted_iota(jnp.int32, (16, channels), 0)
                here = jnp.where(row == 0, firsts[w].astype(f32), 0.0).astype(bf16)
                taps[1] += dot(here, wides[slot][0:16, channels : 2 * channels], TN)

            @pl.when(i + 1 < tiles)
            def _():
                wait_for(wide.at[(i + 1) % SLOTS], r_sem.at[(i + 1) % SLOTS])
                s_copy(i + 1, other).start()

            @pl.when(i + SLOTS - 1 < tiles)
            def _():
                wide_load(i + SLOTS - 1)

            @pl.when(i >= 1)
            def _():
                l_copy(i - 1, other).wait()

            s_copy(i, slot).wait()

            def part(n, _):
                cols = lanes(n, 256)

                def weigh(k):
                    def run():
                        at = pl.ds(pl.multiple_of((k // 2) * channels + n * 256, 256), 256)
                        taps[k, :, cols] += dot(ss[slot, k % 2], wides[slot][:, at], TN)

                    return run

                units = shift_slab(i + 1, other, 2 * n) + shift_slab(i + 1, other, 2 * n + 1)
                interleave([weigh(k) for k in range(EARLY)], units)
                if joined:
                    sharing.step(2 * tiles + i * (channels // 256) + n)
                return 0

            lax.fori_loop(0, channels // 256, part, 0)

            @pl.when(i + 1 < tiles)
            def _():
                l_copy(i + 1, other).start()

        return 0

    lax.fori_loop(0, tiles // 2, wide_pair, 0)
    l_copy(tiles - 1, 1).wait()
    g_copies = [pltpu.make_async_copy(packed.at[k], w_grad.at[k], g_sem.at[k]) for k in range(EARLY)]
    for k in range(EARLY):
        for c in range(slabs):
            packed[k, c] = ((0.5 / ROOT) * taps[k, :, lanes_of(c)]).astype(bf16)
        g_copies[k].start()
    if joined:
        def more(t, _):
            sharing.step(t)
            return 0

        lax.fori_loop(2 * tiles + tiles * (channels // 256), sharing.steps, more, 0)
        sharing.drain()
    else:
        d_copy = pltpu.make_async_copy(data, small, d_sem)
        d_copy.start()
        d_copy.wait()
    for copy in g_copies:
        copy.wait()


def conv_two_back(
    da, stats3, v, v_sides, sums3, gain3, pooled, p_sides, sums2, gain2, shift2, h, weight, ct, ct_sides, s, first, three,
    entries, number,
):
    windows, length, width = da.shape
    channels = pooled.shape[2]
    tile = min(512, length)
    thin, slabs = width // LANES, channels // LANES
    back = jax.ShapeDtypeStruct((windows, length, channels), f32)
    packed = (EARLY, slabs, channels, LANES)
    rows = 2 * channels
    chunks = (3 * channels * width + width * channels) // (rows * LANES)
    joined = Reduction.fits(rows)
    got = pl.pallas_call(
        functools.partial(conv_two_back_kernel, tile, entries, joined),
        out_shape=[
            back,
            jax.ShapeDtypeStruct((windows, length, 3 * channels), bf16),
            jax.ShapeDtypeStruct(packed, bf16),
            jax.ShapeDtypeStruct((chunks, rows, LANES), bf16),
            jax.ShapeDtypeStruct((8, width), f32),
            jax.ShapeDtypeStruct((8, channels), f32),
        ],
        in_specs=[ANY, VM] + [ANY] * 3 + [VM] * 2 + [ANY] * 3 + [VM] * 3 + [ANY] * 8,
        out_specs=[ANY] * 4 + [VM] * 2,
        scratch_shapes=[
            pltpu.VMEM((SLOTS, tile + 2 * EDGE, width), f32),
            pltpu.VMEM((SLOTS, tile + 2 * EDGE, width), f32),
            pltpu.VMEM((SLOTS, tile, channels), bf16),
            pltpu.VMEM((thin, tile + 2 * EDGE, LANES), f32),
            pltpu.VMEM((tile, 3 * width), bf16),
            pltpu.VMEM((tile, 3 * width), bf16),
            pltpu.VMEM((channels, 3 * width), f32),
            pltpu.VMEM(weight.shape, bf16),
            pltpu.VMEM((3 * width, channels), bf16),
            pltpu.VMEM((2, 8, channels), f32),
            pltpu.VMEM((SLOTS, 3, tile + 2 * EDGE, channels), f32),
            pltpu.VMEM((slabs, tile + 2 * EDGE, LANES), f32),
            pltpu.VMEM((tile, 3 * channels), bf16),
            pltpu.VMEM((tile, 3 * channels), bf16),
            pltpu.VMEM((2, 2, tile, channels), bf16),
            pltpu.VMEM(first.shape, bf16),
            pltpu.VMEM((slabs, 8, LANES), f32),
            pltpu.VMEM((EARLY, channels, channels), f32),
            pltpu.VMEM(packed, bf16),
            pltpu.VMEM((chunks, rows, LANES), bf16),
        ]
        + [DMA((SLOTS,))] * 4
        + [DMA((2,))]
        + [DMA, DMA((SLOTS,)), DMA((2,)), DMA, DMA((2,)), DMA((EARLY,)), DMA, DMA((slabs,))]
        + Exchange.scratch(width)
        + Exchange.scratch(channels)
        + Exchange.edge_scratch([da])
        + Exchange.edge_scratch([back])
        + (Reduction.scratch(chunks, rows) if joined else []),
        name="conv_two_back",
        **joining(params(20 * pooled.size * channels, 40 * pooled.size, pooled.size), number),
    )(
        da, stats3, v, *v_sides, sums3, gain3, pooled, *p_sides, sums2, gain2, shift2, h, weight, ct, *ct_sides, s, first,
        three,
    )
    low, parts, small = got[1:4]
    if not joined:
        small = lax.psum(small, ("dp", "seq"))
    return low, parts, small, got[4], got[5]


def conv_one_spread_kernel(
    tile, entries, joined, low, x, sums1, gain1, shift1, w_hbm, s, parts, da_out, q_out, w_grad, grads1,
    lows, xs, g_buf, outs, q_buf, coef, w_ref, total, ss, ls, data, stats, l_sem, x_sem, o_sem, q_sem, w_sem, d_sem, t_sem, *refs,
):
    windows, length, _ = low.shape
    channels = x.shape[2]
    slabs = channels // LANES
    span = 2 * tile
    walk = Walk(windows, length, tile)
    tiles = walk.count
    tall = Walk(windows, length, min(TALL, length))
    center, inverse = center_inverse(sums1[...], entries)
    scale = inverse * flat_row(gain1)
    offset = flat_row(shift1) - center * scale
    for c in range(slabs):
        for row, values in enumerate((ROOT * scale, ROOT * offset)):
            coef[c, row : row + 1] = values[:, lanes_of(c)]
    stats[...] = jnp.zeros_like(stats)

    def l_copy(i, slot):
        w, _ = walk.where(i)
        return pltpu.make_async_copy(low.at[w, walk.rows(i)], lows.at[slot], l_sem.at[slot])

    def x_copy(i, slot):
        w, _ = walk.where(i)
        return pltpu.make_async_copy(x.at[w, walk.rows(i, 2)], xs.at[slot], x_sem.at[slot])

    def o_copies(i, slot):
        w, _ = walk.where(i)
        return (
            pltpu.make_async_copy(outs.at[slot], da_out.at[w, walk.rows(i, 2)], o_sem.at[slot]),
            pltpu.make_async_copy(q_buf.at[slot], q_out.at[w, walk.rows(i, 2)], q_sem.at[slot]),
        )

    def t_copies(g, slot):
        k = EARLY + g // tall.count
        w, _ = tall.where(g % tall.count)
        rows = tall.rows(g % tall.count)
        at = pl.ds(pl.multiple_of((k // 2) * channels, channels), channels)
        return (
            pltpu.make_async_copy(s.at[k % 2, w, rows], ss.at[slot], t_sem.at[slot, 0]),
            pltpu.make_async_copy(low.at[w, rows, at], ls.at[slot], t_sem.at[slot, 1]),
        )

    d_copy = pltpu.make_async_copy(parts, data.at[pl.ds(0, EARLY * slabs // 2)], d_sem)
    d_copy.start()
    for g in range(AHEAD):
        for copy in t_copies(g, g):
            copy.start()
    talk, reduction = Exchange(refs[: Exchange.SUMS]), refs[Exchange.SUMS :]
    greet(talk.seqs, talk.dps)
    l_copy(0, 0).start()
    w_copy = pltpu.make_async_copy(w_hbm, w_ref, w_sem)
    w_copy.start()
    if joined:
        sharing = Reduction.of(data, reduction, 3, w_grad)

    late = (5 - EARLY) * tall.count
    triple = slabs // 2

    def due(g):
        whole, part = g // tall.count, g % tall.count
        first = jnp.where(whole == 0, 0, (EARLY + whole - 1) * triple)
        count = jnp.where(whole == 0, EARLY * triple, triple)
        return first + count * part // tall.count, first + count * (part + 1) // tall.count

    def weigh(g, _):
        slot = g % (AHEAD + 1)
        for copy in t_copies(g, slot):
            copy.wait()

        @pl.when(g + AHEAD < late)
        def _():
            for copy in t_copies(g + AHEAD, (g + AHEAD) % (AHEAD + 1)):
                copy.start()

        @pl.when(g % tall.count == 0)
        def _():
            total[...] = dot(ss[slot], ls[slot], TN)

        @pl.when(g % tall.count > 0)
        def _():
            total[...] += dot(ss[slot], ls[slot], TN)

        @pl.when(g % tall.count == tall.count - 1)
        def _():
            for c in range(slabs):
                at = slice((c % 2) * channels, (c % 2 + 1) * channels)
                data[(EARLY + g // tall.count) * triple + c // 2, at] = ((0.5 / ROOT) * total[:, lanes_of(c)]).astype(bf16)

        @pl.when(g == 0)
        def _():
            d_copy.wait()
            meet(talk.seqs, talk.dps)

        if joined:
            def take(t, _):
                sharing.step(t)
                return 0

            lax.fori_loop(*due(g), take, 0)

        return 0

    lax.fori_loop(0, late, weigh, 0)
    w_copy.wait()

    def finish(slot, c):
        cols = lanes(c)
        a, b = coef[c, 0:1], coef[c, 1:2]
        held = [jnp.zeros((8, LANES), f32), jnp.zeros((8, LANES), f32)]

        def rows(r):
            def run():
                q = xs[slot, r : r + UNIT, cols] * a + b
                incoming = g_buf[slot, c, EDGE + r : EDGE + r + UNIT] + g_buf[slot, c, EDGE + r - 1 : EDGE + r - 1 + UNIT]
                back = slope_scaled(q) * incoming
                outs[slot, r : r + UNIT, cols] = back.astype(bf16)
                q_buf[slot, r : r + UNIT, cols] = q.astype(bf16)
                held[0] = held[0] + folded(back * q)
                held[1] = held[1] + folded(back)

            return run

        def close():
            stats[0, :, cols] += held[0]
            stats[1, :, cols] += held[1]

        return [rows(r) for r in range(0, span, UNIT)] + [close]

    def settle():
        shifts = 0.5 * stats[1]
        stats[0] = (0.5 / ROOT * stats[0] - shifts * flat_row(shift1)) / flat_row(gain1)
        stats[1] = shifts

    def spread(slot, n):
        at = lanes(n, 256)

        def even():
            part = dot(lows[slot, :, 0:channels], w_ref[0, at], NT)
            part += dot(lows[slot, :, channels : 2 * channels], w_ref[2, at], NT)
            part += dot(lows[slot, :, 2 * channels : 3 * channels], w_ref[4, at], NT)
            for c in range(2):
                g_buf[slot, 2 * n + c, pl.ds(EDGE, tile, stride=2)] = part[:, lanes_of(c)]

        def odd():
            part = dot(lows[slot, :, 0:channels], w_ref[1, at], NT)
            part += dot(lows[slot, :, channels : 2 * channels], w_ref[3, at], NT)
            for c in range(2):
                g_buf[slot, 2 * n + c, pl.ds(EDGE + 1, tile, stride=2)] = part[:, lanes_of(c)]

        return [even, odd]

    def turn(i, slot, last):
        other = 1 - slot
        w, p = walk.where(i)
        if not last:
            l_copy(i, slot).wait()

            @pl.when(i + 1 < tiles)
            def _():
                l_copy(i + 1, other).start()

            @pl.when(p == 0)
            def _():
                edge = lows[slot, 0:16]
                part = dot(edge[:, channels : 2 * channels], w_ref[1], NT) + dot(edge[:, 2 * channels :], w_ref[3], NT)
                for c in range(slabs):
                    g_buf[slot, c, EDGE - 1 : EDGE] = part[0:1, lanes_of(c)]

            @pl.when(p > 0)
            def _():
                for c in range(slabs):
                    g_buf[slot, c, EDGE - 1 : EDGE] = g_buf[other, c, EDGE + span - 1 : EDGE + span]

        @pl.when(i >= 1)
        def _():
            x_copy(i - 1, other).wait()

        @pl.when(i >= 3)
        def _():
            for copy in o_copies(i - 3, other):
                copy.wait()

        if not last:
            x_copy(i, slot).start()

        def part(n, _):
            units = finish(other, 2 * n) + finish(other, 2 * n + 1)
            interleave([] if last else spread(slot, n), units)
            if last:
                for unit in units:
                    unit()
            elif joined:
                sharing.step(4 * triple + i * (channels // 256) + n)
            return 0

        lax.fori_loop(0, channels // 256, part, 0)

        @pl.when(i >= 1)
        def _():
            for copy in o_copies(i - 1, other):
                copy.start()

        @pl.when(i == 0)
        def _():
            stats[...] = jnp.zeros_like(stats)


    def pair(j, _):
        for slot in range(2):
            turn(2 * j + slot, slot, False)
        return 0

    lax.fori_loop(0, tiles // 2, pair, 0)
    turn(tiles, 0, True)
    settle()
    talk.start_sums(stats)
    for copy in o_copies(tiles - 2, 0) + o_copies(tiles - 1, 1):
        copy.wait()
    if joined:
        def more(t, _):
            sharing.step(t)
            return 0

        lax.fori_loop(4 * triple + tiles * (channels // 256), sharing.steps, more, 0)
    talk.finish_sums(grads1)
    if joined:
        sharing.drain()
    else:
        d_copy = pltpu.make_async_copy(data, w_grad, d_sem)
        d_copy.start()
        d_copy.wait()


def conv_one_spread(low, x, sums1, gain1, shift1, weight, s, parts, entries, number):
    windows, length, _ = low.shape
    channels = x.shape[2]
    tile = min(512, length)
    slabs = channels // LANES
    rows, chunks = 2 * channels, 5 * slabs // 2
    parts = parts.reshape(EARLY * slabs // 2, rows, LANES)
    joined = Reduction.fits(rows)
    estimate = params(10 * low.size * channels // 3, 12 * x.size, x.size)
    da, q, grad, grads1 = pl.pallas_call(
        functools.partial(conv_one_spread_kernel, tile, entries, joined),
        out_shape=(
            jax.ShapeDtypeStruct((windows, 2 * length, channels), bf16),
            jax.ShapeDtypeStruct((windows, 2 * length, channels), bf16),
            jax.ShapeDtypeStruct((chunks, rows, LANES), bf16),
            jax.ShapeDtypeStruct((8, channels), f32),
        ),
        in_specs=[ANY] * 2 + [VM] * 3 + [ANY] * 3,
        out_specs=(ANY, ANY, ANY, VM),
        scratch_shapes=[
            pltpu.VMEM((2, tile, 3 * channels), bf16),
            pltpu.VMEM((2, 2 * tile, channels), f32),
            pltpu.VMEM((2, slabs, 2 * tile + 2 * EDGE, LANES), f32),
            pltpu.VMEM((2, 2 * tile, channels), bf16),
            pltpu.VMEM((2, 2 * tile, channels), bf16),
            pltpu.VMEM((slabs, 8, LANES), f32),
            pltpu.VMEM(weight.shape, bf16),
            pltpu.VMEM((channels, channels), f32),
            pltpu.VMEM((AHEAD + 1, min(TALL, length), channels), bf16),
            pltpu.VMEM((AHEAD + 1, min(TALL, length), channels), bf16),
            pltpu.VMEM((chunks, rows, LANES), bf16),
            pltpu.VMEM((2, 8, channels), f32),
            DMA((2,)),
            DMA((2,)),
            DMA((2,)),
            DMA((2,)),
            DMA,
            DMA,
            DMA((AHEAD + 1, 2)),
        ]
        + Exchange.scratch(channels)
        + (Reduction.scratch(chunks, rows) if joined else []),
        name="conv_one_spread",
        **joining(estimate, number),
    )(low, x, sums1, gain1, shift1, weight, s, parts)
    if not joined:
        grad = lax.psum(grad, ("dp", "seq"))
    return da, q, grad, grads1


def last_kernel(
    entries, taps, da, q, sums, grads1, gain, shift, one, small, grads2, grads3, out, one_out, two_out, three_out, *vectors
):
    center, inverse = center_inverse(sums[...], entries)
    both = grads1[...]
    scale = inverse * flat_row(gain)
    lean = inverse * (both[0:1] / entries)
    flat = flat_row(shift) * lean - scale * (both[1:2] / entries)
    for c in range(da.shape[2] // LANES):
        cols, at = lanes(c), lanes_of(c)
        s, l, f = 0.5 * scale[:, at], (1.0 / ROOT) * lean[:, at], flat[:, at]
        for r in range(0, da.shape[1], 128):
            rows = slice(r, r + 128)
            out[0, rows, cols] = da[0, rows, cols].astype(f32) * s - q[0, rows, cols].astype(f32) * l + f

    @pl.when(pl.program_id(0) < taps)
    def _():
        for c in range(one.shape[1]):
            one_out[0, :, lanes_of(c)] = one[0, c].astype(f32)

    @pl.when(pl.program_id(0) == 0)
    def _():
        kinds, rows, width = two_out.shape
        at = 0
        for k in range(kinds):
            for c in range(width // LANES):
                two_out[k, :, lanes_of(c)] = small[at : at + rows].astype(f32)
                at += rows
        rows = three_out.shape[0]
        for c in range(three_out.shape[1] // LANES):
            three_out[:, lanes_of(c)] = small[at : at + rows].astype(f32)
            at += rows
        for n, grads in enumerate((grads1, grads2, grads3)):
            vectors[2 * n][...] = grads[0]
            vectors[2 * n + 1][...] = grads[1]


def last(da, q, sums, gain, shift, one, small, two_shape, three_shape, grads, entries):
    windows, length, channels = da.shape
    slabs = channels // LANES
    tile = min(1024, windows * length // 8)
    per = length // tile
    taps = 5
    one = one.reshape(taps, slabs, channels, LANES)
    small = small.reshape(-1, LANES)
    rows = pl.BlockSpec((1, tile, channels), lambda i: (i // per, i % per, 0))
    flat = lambda i: (0, 0)
    vector = lambda v: pl.BlockSpec((v.shape[0],), lambda i: (0,))
    lengths = [g.shape[1] for g in grads for _ in range(2)]
    tap = lambda i: jnp.minimum(i, taps - 1)
    grads1, grads2, grads3 = grads
    return pl.pallas_call(
        functools.partial(last_kernel, entries, taps),
        grid=(windows * per,),
        out_shape=[
            jax.ShapeDtypeStruct(da.shape, f32),
            jax.ShapeDtypeStruct((taps, channels, channels), f32),
            jax.ShapeDtypeStruct(two_shape, f32),
            jax.ShapeDtypeStruct(three_shape, f32),
        ]
        + [jax.ShapeDtypeStruct((n,), f32) for n in lengths],
        in_specs=[rows, rows, pl.BlockSpec(sums.shape, flat), pl.BlockSpec(grads1.shape, flat), vector(gain), vector(shift)]
        + [pl.BlockSpec((1, slabs, channels, LANES), lambda i: (tap(i), 0, 0, 0)), pl.BlockSpec(small.shape, flat)]
        + [pl.BlockSpec(g.shape, flat) for g in grads[1:]],
        out_specs=[
            rows,
            pl.BlockSpec((1, channels, channels), lambda i: (tap(i), 0, 0)),
            pl.BlockSpec(two_shape, lambda i: (0, 0, 0)),
            pl.BlockSpec(three_shape, flat),
        ]
        + [pl.BlockSpec((n,), lambda i: (0,)) for n in lengths],
        name="last",
        **params(moved=8 * da.size + 6 * one.size),
    )(da, q, sums, grads1, gain, shift, one, small, grads2, grads3)


def on_device(
    inputs,
    conv_one,
    conv_two,
    conv_three,
    gain_one,
    shift_one,
    gain_two,
    shift_two,
    gain_three,
    shift_three,
    cotangent,
):
    windows, length, channels = inputs.shape
    entries = float(windows * length * lax.axis_size("dp") * lax.axis_size("seq"))
    half = entries / 2
    (pooled, pooled_low, s, first, narrow, hidden_two), (sums1, sums2, sums3), c_sides, p_sides, n_sides = conv_forward(
        inputs, cotangent, gain_one, shift_one, conv_one, gain_two, shift_two, conv_two, entries, 0
    )
    outputs, da3, stats, three_grad = conv_three_both(
        narrow, cotangent, pooled_low, sums3, gain_three, shift_three, conv_three, half
    )
    low, parts, small, grads3, grads2 = conv_two_back(
        da3, stats, narrow, n_sides, sums3, gain_three, pooled, p_sides, sums2, gain_two, shift_two, hidden_two, conv_two,
        cotangent, c_sides, s, first, three_grad, half, 2,
    )
    da1, q1, one_grad, grads1 = conv_one_spread(
        low, inputs, sums1, gain_one, shift_one, conv_one, s, parts, entries, 3
    )
    input_grad, *small_grads = last(
        da1, q1, sums1, gain_one, shift_one, one_grad, small, conv_two.shape, conv_three.shape,
        (grads1, grads2, grads3), entries,
    )
    return (outputs, input_grad, *small_grads)


def solution(mesh):
    rows = P("dp", "seq", None)
    in_specs = (rows,) + (P(),) * 9 + (rows,)
    out_specs = (rows, rows) + (P(),) * 9
    return jax.shard_map(on_device, mesh=mesh, in_specs=in_specs, out_specs=out_specs, check_vma=False)
```
